512 devices in a mesh: grp: 16 (over z, core), tp: 32 (over y, x).
Axes of the slice: x: 4, y: 8, z: 8, core: 2. Of those that a mesh axis runs over, the one named last changes fastest.
Arguments:
- residual_input: bfloat16 [2048, 5120], P('grp', 'tp'), may hold values from -6 to 6
- input_norm_gain: float32 [5120], replicated, may hold values from 0.1 to 1.9
- query_weight: bfloat16 [5120, 4096], P(None, 'tp'), may hold values from -0.078125 to 0.078125
- key_value_weight: bfloat16 [5120, 1024], P(None, 'tp'), may hold values from -0.3125 to 0.3125
- shared_down_factors: bfloat16 [5120, 48], replicated, may hold values from -0.078125 to 0.078125
- query_up_factors: bfloat16 [16, 16, 4096], P(None, None, 'tp'), may hold values from -1 to 1
- key_value_up_factors: bfloat16 [16, 16, 1024], replicated, may hold values from -1 to 1
- paged_base_keys: bfloat16 [2048, 128, 512], P(('grp', 'tp')), may hold values from -100 to 100
- paged_base_values: bfloat16 [2048, 128, 512], P(('grp', 'tp')), may hold values from -6 to 6
- paged_down_factors: bfloat16 [2048, 128, 32], P(('grp', 'tp')), may hold values from -6 to 6
- adapter_of_row: int32 [2048], P('grp'), may hold values from 0 to 15
- document_of_row: int32 [2048, 1], P('grp'), may hold values from 0 to 15; in each aligned block of 128 rows (0 to 127, 128 to 255, ...) at most 16 rows name the same one
- document_page_slots: int32 [16, 128], replicated, may hold values from 0 to 2047, as said below
Outputs:
- attended: bfloat16 [2048, 4096], P('grp', 'tp')
The draws below stay inside these ranges and needn't reach their ends.
Inputs may be any that keep to these rules, and one draw needn't show every extreme that they name: `document_of_row`: in each aligned block of 128 rows no document is named by more than 16 rows. `document_page_slots`: each page slot is used once; all pages of one document lie on the 32 devices of one index of grp, 4 on each, documents and indices of grp one to one.
All inputs are finite; a program needn't handle non-finite values.
Results may differ from the reference program's by a relative error of at most 0.034.
Values may be sent and summed in bfloat16 or wider, within the bound.
No kernel may reach another device: no remote copies, remote signals or barrier semaphores. Data moves between devices by JAX's collectives and lax.ppermute only.
A program may use at most 64 MiB of HBM per device.

```python
import math
import jax
import jax.numpy as jnp
import numpy as np
from jax import lax

MODEL_WIDTH = 5120
QH = 32
KEY_VALUE_HEADS = 4
HEAD_SIZE = 128
UPDATE_RANK = 16
PAGE = 128
ADAPTER_COUNT = 16
ROWS_GRP = 128
QUERY_WIDTH = 4096
KEY_WIDTH = 512
ROWS = 2048
DOCS = 16
DOC_PAGES = 128
CTX = 16384
TOTAL_PAGES = 2048
CAP = 16


def draw_document_page_slots(key, part):
    key = jax.random.fold_in(key, 5)
    first_key, second_key = jax.random.split(key)
    group_of_doc = jax.random.permutation(first_key, DOCS)
    doc_keys = jax.random.split(second_key, DOCS)
    within = jax.vmap(lambda one_key: jax.random.permutation(one_key, DOC_PAGES))(doc_keys)
    return (group_of_doc[:, None] * DOC_PAGES + within).astype(jnp.int32)


def draw_paged_base_keys(key, part):
    key = jax.random.fold_in(key, 9)
    base_key = jax.random.fold_in(key, 0)
    array_shape = (TOTAL_PAGES, PAGE, KEY_WIDTH)
    base_keys = 2.5 * jax.random.normal(base_key, array_shape, jnp.float32)
    return jnp.clip(base_keys, -100.0, 100.0).astype(jnp.bfloat16)


def set_ends(drawn, key, smallest, largest):
    place = [jax.random.randint(jax.random.fold_in(key, axis), (), 0, length) for axis, length in enumerate(drawn.shape)]
    widest = drawn.shape.index(max(drawn.shape))
    beside = place[:widest] + [(place[widest] + 1) % drawn.shape[widest]] + place[widest + 1:]
    return drawn.at[tuple(place)].set(smallest).at[tuple(beside)].set(largest)


def shard_levels(stream_key, dims, cuts, smallest, largest):
    def one(dim, blocks):
        draws = jax.random.uniform(jax.random.fold_in(jax.random.fold_in(stream_key, 6), dim), (blocks,), jnp.float32, smallest / len(cuts), largest / len(cuts))
        return jnp.repeat(jnp.exp(draws), dims[dim] // blocks).reshape((-1,) + (1,) * (len(dims) - dim - 1))

    loudness = one(*cuts[0])
    for cut in cuts[1:]:
        loudness = loudness * one(*cut)
    return loudness


def rank_bounds(amount, slope):
    portions = [(1 << 20) // math.isqrt(rank ** slope) + 1 for rank in range(1, amount + 1)]
    deviation = 1 + sum(portions) // (1 << 30)
    return np.cumsum(np.array([max(1, weight // deviation) for weight in portions]))


def ranked(rng, dims, count, lean):
    grid = rank_bounds(count, lean)
    ticket = jax.random.randint(jax.random.fold_in(rng, 1), dims, 0, int(grid[count - 1]))
    grade = jnp.searchsorted(jnp.asarray(grid, jnp.int32), ticket, side="right")
    return jax.random.permutation(jax.random.fold_in(rng, 2), count)[grade].astype(jnp.int32)


def routed_block(key, own, number, rows, number_of, top, most, skew):
    ranking = jax.random.permutation(key, number_of)
    crowded, common = portions_of(number_of, rows * top, most, skew, True), portions_of(number_of, rows * top, most, skew, False)
    places = jnp.arange(number_of)

    def named(tallies, turn):
        used = int((tallies > 0).sum())
        fixed = max(1, used // 4)
        moved = fixed + (places - fixed + turn * (used - fixed)) % max(1, number_of - fixed)
        return jnp.zeros((number_of,), jnp.int32).at[ranking[jnp.where(places < fixed, places, moved)]].set(jnp.asarray(tallies, jnp.int32))

    tallies = jnp.where(number % 4 == 0, named(crowded, number // 4), named(common, number - number // 4 - 1))
    mixed = jax.random.permutation(jax.random.fold_in(own, 3), number_of)
    donor, sink = mixed[0:number_of // 2 * 2:2], mixed[1:number_of // 2 * 2:2]
    margin = jnp.minimum(tallies[donor] - 1, most - tallies[sink]) // 2
    margin = jnp.where((donor == ranking[0]) | (sink == ranking[0]) | (tallies[sink] == 0), 0, jnp.maximum(margin, 0))
    moved = jax.random.randint(jax.random.fold_in(own, 4), (number_of // 2,), 0, 1 << 20) % (margin + 1)
    tallies = tallies.at[donor].add(-moved).at[sink].add(moved)
    labels = jnp.searchsorted(jnp.cumsum(tallies), jnp.arange(rows * top), side="right").astype(jnp.int32)
    table = labels.reshape(top, rows).T
    table = table[jax.random.permutation(jax.random.fold_in(own, 1), rows)]
    turn = jax.random.randint(jax.random.fold_in(own, 2), (rows, 1), 0, top)
    return jnp.take_along_axis(table, (jnp.arange(top)[None, :] + turn) % top, axis=1)


def portions_of(amount, total, reach, slope, full):
    loads = [(1 << 20) // math.isqrt(grade ** slope) + 1 for grade in range(1, amount + 1)]
    largest = reach if full else min(reach, max(-(-total // amount), total * loads[0] // sum(loads)))
    least = 1 if total - largest >= amount - 1 else 0
    given, spare = [largest] + [least] * (amount - 1), total - largest - least * (amount - 1)
    while spare > 0:
        movable = [i for i in range(1, amount) if given[i] < largest] or [i for i in range(1, amount) if given[i] < reach]
        pool, remaining = sum([loads[i] for i in movable]), spare
        for i in movable:
            addition = min(reach - given[i], max(1, remaining * loads[i] // pool), spare)
            given[i] = given[i] + addition
            spare = spare - addition
    return np.array(given)


def bell_draw(rng, extent, spread, limit, cuts=(), dtype=jnp.bfloat16):
    drawn = spread * jax.random.normal(rng, extent, jnp.float32)
    if cuts:
        drawn = drawn * shard_levels(rng, extent, cuts, -0.22, 0.18)
    return jnp.clip(drawn, -limit, limit).astype(dtype)


def setup_inputs(seed: int = 0) -> dict:
    arg_keys = jax.random.split(jax.random.key(seed), 14)
    residual_input = bell_draw(arg_keys[0], (ROWS, MODEL_WIDTH), 1.0, 6.0, ((0, 16), (1, 32)))
    input_norm_gain = jnp.clip(1.0 + 0.18 * jax.random.normal(arg_keys[1], (MODEL_WIDTH,), jnp.float32), 0.1, 1.9)
    query_weight = bell_draw(arg_keys[2], (MODEL_WIDTH, QUERY_WIDTH), MODEL_WIDTH ** -0.5, 0.078125, ((1, 32),))
    key_value_weight = bell_draw(arg_keys[3], (MODEL_WIDTH, 2 * KEY_WIDTH), (MODEL_WIDTH // 12) ** -0.5, 0.3125, ((1, 32),))
    shared_down_factors = bell_draw(arg_keys[4], (MODEL_WIDTH, 3 * UPDATE_RANK), MODEL_WIDTH ** -0.5, 0.078125)
    query_up_factors = bell_draw(arg_keys[5], (ADAPTER_COUNT, UPDATE_RANK, QUERY_WIDTH), 0.125, 1.0, ((2, 32),))
    key_value_up_factors = bell_draw(arg_keys[6], (ADAPTER_COUNT, UPDATE_RANK, 2 * KEY_WIDTH), 0.125, 1.0)
    paged_base_keys = draw_paged_base_keys(jax.random.fold_in(arg_keys[13], 71), 0)
    paged_base_values = bell_draw(arg_keys[8], (TOTAL_PAGES, PAGE, KEY_WIDTH), 1.0, 6.0, ((0, 512),))
    paged_down_factors = bell_draw(arg_keys[9], (TOTAL_PAGES, PAGE, 2 * UPDATE_RANK), 1.0, 6.0, ((0, 512),))
    adapter_of_row = set_ends(ranked(arg_keys[10], (ROWS,), ADAPTER_COUNT, 2), jax.random.fold_in(arg_keys[10], 3), 0, ADAPTER_COUNT - 1).astype(jnp.int32)
    document_of_row_keys = jax.random.split(jax.random.fold_in(arg_keys[11], 1), ROWS // ROWS_GRP)
    document_of_row_turns = jax.random.permutation(jax.random.fold_in(arg_keys[11], 3), ROWS // ROWS_GRP)
    document_of_row = jax.vmap(lambda own, number: routed_block(jax.random.fold_in(arg_keys[11], 2), own, number, ROWS_GRP, DOCS, 1, CAP, 2))(document_of_row_keys, document_of_row_turns).reshape((ROWS, 1))
    document_page_slots = draw_document_page_slots(jax.random.fold_in(arg_keys[13], 71), 0)
    return {"residual_input": residual_input, "input_norm_gain": input_norm_gain, "query_weight": query_weight, "key_value_weight": key_value_weight, "shared_down_factors": shared_down_factors, "query_up_factors": query_up_factors, "key_value_up_factors": key_value_up_factors, "paged_base_keys": paged_base_keys, "paged_base_values": paged_base_values, "paged_down_factors": paged_down_factors, "adapter_of_row": adapter_of_row, "document_of_row": document_of_row, "document_page_slots": document_page_slots}


def reference(residual_input, input_norm_gain, query_weight, key_value_weight, shared_down_factors, query_up_factors, key_value_up_factors, paged_base_keys, paged_base_values, paged_down_factors, adapter_of_row, document_of_row, document_page_slots):
    single_row = jnp.float32
    half_width = jnp.bfloat16
    widened = residual_input.astype(single_row)
    normed_input = (widened * lax.rsqrt(lax.optimization_barrier(jnp.mean(widened * widened, -1, keepdims=True)) + 1e-06) * input_norm_gain).astype(half_width)
    low_rank_part = jnp.dot(normed_input, shared_down_factors, preferred_element_type=single_row).astype(half_width)
    query_low_rank = low_rank_part[:, :UPDATE_RANK]
    key_low_rank = low_rank_part[:, UPDATE_RANK:2 * UPDATE_RANK]
    value_low_rank = low_rank_part[:, 2 * UPDATE_RANK:]
    query_total = jnp.dot(normed_input, query_weight, preferred_element_type=single_row)
    key_total = jnp.dot(normed_input, key_value_weight[:, :KEY_WIDTH], preferred_element_type=single_row)
    value_total = jnp.dot(normed_input, key_value_weight[:, KEY_WIDTH:], preferred_element_type=single_row)
    for adapter_index in range(ADAPTER_COUNT):
        picked_factors = (adapter_of_row == adapter_index)[:, None]
        query_total = query_total + jnp.where(picked_factors, jnp.dot(query_low_rank, query_up_factors[adapter_index], preferred_element_type=single_row), 0.0)
        key_total = key_total + jnp.where(picked_factors, jnp.dot(key_low_rank, key_value_up_factors[adapter_index][:, :KEY_WIDTH], preferred_element_type=single_row), 0.0)
        value_total = value_total + jnp.where(picked_factors, jnp.dot(value_low_rank, key_value_up_factors[adapter_index][:, KEY_WIDTH:], preferred_element_type=single_row), 0.0)
    query_matrix = query_total.astype(half_width)
    fresh_key = key_total.astype(half_width)
    fresh_value = value_total.astype(half_width)
    query_group_size = QH // KEY_VALUE_HEADS
    query_wide = query_matrix.astype(single_row).reshape(ROWS, KEY_VALUE_HEADS, query_group_size, HEAD_SIZE)
    factor_sum = jnp.zeros((ROWS, KEY_VALUE_HEADS, query_group_size, UPDATE_RANK), single_row)
    for adapter_index in range(ADAPTER_COUNT):
        picked_wide = (adapter_of_row == adapter_index)[:, None, None, None]
        key_projected = key_value_up_factors[adapter_index][:, :KEY_WIDTH].astype(single_row).reshape(UPDATE_RANK, KEY_VALUE_HEADS, HEAD_SIZE)
        factor_sum = factor_sum + jnp.where(picked_wide, jnp.einsum('rkgd,jkd->rkgj', query_wide, key_projected), 0.0)
    down_factors = factor_sum.astype(half_width)
    value_update = key_value_up_factors[adapter_of_row][:, :, KEY_WIDTH:]
    row_page_block = 8
    page_block_count = ROWS // row_page_block
    score_scaling = HEAD_SIZE ** (-0.5)

    def attend(bundle):
        query_rows, factor_rows, own_key, value_own, value_up, doc_ids = bundle
        page_ids = document_page_slots[doc_ids]
        key_block = paged_base_keys[page_ids].reshape(row_page_block, CTX, KEY_VALUE_HEADS, HEAD_SIZE).astype(single_row)
        value_block = paged_base_values[page_ids].reshape(row_page_block, CTX, KEY_VALUE_HEADS, HEAD_SIZE).astype(single_row)
        cached = paged_down_factors[page_ids].reshape(row_page_block, CTX, 2 * UPDATE_RANK).astype(single_row)
        query_head_count = query_rows.astype(single_row).reshape(row_page_block, KEY_VALUE_HEADS, query_group_size, HEAD_SIZE)
        factor_heads = factor_rows.astype(single_row)
        scores = (jnp.einsum('bkgd,btkd->bkgt', query_head_count, key_block) + jnp.einsum('bkgj,btj->bkgt', factor_heads, cached[..., :UPDATE_RANK])) * score_scaling
        own_token_score = jnp.einsum('amzu,amu->amz', query_head_count, own_key.astype(single_row).reshape(row_page_block, KEY_VALUE_HEADS, HEAD_SIZE)) * score_scaling
        peak_all = jnp.maximum(lax.optimization_barrier(jnp.max(scores, -1)), own_token_score)
        weights = jnp.exp(scores - peak_all[..., None])
        own_weight = jnp.exp(own_token_score - peak_all)
        totals = lax.optimization_barrier(jnp.sum(weights, -1)) + own_weight
        rounded = lax.optimization_barrier(weights.astype(half_width)).astype(single_row)
        numerator = jnp.einsum('bkgt,btkd->bkgd', rounded, value_block) + own_weight[..., None] * value_own.astype(single_row).reshape(row_page_block, KEY_VALUE_HEADS, 1, HEAD_SIZE)
        low_sum = jnp.einsum('bkgt,btj->bkgj', rounded, cached[..., UPDATE_RANK:])
        value_shift = jnp.einsum('bkgj,bjkd->bkgd', low_sum, value_up.astype(single_row).reshape(row_page_block, UPDATE_RANK, KEY_VALUE_HEADS, HEAD_SIZE), precision=lax.Precision.HIGHEST)
        return ((numerator + value_shift) / totals[..., None]).astype(half_width).reshape(row_page_block, QH * HEAD_SIZE)
    factor_bundles = (query_matrix.reshape(page_block_count, row_page_block, QUERY_WIDTH), down_factors.reshape(page_block_count, row_page_block, KEY_VALUE_HEADS, query_group_size, UPDATE_RANK), fresh_key.reshape(page_block_count, row_page_block, KEY_WIDTH), fresh_value.reshape(page_block_count, row_page_block, KEY_WIDTH), value_update.reshape(page_block_count, row_page_block, UPDATE_RANK, KEY_WIDTH), document_of_row[:, 0].reshape(page_block_count, row_page_block))
    return lax.map(attend, factor_bundles).reshape(ROWS, QUERY_WIDTH)
```

```python
import functools
import math

import jax
import jax.numpy as jnp
from jax import lax
from jax.experimental import pallas as pl
from jax.experimental.pallas import tpu as pltpu
from jax.sharding import Mesh, PartitionSpec as P

HEAD_SIZE = 128
RANK = 16
LANES = 128
Y_HIGH, Y_LOW, X = 4, 2, 4
Y = Y_HIGH * Y_LOW
BLOCK = Y_LOW * X
SLOTS = 256
TILES = SLOTS // LANES
QUERY_ROWS = HEAD_SIZE + RANK
MESSAGE_ROWS = TILES * QUERY_ROWS + 32
RETURN_ROWS = TILES * HEAD_SIZE + 16
PIECE_TOKENS = 512
SCORE_SCALE = HEAD_SIZE**-0.5
F32 = jnp.float32
BF16 = jnp.bfloat16
VMEM = pl.BlockSpec(memory_space=pltpu.VMEM)
SMEM = pl.BlockSpec(memory_space=pltpu.SMEM)


def dot(left, right, left_dim, right_dim):
    return lax.dot_general(
        left, right, (((left_dim,), (right_dim,)), ((), ())), preferred_element_type=F32
    )


def call(kernel, out_shape, in_specs, scratch=(), flops=0, moved=0, limit=32):
    return pl.pallas_call(
        kernel,
        out_shape=out_shape,
        in_specs=in_specs,
        out_specs=jax.tree.map(lambda _: VMEM, out_shape),
        scratch_shapes=list(scratch),
        compiler_params=pltpu.CompilerParams(vmem_limit_bytes=limit * 1024 * 1024),
        cost_estimate=pl.CostEstimate(flops=flops, bytes_accessed=moved, transcendentals=0),
    )


def shape(*dims, dtype=BF16):
    return jax.ShapeDtypeStruct(dims, dtype)


def of_adapter(low, adapters):
    repeated = jnp.concatenate([low] * 16, axis=0)
    adapter = lax.broadcasted_iota(jnp.int32, repeated.shape, 0) // RANK
    return jnp.where(adapter == adapters, repeated, jnp.zeros_like(repeated))


def split_float(value):
    high = value.astype(BF16).astype(F32)
    middle = (value - high).astype(BF16).astype(F32)
    return high, middle, value - high - middle


def pack_kernel(place, keys, values, factors, *pieces):
    own = place[1]
    factors_t = factors[...].astype(F32).T.astype(BF16)
    for shift, piece in enumerate(pieces):
        head = lax.rem(own + shift, Y_HIGH)
        columns = pl.ds(pl.multiple_of(head * HEAD_SIZE, HEAD_SIZE), HEAD_SIZE)
        piece[0:PIECE_TOKENS, :] = keys[:, columns]
        piece[PIECE_TOKENS : 2 * PIECE_TOKENS, :] = values[:, columns]
        for page in range(PIECE_TOKENS // LANES):
            start = 2 * PIECE_TOKENS + page * 2 * RANK
            piece[start : start + 2 * RANK, :] = factors_t[:, page * LANES : (page + 1) * LANES]


def project_kernel(
    groups,
    place,
    page_slots,
    features,
    query_weight,
    key_value_weight,
    down,
    gain,
    query_up,
    key_value_up,
    adapters,
    documents,
    message,
    fresh,
    queries_t,
    placing,
    normed,
    weights,
    update,
):
    device = place[0]
    part = gain.shape[1]
    width = normed.shape[0]
    rows = features.shape[-1]

    squares = jnp.zeros((part, rows), F32)
    for x in range(X):
        for y in range(Y):
            block = features[x, y].astype(F32)
            squares = squares + block * block
    scale = lax.rsqrt(jnp.sum(squares, axis=0, keepdims=True) / width + 1e-06)
    gain_t = gain[...].T
    for x in range(X):
        for y in range(Y):
            t = y * X + x
            block = features[x, y].astype(F32) * scale * gain_t[:, t : t + 1]
            normed[t * part : (t + 1) * part, :] = block.astype(BF16)
    weights[:, 0:HEAD_SIZE] = query_weight[...]
    weights[:, HEAD_SIZE:] = jnp.concatenate(
        [key_value_weight[...], down[...], jnp.zeros((width, HEAD_SIZE - 80), BF16)], axis=1
    )
    total = dot(normed[...], weights[...], 0, 0).T

    adapter = adapters[...]
    low = total[HEAD_SIZE + 32 : HEAD_SIZE + 80].astype(BF16)
    query_update = dot(query_up[...], of_adapter(low[0:RANK], adapter), 0, 0)
    queries = (total[0:HEAD_SIZE] + query_update).astype(BF16)
    queries_t[...] = queries

    is_key = device < Y * X // 2
    low_kv = jnp.where(is_key, low[RANK : 2 * RANK], low[2 * RANK :])
    columns = pl.ds(pl.multiple_of(device // X * HEAD_SIZE, HEAD_SIZE), HEAD_SIZE)
    update[...] = dot(key_value_up[:, columns], of_adapter(low_kv, adapter), 0, 0)
    mine = pl.ds(pl.multiple_of(lax.rem(device, X) * 32, 32), 32)
    fresh[...] = (total[HEAD_SIZE : HEAD_SIZE + 32] + update[mine, :]).astype(BF16)

    document = documents[...]
    target = jnp.zeros_like(document)
    for d in range(page_slots.shape[0]):
        target = jnp.where(document == d, page_slots[d, 0] // page_slots.shape[1], target)
    capacity = SLOTS // groups
    group = lax.broadcasted_iota(jnp.int32, (16, rows), 0)
    match = (group == target).astype(F32)
    before = (
        lax.broadcasted_iota(jnp.int32, (rows, rows), 0)
        < lax.broadcasted_iota(jnp.int32, (rows, rows), 1)
    ).astype(F32)
    earlier = dot(match.astype(BF16), before.astype(BF16), 1, 0)
    position = jnp.sum(earlier * match, axis=0, keepdims=True).astype(jnp.int32)
    slot = target * capacity + position
    place_here = lax.broadcasted_iota(jnp.int32, (SLOTS, rows), 0) == slot
    placed = place_here.astype(F32)
    placing[...] = placed.astype(BF16)
    message[:, 0:capacity, :] = (
        dot(placed.astype(BF16), queries, 1, 1).astype(BF16).reshape(groups, capacity, HEAD_SIZE)
    )
    slot_adapter = jnp.sum(placed * adapter.astype(F32), axis=1, keepdims=True)
    message[:, capacity:, :] = (
        jnp.broadcast_to(slot_adapter, (SLOTS, LANES)).astype(BF16).reshape(groups, capacity, LANES)
    )


def factor_kernel(groups, place, received, fresh, key_value_up, message, slot_adapters):
    capacity = SLOTS // groups
    queries = received[:, 0:capacity, :].reshape(SLOTS, HEAD_SIZE)
    queries_t = queries.astype(F32).T.astype(BF16)
    adapters = received[:, capacity:, :].reshape(SLOTS, LANES).astype(F32).T[0:1]
    slot_adapters[...] = jnp.broadcast_to(adapters, slot_adapters.shape)
    columns = pl.ds(pl.multiple_of(place[1] * HEAD_SIZE, HEAD_SIZE), HEAD_SIZE)
    every = dot(key_value_up[:, columns], queries, 1, 1)
    adapter = (lax.broadcasted_iota(jnp.int32, every.shape, 0) // RANK).astype(F32)
    kept = jnp.where(adapter == adapters, every, 0.0)
    factors = kept[0:RANK]
    for a in range(1, 16):
        factors = factors + kept[a * RANK : (a + 1) * RANK]
    factors = factors.astype(BF16)
    new = fresh[...]
    for member in range(BLOCK):
        for tile in range(TILES):
            lanes = slice(tile * LANES, (tile + 1) * LANES)
            start = tile * QUERY_ROWS
            message[member, start : start + HEAD_SIZE, :] = queries_t[:, lanes]
            message[member, start + HEAD_SIZE : start + QUERY_ROWS, :] = factors[:, lanes]
        message[member, TILES * QUERY_ROWS :, :] = new


def attend_kernel(
    place,
    queries,
    slot_adapters,
    key_value_up,
    piece_0,
    piece_1,
    piece_2,
    piece_3,
    message,
    keys,
    values_t,
    query,
    scores,
):
    pieces = (piece_0, piece_1, piece_2, piece_3)
    tokens = PIECE_TOKENS * len(pieces)
    depth = 2 * HEAD_SIZE
    value_rows = values_t.shape[0]
    ones = (
        lax.broadcasted_iota(jnp.int32, (value_rows - QUERY_ROWS, tokens), 0) == 0
    ).astype(F32)
    values_t[QUERY_ROWS:, :] = ones.astype(BF16)
    for index, piece in enumerate(pieces):
        for page in range(PIECE_TOKENS // LANES):
            start = page * LANES
            here = slice(index * PIECE_TOKENS + start, index * PIECE_TOKENS + start + LANES)
            row = 2 * PIECE_TOKENS + page * 2 * RANK
            factors = piece[row : row + 2 * RANK, :]
            key_factors = jnp.concatenate(
                [factors[0:RANK].astype(F32), jnp.zeros((LANES - RANK, LANES), F32)], axis=0
            )
            keys[here, 0:HEAD_SIZE] = piece[start : start + LANES, :]
            keys[here, HEAD_SIZE:] = key_factors.T.astype(BF16)
            value = piece[PIECE_TOKENS + start : PIECE_TOKENS + start + LANES, :]
            values_t[0:HEAD_SIZE, here] = value.astype(F32).T.astype(BF16)
            values_t[HEAD_SIZE:QUERY_ROWS, here] = factors[RANK:]
    query[QUERY_ROWS:, :] = jnp.zeros((depth - QUERY_ROWS, SLOTS), BF16)

    columns = pl.ds(pl.multiple_of((place[1] + Y_HIGH) * HEAD_SIZE, HEAD_SIZE), HEAD_SIZE)
    value_up = key_value_up[:, columns]
    adapters = slot_adapters[0:1, :].astype(jnp.int32)
    chunk = 512

    def one_head(head, carry):
        for tile in range(TILES):
            query[0:QUERY_ROWS, tile * LANES : (tile + 1) * LANES] = queries[
                head, tile * QUERY_ROWS : (tile + 1) * QUERY_ROWS, :
            ]
        highest = None
        for start in range(0, tokens, chunk):
            score = dot(keys[start : start + chunk, :], query[...], 1, 0)
            scores[start : start + chunk, :] = score
            top = jnp.max(score.reshape(chunk // 8, 8, SLOTS), axis=0)
            highest = top if highest is None else jnp.maximum(highest, top)
        peak = jnp.max(highest, axis=0, keepdims=True)
        total = jnp.zeros((value_rows, SLOTS), F32)
        for start in range(0, tokens, chunk):
            shifted = scores[start : start + chunk, :] - peak
            weight = jnp.exp2(shifted * (SCORE_SCALE * math.log2(math.e))).astype(BF16)
            total = total + dot(values_t[:, start : start + chunk], weight, 1, 0)
        mass = total[QUERY_ROWS : QUERY_ROWS + 1]
        inverse = 1.0 / mass
        low = (total[HEAD_SIZE:QUERY_ROWS] * inverse).astype(BF16)
        shift = dot(value_up, of_adapter(low, adapters), 0, 0)
        result = (total[0:HEAD_SIZE] * inverse + shift).astype(BF16)
        log_mass = peak * SCORE_SCALE + jnp.log(mass)
        parts = split_float(log_mass)
        stats = [part[:, tile * LANES : (tile + 1) * LANES] for tile in range(TILES) for part in parts]
        stats = jnp.concatenate(stats + [jnp.zeros((16 - len(stats), LANES), F32)], axis=0)
        for tile in range(TILES):
            message[head, tile * HEAD_SIZE : (tile + 1) * HEAD_SIZE, :] = result[
                :, tile * LANES : (tile + 1) * LANES
            ]
        message[head, TILES * HEAD_SIZE :, :] = stats.astype(BF16)
        return carry

    lax.fori_loop(0, BLOCK, one_head, 0)


def merge_kernel(groups, partials, message):
    capacity = SLOTS // groups
    stats = [partials[member, TILES * HEAD_SIZE :, :].astype(F32) for member in range(BLOCK)]
    results, masses = [], []
    for tile in range(TILES):
        first = 3 * tile
        logs = [s[first : first + 1] + s[first + 1 : first + 2] + s[first + 2 : first + 3] for s in stats]
        peak = functools.reduce(jnp.maximum, logs)
        weights = [jnp.exp(one - peak) for one in logs]
        whole = functools.reduce(jnp.add, weights)
        rows = slice(tile * HEAD_SIZE, (tile + 1) * HEAD_SIZE)
        total = jnp.zeros((HEAD_SIZE, LANES), F32)
        for member in range(BLOCK):
            total = total + partials[member, rows, :].astype(F32) * weights[member]
        results.append((total / whole).T.astype(BF16))
        parts = list(split_float(peak + jnp.log(whole)))
        parts = jnp.concatenate(parts + [jnp.zeros((LANES - 3, LANES), F32)], axis=0)
        masses.append(parts.T.astype(BF16))
    message[:, 0:capacity, :] = jnp.concatenate(results, axis=0).reshape(groups, capacity, HEAD_SIZE)
    message[:, capacity:, :] = jnp.concatenate(masses, axis=0).reshape(groups, capacity, LANES)


def finish_kernel(groups, received, placing, queries_t, gathered, out):
    capacity = SLOTS // groups
    place = placing[...]
    shared = dot(received[:, 0:capacity, :].reshape(SLOTS, HEAD_SIZE), place, 0, 0)
    stats = dot(received[:, capacity:, :].reshape(SLOTS, LANES), place, 0, 0)
    log_mass = stats[0:1] + stats[1:2] + stats[2:3]
    new = gathered[:, TILES * QUERY_ROWS :, :]
    key = new[0:X].reshape(HEAD_SIZE, LANES).astype(F32)
    value = new[X:].reshape(HEAD_SIZE, LANES).astype(F32)
    own = jnp.sum(queries_t[...].astype(F32) * key, axis=0, keepdims=True) * SCORE_SCALE
    peak = jnp.maximum(log_mass, own)
    shared_weight = jnp.exp(log_mass - peak)
    own_weight = jnp.exp(own - peak)
    result = (shared * shared_weight + value * own_weight) / (shared_weight + own_weight)
    out[...] = result.T.astype(BF16)


def per_device(
    residual_input,
    input_norm_gain,
    query_weight,
    key_value_weight,
    shared_down_factors,
    query_up_factors,
    key_value_up_factors,
    paged_base_keys,
    paged_base_values,
    paged_down_factors,
    adapter_of_row,
    document_of_row,
    document_page_slots,
):
    groups = lax.axis_size("grp")
    capacity = SLOTS // groups
    rows, part = residual_input.shape
    width = part * Y * X
    y_high = lax.axis_index("yh")
    device = (y_high * Y_LOW + lax.axis_index("yl")) * X + lax.axis_index("x")
    place = jnp.stack([device, y_high]).astype(jnp.int32)
    query_up = query_up_factors.reshape(-1, HEAD_SIZE)
    key_value_up = key_value_up_factors.reshape(-1, key_value_up_factors.shape[2])

    features = jnp.broadcast_to(residual_input.T[None], (Y, part, rows))
    features = lax.all_to_all(features, ("yh", "yl"), 0, 0, tiled=True)

    piece_rows = 2 * PIECE_TOKENS + 2 * RANK * PIECE_TOKENS // LANES
    pieces = call(
        pack_kernel,
        [shape(piece_rows, HEAD_SIZE)] * Y_HIGH,
        [SMEM, VMEM, VMEM, VMEM],
        moved=3 * 1024 * 1024,
    )(
        place,
        paged_base_keys.reshape(PIECE_TOKENS, -1),
        paged_base_values.reshape(PIECE_TOKENS, -1),
        paged_down_factors.reshape(PIECE_TOKENS, -1),
    )
    pieces = [pieces[0]] + [
        lax.ppermute(pieces[s], "yh", [(i, (i + s) % Y_HIGH) for i in range(Y_HIGH)])
        for s in range(1, Y_HIGH)
    ]

    features = jnp.broadcast_to(features.reshape(1, Y * part, rows), (X, Y * part, rows))
    features = lax.all_to_all(features, "x", 0, 0, tiled=True).reshape(X, Y, part, rows)

    message, fresh, queries_t, placing = call(
        functools.partial(project_kernel, groups),
        [
            shape(groups, 2 * capacity, HEAD_SIZE),
            shape(32, rows),
            shape(HEAD_SIZE, rows),
            shape(SLOTS, rows),
        ],
        [SMEM, SMEM] + [VMEM] * 9,
        [
            pltpu.VMEM((width, rows), BF16),
            pltpu.VMEM((width, 2 * HEAD_SIZE), BF16),
            pltpu.VMEM((HEAD_SIZE, rows), F32),
        ],
        flops=2 * width * rows * 256,
        moved=6 * 1024 * 1024,
    )(
        place,
        document_page_slots,
        features,
        query_weight,
        key_value_weight,
        shared_down_factors,
        input_norm_gain.reshape(Y * X, part),
        query_up,
        key_value_up,
        adapter_of_row.reshape(1, rows),
        document_of_row.reshape(1, rows),
    )
    fresh = lax.ppermute(
        fresh,
        ("yh", "yl"),
        [(y, 2 * y if y < Y_HIGH else 2 * (y - Y_HIGH) + 1) for y in range(Y)],
    )
    received = lax.all_to_all(message, "grp", 0, 0, tiled=True)

    message, slot_adapters = call(
        functools.partial(factor_kernel, groups),
        [shape(BLOCK, MESSAGE_ROWS, LANES), shape(8, SLOTS, dtype=F32)],
        [SMEM] + [VMEM] * 3,
        flops=2 * 256 * 256 * 128,
        moved=1024 * 1024,
    )(place, received, fresh, key_value_up)
    gathered = lax.all_to_all(message, ("yl", "x"), 0, 0, tiled=True)

    tokens = PIECE_TOKENS * Y_HIGH
    message = call(
        attend_kernel,
        shape(BLOCK, RETURN_ROWS, LANES),
        [SMEM] + [VMEM] * 7,
        [
            pltpu.VMEM((tokens, 2 * HEAD_SIZE), BF16),
            pltpu.VMEM((QUERY_ROWS + 16, tokens), BF16),
            pltpu.VMEM((2 * HEAD_SIZE, SLOTS), BF16),
            pltpu.VMEM((tokens, SLOTS), F32),
        ],
        flops=4 * SLOTS * BLOCK * tokens * 256,
        moved=3 * 1024 * 1024,
    )(place, gathered, slot_adapters, key_value_up, *pieces)
    partials = lax.all_to_all(message, ("yl", "x"), 0, 0, tiled=True)

    message = call(
        functools.partial(merge_kernel, groups),
        shape(groups, 2 * capacity, HEAD_SIZE),
        [VMEM],
        flops=SLOTS * HEAD_SIZE * 16,
        moved=1024 * 1024,
    )(partials)
    received = lax.all_to_all(message, "grp", 0, 0, tiled=True)

    return call(
        functools.partial(finish_kernel, groups),
        shape(rows, HEAD_SIZE),
        [VMEM] * 4,
        flops=2 * SLOTS * rows * 256,
        moved=1024 * 1024,
    )(received, placing, queries_t, gathered)


def solution(mesh):
    groups = mesh.devices.shape[0]
    split = Mesh(
        mesh.devices.reshape(groups, Y_HIGH, Y_LOW, X), ("grp", "yh", "yl", "x")
    )
    tp = ("yh", "yl", "x")
    in_specs = (
        P("grp", tp),
        P(),
        P(None, tp),
        P(None, tp),
        P(),
        P(None, None, tp),
        P(),
        P(("grp",) + tp, None, None),
        P(("grp",) + tp, None, None),
        P(("grp",) + tp, None, None),
        P("grp"),
        P("grp", None),
        P(),
    )
    return jax.shard_map(
        per_device, mesh=split, in_specs=in_specs, out_specs=P("grp", tp), check_vma=False
    )
```

```python
import functools
import math

import jax
import jax.numpy as jnp
from jax import lax
from jax.experimental import pallas as pl
from jax.experimental.pallas import tpu as pltpu
from jax.sharding import Mesh, PartitionSpec as P

HEAD_SIZE = 128
RANK = 16
LANES = 128
Y_HIGH, Y_LOW, X = 4, 2, 4
Y = Y_HIGH * Y_LOW
BLOCK = Y_LOW * X
SLOTS = 256
TILES = SLOTS // LANES
QUERY_ROWS = HEAD_SIZE + RANK
MESSAGE_ROWS = TILES * QUERY_ROWS + 32
RETURN_ROWS = TILES * HEAD_SIZE + 16
PIECE_TOKENS = 512
PIECES = ((0, 0, 512), (1, 0, 512), (3, 0, 512), (2, 0, 256), (2, 256, 256))
SCORE_SCALE = HEAD_SIZE**-0.5
F32 = jnp.float32
BF16 = jnp.bfloat16
VMEM = pl.BlockSpec(memory_space=pltpu.VMEM)
SMEM = pl.BlockSpec(memory_space=pltpu.SMEM)


def dot(left, right, left_dim, right_dim):
    return lax.dot_general(
        left, right, (((left_dim,), (right_dim,)), ((), ())), preferred_element_type=F32
    )


def call(kernel, out_shape, in_specs, scratch=(), flops=0, moved=0, limit=32):
    return pl.pallas_call(
        kernel,
        out_shape=out_shape,
        in_specs=in_specs,
        out_specs=jax.tree.map(lambda _: VMEM, out_shape),
        scratch_shapes=list(scratch),
        compiler_params=pltpu.CompilerParams(vmem_limit_bytes=limit * 1024 * 1024),
        cost_estimate=pl.CostEstimate(flops=flops, bytes_accessed=moved, transcendentals=0),
    )


def shape(*dims, dtype=BF16):
    return jax.ShapeDtypeStruct(dims, dtype)


def of_adapter(low, adapters):
    repeated = jnp.concatenate([low] * 16, axis=0)
    adapter = lax.broadcasted_iota(jnp.int32, repeated.shape, 0) // RANK
    return jnp.where(adapter == adapters, repeated, jnp.zeros_like(repeated))


def split_float(value):
    high = value.astype(BF16).astype(F32)
    middle = (value - high).astype(BF16).astype(F32)
    return high, middle, value - high - middle


def pack_kernel(place, keys, values, factors, *pieces):
    own = place[1]
    for (shift, start, count), piece in zip(PIECES, pieces):
        head = lax.rem(own + shift, Y_HIGH)
        columns = pl.ds(pl.multiple_of(head * HEAD_SIZE, HEAD_SIZE), HEAD_SIZE)
        piece[0:count, :] = keys[start : start + count, columns]
        piece[count : 2 * count, :] = values[start : start + count, columns]
        first = start // LANES * 2 * RANK
        piece[2 * count :, :] = factors[first : first + count // LANES * 2 * RANK, :]


def project_kernel(
    groups,
    place,
    page_slots,
    features,
    query_weight,
    key_value_weight,
    down,
    gain,
    query_up,
    key_value_up,
    adapters,
    documents,
    message,
    fresh,
    queries_t,
    placing,
    normed,
    weights,
    update,
):
    device = place[0]
    part = gain.shape[1]
    width = normed.shape[0]
    rows = features.shape[-1]

    squares = jnp.zeros((part, rows), F32)
    for x in range(X):
        for y in range(Y):
            block = features[x, y].astype(F32)
            squares = squares + block * block
    scale = lax.rsqrt(jnp.sum(squares, axis=0, keepdims=True) / width + 1e-06)
    gain_t = gain[...].T
    for x in range(X):
        for y in range(Y):
            t = y * X + x
            block = features[x, y].astype(F32) * scale * gain_t[:, t : t + 1]
            normed[t * part : (t + 1) * part, :] = block.astype(BF16)
    weights[0:32, :] = key_value_weight[...]
    weights[32:, :] = down[...]
    query_total = dot(query_weight[...], normed[...], 0, 0)
    total = dot(weights[...], normed[...], 1, 0)

    adapter = adapters[...]
    low = total[32:].astype(BF16)
    query_update = dot(query_up[...], of_adapter(low[0:RANK], adapter), 0, 0)
    queries = (query_total + query_update).astype(BF16)
    queries_t[...] = queries

    is_key = device < Y * X // 2
    low_kv = jnp.where(is_key, low[RANK : 2 * RANK], low[2 * RANK :])
    columns = pl.ds(pl.multiple_of(device // X * HEAD_SIZE, HEAD_SIZE), HEAD_SIZE)
    update[...] = dot(key_value_up[:, columns], of_adapter(low_kv, adapter), 0, 0)
    mine = pl.ds(pl.multiple_of(lax.rem(device, X) * 32, 32), 32)
    fresh[...] = (total[0:32] + update[mine, :]).astype(BF16)

    document = documents[...]
    target = jnp.zeros_like(document)
    for d in range(page_slots.shape[0]):
        target = jnp.where(document == d, page_slots[d, 0] // page_slots.shape[1], target)
    capacity = SLOTS // groups
    group = lax.broadcasted_iota(jnp.int32, (16, rows), 0)
    match = (group == target).astype(F32)
    before = (
        lax.broadcasted_iota(jnp.int32, (rows, rows), 0)
        < lax.broadcasted_iota(jnp.int32, (rows, rows), 1)
    ).astype(F32)
    earlier = dot(match.astype(BF16), before.astype(BF16), 1, 0)
    position = jnp.sum(earlier * match, axis=0, keepdims=True).astype(jnp.int32)
    slot = target * capacity + position
    place_here = lax.broadcasted_iota(jnp.int32, (SLOTS, rows), 0) == slot
    placed = place_here.astype(F32)
    placing[...] = placed.astype(BF16)
    message[:, 0:capacity, :] = (
        dot(placed.astype(BF16), queries, 1, 1).astype(BF16).reshape(groups, capacity, HEAD_SIZE)
    )
    slot_adapter = jnp.sum(placed * adapter.astype(F32), axis=1, keepdims=True)
    message[:, capacity:, :] = (
        jnp.broadcast_to(slot_adapter, (SLOTS, LANES)).astype(BF16).reshape(groups, capacity, LANES)
    )


def factor_kernel(groups, place, received, fresh, key_value_up, message, slot_adapters):
    capacity = SLOTS // groups
    queries = received[:, 0:capacity, :].reshape(SLOTS, HEAD_SIZE)
    queries_t = queries.astype(F32).T.astype(BF16)
    adapters = received[:, capacity:, :].reshape(SLOTS, LANES).astype(F32).T[0:1]
    slot_adapters[...] = jnp.broadcast_to(adapters, slot_adapters.shape)
    columns = pl.ds(pl.multiple_of(place[1] * HEAD_SIZE, HEAD_SIZE), HEAD_SIZE)
    every = dot(key_value_up[:, columns], queries, 1, 1)
    adapter = (lax.broadcasted_iota(jnp.int32, every.shape, 0) // RANK).astype(F32)
    kept = jnp.where(adapter == adapters, every, 0.0)
    factors = kept[0:RANK]
    for a in range(1, 16):
        factors = factors + kept[a * RANK : (a + 1) * RANK]
    factors = factors.astype(BF16)
    new = fresh[...]
    for member in range(BLOCK):
        for tile in range(TILES):
            lanes = slice(tile * LANES, (tile + 1) * LANES)
            start = tile * QUERY_ROWS
            message[member, start : start + HEAD_SIZE, :] = queries_t[:, lanes]
            message[member, start + HEAD_SIZE : start + QUERY_ROWS, :] = factors[:, lanes]
        message[member, TILES * QUERY_ROWS :, :] = new


def prepare_kernel(*refs):
    pieces, (keys, values_t) = refs[:-2], refs[-2:]
    tokens = keys.shape[0]
    ones = lax.broadcasted_iota(jnp.int32, (values_t.shape[0] - QUERY_ROWS, tokens), 0) == 0
    values_t[QUERY_ROWS:, :] = ones.astype(F32).astype(BF16)
    base = 0
    for (_, _, count), piece in zip(PIECES, pieces):
        for page in range(count // LANES):
            start = page * LANES
            here = slice(base + start, base + start + LANES)
            row = 2 * count + page * 2 * RANK
            factors = piece[row : row + 2 * RANK, :]
            key_factors = jnp.concatenate(
                [factors[0:RANK].astype(F32), jnp.zeros((LANES - RANK, LANES), F32)], axis=0
            )
            keys[here, 0:HEAD_SIZE] = piece[start : start + LANES, :]
            keys[here, HEAD_SIZE:] = key_factors.T.astype(BF16)
            value = piece[count + start : count + start + LANES, :]
            values_t[0:HEAD_SIZE, here] = value.astype(F32).T.astype(BF16)
            values_t[HEAD_SIZE:QUERY_ROWS, here] = factors[RANK:]
        base += count


def attend_kernel(
    place, queries, slot_adapters, key_value_up, keys, values_t, message, query, scores
):
    tokens = keys.shape[0]
    depth = 2 * HEAD_SIZE
    value_rows = values_t.shape[0]
    query[:, QUERY_ROWS:, :] = jnp.zeros((2, depth - QUERY_ROWS, SLOTS), BF16)
    columns = pl.ds(pl.multiple_of((place[1] + Y_HIGH) * HEAD_SIZE, HEAD_SIZE), HEAD_SIZE)
    value_up = key_value_up[:, columns]
    adapters = slot_adapters[0:1, :].astype(jnp.int32)
    chunk = 512

    def score_head(head, side):
        for tile in range(TILES):
            query[side, 0:QUERY_ROWS, tile * LANES : (tile + 1) * LANES] = queries[
                head, tile * QUERY_ROWS : (tile + 1) * QUERY_ROWS, :
            ]
        highest = None
        for start in range(0, tokens, chunk):
            score = dot(keys[start : start + chunk, :], query[side], 1, 0)
            scores[side, start : start + chunk, :] = score
            top = jnp.max(score.reshape(chunk // 8, 8, SLOTS), axis=0)
            highest = top if highest is None else jnp.maximum(highest, top)
        return jnp.max(highest, axis=0, keepdims=True)

    def sum_head(head, side, peak):
        total = jnp.zeros((value_rows, SLOTS), F32)
        for start in range(0, tokens, chunk):
            shifted = scores[side, start : start + chunk, :] - peak
            weight = jnp.exp2(shifted * (SCORE_SCALE * math.log2(math.e))).astype(BF16)
            total = total + dot(values_t[:, start : start + chunk], weight, 1, 0)
        mass = total[QUERY_ROWS : QUERY_ROWS + 1]
        inverse = 1.0 / mass
        low = (total[HEAD_SIZE:QUERY_ROWS] * inverse).astype(BF16)
        shift = dot(value_up, of_adapter(low, adapters), 0, 0)
        result = (total[0:HEAD_SIZE] * inverse + shift).astype(BF16)
        parts = split_float(peak * SCORE_SCALE + jnp.log(mass))
        stats = [part[:, tile * LANES : (tile + 1) * LANES] for tile in range(TILES) for part in parts]
        stats = jnp.concatenate(stats + [jnp.zeros((16 - len(stats), LANES), F32)], axis=0)
        for tile in range(TILES):
            message[head, tile * HEAD_SIZE : (tile + 1) * HEAD_SIZE, :] = result[
                :, tile * LANES : (tile + 1) * LANES
            ]
        message[head, TILES * HEAD_SIZE :, :] = stats.astype(BF16)

    def two_heads(pair, carry):
        first = score_head(2 * pair, 0)
        second = score_head(2 * pair + 1, 1)
        sum_head(2 * pair, 0, first)
        sum_head(2 * pair + 1, 1, second)
        return carry

    lax.fori_loop(0, BLOCK // 2, two_heads, 0)


def merge_kernel(groups, partials, message):
    capacity = SLOTS // groups
    stats = [partials[member, TILES * HEAD_SIZE :, :].astype(F32) for member in range(BLOCK)]
    results, masses = [], []
    for tile in range(TILES):
        first = 3 * tile
        logs = [s[first : first + 1] + s[first + 1 : first + 2] + s[first + 2 : first + 3] for s in stats]
        peak = functools.reduce(jnp.maximum, logs)
        weights = [jnp.exp(one - peak) for one in logs]
        whole = functools.reduce(jnp.add, weights)
        rows = slice(tile * HEAD_SIZE, (tile + 1) * HEAD_SIZE)
        total = jnp.zeros((HEAD_SIZE, LANES), F32)
        for member in range(BLOCK):
            total = total + partials[member, rows, :].astype(F32) * weights[member]
        results.append((total / whole).T.astype(BF16))
        parts = list(split_float(peak + jnp.log(whole)))
        parts = jnp.concatenate(parts + [jnp.zeros((LANES - 3, LANES), F32)], axis=0)
        masses.append(parts.T.astype(BF16))
    message[:, 0:capacity, :] = jnp.concatenate(results, axis=0).reshape(groups, capacity, HEAD_SIZE)
    message[:, capacity:, :] = jnp.concatenate(masses, axis=0).reshape(groups, capacity, LANES)


def finish_kernel(groups, received, placing, queries_t, gathered, out):
    capacity = SLOTS // groups
    place = placing[...]
    shared = dot(received[:, 0:capacity, :].reshape(SLOTS, HEAD_SIZE), place, 0, 0)
    stats = dot(received[:, capacity:, :].reshape(SLOTS, LANES), place, 0, 0)
    log_mass = stats[0:1] + stats[1:2] + stats[2:3]
    new = gathered[:, TILES * QUERY_ROWS :, :]
    key = new[0:X].reshape(HEAD_SIZE, LANES).astype(F32)
    value = new[X:].reshape(HEAD_SIZE, LANES).astype(F32)
    own = jnp.sum(queries_t[...].astype(F32) * key, axis=0, keepdims=True) * SCORE_SCALE
    peak = jnp.maximum(log_mass, own)
    shared_weight = jnp.exp(log_mass - peak)
    own_weight = jnp.exp(own - peak)
    result = (shared * shared_weight + value * own_weight) / (shared_weight + own_weight)
    out[...] = result.T.astype(BF16)


def send(value, shift):
    return lax.ppermute(value, "yh", [(i, (i + shift) % Y_HIGH) for i in range(Y_HIGH)])


def per_device(
    residual_input,
    input_norm_gain,
    query_weight,
    key_value_weight,
    shared_down_factors,
    query_up_factors,
    key_value_up_factors,
    paged_base_keys,
    paged_base_values,
    paged_down_factors,
    adapter_of_row,
    document_of_row,
    document_page_slots,
):
    groups = lax.axis_size("grp")
    capacity = SLOTS // groups
    rows, part = residual_input.shape
    width = part * Y * X
    y_high = lax.axis_index("yh")
    device = (y_high * Y_LOW + lax.axis_index("yl")) * X + lax.axis_index("x")
    place = jnp.stack([device, y_high]).astype(jnp.int32)
    query_up = query_up_factors.reshape(-1, HEAD_SIZE)
    key_value_up = key_value_up_factors.reshape(-1, key_value_up_factors.shape[2])

    features = jnp.broadcast_to(residual_input.T[None], (Y, part, rows))
    pieces = call(
        pack_kernel,
        [shape(2 * n + 2 * RANK * n // LANES, HEAD_SIZE) for _, _, n in PIECES],
        [SMEM, VMEM, VMEM, VMEM],
        moved=3 * 1024 * 1024,
    )(
        place,
        paged_base_keys.reshape(PIECE_TOKENS, -1),
        paged_base_values.reshape(PIECE_TOKENS, -1),
        paged_down_factors.transpose(0, 2, 1).reshape(-1, LANES),
    )
    features, pieces = lax.optimization_barrier((features, pieces))
    own, right, left, far_right, far_left = pieces
    right, left = send(right, 1), send(left, -1)
    far_right, far_left = send(far_right, 1), send(far_left, -1)
    features = lax.all_to_all(features, ("yh", "yl"), 0, 0, tiled=True)
    features = jnp.broadcast_to(features.reshape(1, Y * part, rows), (X, Y * part, rows))
    features = lax.all_to_all(features, "x", 0, 0, tiled=True).reshape(X, Y, part, rows)

    message, fresh, queries_t, placing = call(
        functools.partial(project_kernel, groups),
        [
            shape(groups, 2 * capacity, HEAD_SIZE),
            shape(32, rows),
            shape(HEAD_SIZE, rows),
            shape(SLOTS, rows),
        ],
        [SMEM, SMEM] + [VMEM] * 9,
        [
            pltpu.VMEM((width, rows), BF16),
            pltpu.VMEM((32 + 3 * RANK, width), BF16),
            pltpu.VMEM((HEAD_SIZE, rows), F32),
        ],
        flops=2 * width * rows * 256,
        moved=6 * 1024 * 1024,
    )(
        place,
        document_page_slots,
        features,
        query_weight,
        key_value_weight.T,
        shared_down_factors.T,
        input_norm_gain.reshape(Y * X, part),
        query_up,
        key_value_up,
        adapter_of_row.reshape(1, rows),
        document_of_row.reshape(1, rows),
    )
    fresh = lax.ppermute(
        fresh,
        ("yh", "yl"),
        [(y, 2 * y if y < Y_HIGH else 2 * (y - Y_HIGH) + 1) for y in range(Y)],
    )
    message, right, left, far_right, far_left = lax.optimization_barrier(
        (message, right, left, far_right, far_left)
    )
    far_right, far_left = send(far_right, 1), send(far_left, -1)
    received = lax.all_to_all(message, "grp", 0, 0, tiled=True)

    message, slot_adapters = call(
        functools.partial(factor_kernel, groups),
        [shape(BLOCK, MESSAGE_ROWS, LANES), shape(8, SLOTS, dtype=F32)],
        [SMEM] + [VMEM] * 3,
        flops=2 * 256 * 256 * 128,
        moved=1024 * 1024,
    )(place, received, fresh, key_value_up)
    message, far_right, far_left = lax.optimization_barrier((message, far_right, far_left))
    pieces = (own, right, left, far_right, far_left)
    gathered = lax.all_to_all(message, ("yl", "x"), 0, 0, tiled=True)

    tokens = PIECE_TOKENS * Y_HIGH
    keys, values_t = call(
        prepare_kernel,
        [shape(tokens, 2 * HEAD_SIZE), shape(QUERY_ROWS + 16, tokens)],
        [VMEM] * len(pieces),
        moved=3 * 1024 * 1024,
    )(*pieces)
    message = call(
        attend_kernel,
        shape(BLOCK, RETURN_ROWS, LANES),
        [SMEM] + [VMEM] * 5,
        [
            pltpu.VMEM((2, 2 * HEAD_SIZE, SLOTS), BF16),
            pltpu.VMEM((2, tokens, SLOTS), F32),
        ],
        flops=4 * SLOTS * BLOCK * tokens * 256,
        moved=3 * 1024 * 1024,
    )(place, gathered, slot_adapters, key_value_up, keys, values_t)
    partials = lax.all_to_all(message, ("yl", "x"), 0, 0, tiled=True)

    message = call(
        functools.partial(merge_kernel, groups),
        shape(groups, 2 * capacity, HEAD_SIZE),
        [VMEM],
        flops=SLOTS * HEAD_SIZE * 16,
        moved=1024 * 1024,
    )(partials)
    received = lax.all_to_all(message, "grp", 0, 0, tiled=True)

    return call(
        functools.partial(finish_kernel, groups),
        shape(rows, HEAD_SIZE),
        [VMEM] * 4,
        flops=2 * SLOTS * rows * 256,
        moved=1024 * 1024,
    )(received, placing, queries_t, gathered)


def solution(mesh):
    groups = mesh.devices.shape[0]
    split = Mesh(
        mesh.devices.reshape(groups, Y_HIGH, Y_LOW, X), ("grp", "yh", "yl", "x")
    )
    tp = ("yh", "yl", "x")
    in_specs = (
        P("grp", tp),
        P(),
        P(None, tp),
        P(None, tp),
        P(),
        P(None, None, tp),
        P(),
        P(("grp",) + tp, None, None),
        P(("grp",) + tp, None, None),
        P(("grp",) + tp, None, None),
        P("grp"),
        P("grp", None),
        P(),
    )
    return jax.shard_map(
        per_device, mesh=split, in_specs=in_specs, out_specs=P("grp", tp), check_vma=False
    )
```

```python
import functools
import math

import jax
import jax.numpy as jnp
from jax import lax
from jax.experimental import pallas as pl
from jax.experimental.pallas import tpu as pltpu
from jax.sharding import Mesh, PartitionSpec as P

HEAD_SIZE = 128
RANK = 16
LANES = 128
Y_HIGH, Y_LOW, X = 4, 2, 4
Y = Y_HIGH * Y_LOW
BLOCK = Y_LOW * X
SLOTS = 256
TILES = SLOTS // LANES
QUERY_ROWS = HEAD_SIZE + RANK
MESSAGE_ROWS = TILES * QUERY_ROWS
RETURN_ROWS = TILES * HEAD_SIZE + 16
FRESH_ROWS = 32
PIECE_TOKENS = 512
PIECES = ((0, 0, 512), (1, 0, 512), (3, 0, 512), (2, 0, 256), (2, 256, 256))
SCORE_SCALE = HEAD_SIZE**-0.5
F32 = jnp.float32
BF16 = jnp.bfloat16
VMEM = pl.BlockSpec(memory_space=pltpu.VMEM)
SMEM = pl.BlockSpec(memory_space=pltpu.SMEM)
ANY = pl.BlockSpec(memory_space=pl.ANY)
HBM = pl.BlockSpec(memory_space=pltpu.HBM)


def dot(left, right, left_dim, right_dim):
    return lax.dot_general(
        left, right, (((left_dim,), (right_dim,)), ((), ())), preferred_element_type=F32
    )


def call(kernel, out_shape, in_specs, scratch=(), flops=0, moved=0, limit=32, out_specs=None):
    return pl.pallas_call(
        kernel,
        out_shape=out_shape,
        in_specs=in_specs,
        out_specs=out_specs or jax.tree.map(lambda _: VMEM, out_shape),
        scratch_shapes=list(scratch),
        compiler_params=pltpu.CompilerParams(vmem_limit_bytes=limit * 1024 * 1024),
        cost_estimate=pl.CostEstimate(flops=flops, bytes_accessed=moved, transcendentals=0),
    )


def shape(*dims, dtype=BF16):
    return jax.ShapeDtypeStruct(dims, dtype)


def of_adapter(low, adapters):
    repeated = jnp.concatenate([low] * 16, axis=0)
    adapter = lax.broadcasted_iota(jnp.int32, repeated.shape, 0) // RANK
    return jnp.where(adapter == adapters, repeated, jnp.zeros_like(repeated))


def split_float(value):
    high = value.astype(BF16).astype(F32)
    middle = (value - high).astype(BF16).astype(F32)
    return high, middle, value - high - middle


def pack_kernel(place, keys, values, factors, features, copies, *rest):
    pieces, sems = rest[:-1], rest[-1]
    own = place[1]
    moves = []
    for (shift, start, count), piece in zip(PIECES, pieces):
        head = lax.rem(own + shift, Y_HIGH)
        columns = pl.ds(pl.multiple_of(head * HEAD_SIZE, HEAD_SIZE), HEAD_SIZE)
        tokens = pl.ds(start, count)
        first = start // LANES * 2 * RANK
        rows = count // LANES * 2 * RANK
        moves += [
            (keys.at[tokens, columns], piece.at[pl.ds(0, count), :]),
            (values.at[tokens, columns], piece.at[pl.ds(count, count), :]),
            (factors.at[pl.ds(first, rows), :], piece.at[pl.ds(2 * count, rows), :]),
        ]
    moves = [pltpu.make_async_copy(*move, sems.at[i]) for i, move in enumerate(moves)]
    for move in moves:
        move.start()
    mine = features[...]
    for member in range(Y):
        copies[member] = mine
    for move in moves:
        move.wait()


def spread_kernel(features, held_right, held_left, copies):
    for member in range(X):
        copies[member] = features[...]


def project_kernel(
    groups,
    place,
    page_slots,
    features,
    query_weight_far,
    key_value_weight_far,
    down_far,
    gain,
    query_up_far,
    key_value_up_far,
    adapters,
    documents,
    held_right,
    held_left,
    held_far_right,
    held_far_left,
    message,
    fresh,
    queries_t,
    placing,
    normed,
    query_weight,
    weights,
    query_up,
    key_value_up,
    update,
    sems,
):
    columns = pl.ds(pl.multiple_of(place[0] // X * HEAD_SIZE, HEAD_SIZE), HEAD_SIZE)
    moves = [
        (query_weight_far, query_weight),
        (key_value_weight_far, weights.at[pl.ds(0, FRESH_ROWS), :]),
        (down_far, weights.at[pl.ds(FRESH_ROWS, 3 * RANK), :]),
        (query_up_far, query_up),
        (key_value_up_far.at[:, columns], key_value_up),
    ]
    moves = [pltpu.make_async_copy(*move, sems.at[i]) for i, move in enumerate(moves)]
    for move in moves:
        move.start()
    device = place[0]
    part = gain.shape[1]
    width = normed.shape[0]
    rows = features.shape[-1]

    squares = jnp.zeros((part, rows), F32)
    for x in range(X):
        for y in range(Y):
            block = features[x, y].astype(F32)
            squares = squares + block * block
    scale = lax.rsqrt(jnp.sum(squares, axis=0, keepdims=True) / width + 1e-06)
    gain_t = gain[...].T
    for x in range(X):
        for y in range(Y):
            t = y * X + x
            block = features[x, y].astype(F32) * scale * gain_t[:, t : t + 1]
            normed[t * part : (t + 1) * part, :] = block.astype(BF16)
    for move in moves:
        move.wait()
    query_total = dot(query_weight[...], normed[...], 0, 0)
    total = dot(weights[...], normed[...], 1, 0)

    adapter = adapters[...]
    low = total[FRESH_ROWS:].astype(BF16)
    query_update = dot(query_up[...], of_adapter(low[0:RANK], adapter), 0, 0)
    queries = (query_total + query_update).astype(BF16)
    queries_t[...] = queries

    is_key = device < Y * X // 2
    low_kv = jnp.where(is_key, low[RANK : 2 * RANK], low[2 * RANK :])
    update[...] = dot(key_value_up[...], of_adapter(low_kv, adapter), 0, 0)
    mine = pl.ds(pl.multiple_of(lax.rem(device, X) * 32, 32), 32)
    fresh[...] = (total[0:FRESH_ROWS] + update[mine, :]).astype(BF16)

    document = documents[...]
    target = jnp.zeros_like(document)
    for d in range(page_slots.shape[0]):
        target = jnp.where(document == d, page_slots[d, 0] // page_slots.shape[1], target)
    capacity = SLOTS // groups
    group = lax.broadcasted_iota(jnp.int32, (16, rows), 0)
    match = (group == target).astype(F32)
    before = (
        lax.broadcasted_iota(jnp.int32, (rows, rows), 0)
        < lax.broadcasted_iota(jnp.int32, (rows, rows), 1)
    ).astype(F32)
    earlier = dot(match.astype(BF16), before.astype(BF16), 1, 0)
    position = jnp.sum(earlier * match, axis=0, keepdims=True).astype(jnp.int32)
    slot = target * capacity + position
    place_here = lax.broadcasted_iota(jnp.int32, (SLOTS, rows), 0) == slot
    placed = place_here.astype(F32)
    placing[...] = placed.astype(BF16)
    message[:, 0:capacity, :] = (
        dot(placed.astype(BF16), queries, 1, 1).astype(BF16).reshape(groups, capacity, HEAD_SIZE)
    )
    slot_adapter = jnp.sum(placed * adapter.astype(F32), axis=1, keepdims=True)
    message[:, capacity:, :] = (
        jnp.broadcast_to(slot_adapter, (SLOTS, LANES)).astype(BF16).reshape(groups, capacity, LANES)
    )


def factor_kernel(groups, place, received, key_value_up, message, slot_adapters):
    capacity = SLOTS // groups
    queries = received[:, 0:capacity, :].reshape(SLOTS, HEAD_SIZE)
    queries_t = queries.astype(F32).T.astype(BF16)
    adapters = received[:, capacity:, :].reshape(SLOTS, LANES).astype(F32).T[0:1]
    slot_adapters[...] = jnp.broadcast_to(adapters, slot_adapters.shape)
    columns = pl.ds(pl.multiple_of(place[1] * HEAD_SIZE, HEAD_SIZE), HEAD_SIZE)
    every = dot(key_value_up[:, columns], queries, 1, 1)
    adapter = (lax.broadcasted_iota(jnp.int32, every.shape, 0) // RANK).astype(F32)
    kept = jnp.where(adapter == adapters, every, 0.0)
    factors = kept[0:RANK]
    for a in range(1, 16):
        factors = factors + kept[a * RANK : (a + 1) * RANK]
    factors = factors.astype(BF16)
    for member in range(BLOCK):
        for tile in range(TILES):
            lanes = slice(tile * LANES, (tile + 1) * LANES)
            start = tile * QUERY_ROWS
            message[member, start : start + HEAD_SIZE, :] = queries_t[:, lanes]
            message[member, start + HEAD_SIZE : start + QUERY_ROWS, :] = factors[:, lanes]


def prepare_kernel(*refs):
    pieces, (keys, values_t) = refs[:-2], refs[-2:]
    tokens = keys.shape[0]
    ones = lax.broadcasted_iota(jnp.int32, (values_t.shape[0] - QUERY_ROWS, tokens), 0) == 0
    values_t[QUERY_ROWS:, :] = ones.astype(F32).astype(BF16)
    base = 0
    for (_, _, count), piece in zip(PIECES, pieces):
        for page in range(count // LANES):
            start = page * LANES
            here = slice(base + start, base + start + LANES)
            row = 2 * count + page * 2 * RANK
            factors = piece[row : row + 2 * RANK, :]
            key_factors = jnp.concatenate(
                [factors[0:RANK].astype(F32), jnp.zeros((LANES - RANK, LANES), F32)], axis=0
            )
            keys[here, 0:HEAD_SIZE] = piece[start : start + LANES, :]
            keys[here, HEAD_SIZE:] = key_factors.T.astype(BF16)
            value = piece[count + start : count + start + LANES, :]
            values_t[0:HEAD_SIZE, here] = value.astype(F32).T.astype(BF16)
            values_t[HEAD_SIZE:QUERY_ROWS, here] = factors[RANK:]
        base += count


def attend_kernel(
    place, queries, slot_adapters, key_value_up, keys, values_t, fresh, message, query, scores
):
    tokens = keys.shape[0]
    depth = 2 * HEAD_SIZE
    value_rows = values_t.shape[0]
    query[:, QUERY_ROWS:, :] = jnp.zeros((2, depth - QUERY_ROWS, SLOTS), BF16)
    columns = pl.ds(pl.multiple_of((place[1] + Y_HIGH) * HEAD_SIZE, HEAD_SIZE), HEAD_SIZE)
    value_up = key_value_up[:, columns]
    adapters = slot_adapters[0:1, :].astype(jnp.int32)
    chunk = 512

    def score_head(head, side):
        for tile in range(TILES):
            query[side, 0:QUERY_ROWS, tile * LANES : (tile + 1) * LANES] = queries[
                head, tile * QUERY_ROWS : (tile + 1) * QUERY_ROWS, :
            ]
        highest = None
        for start in range(0, tokens, chunk):
            score = dot(keys[start : start + chunk, :], query[side], 1, 0)
            scores[side, start : start + chunk, :] = score
            top = jnp.max(score.reshape(chunk // 8, 8, SLOTS), axis=0)
            highest = top if highest is None else jnp.maximum(highest, top)
        return jnp.max(highest, axis=0, keepdims=True)

    def sum_head(head, side, peak):
        total = jnp.zeros((value_rows, SLOTS), F32)
        for start in range(0, tokens, chunk):
            shifted = scores[side, start : start + chunk, :] - peak
            weight = jnp.exp2(shifted * (SCORE_SCALE * math.log2(math.e))).astype(BF16)
            total = total + dot(values_t[:, start : start + chunk], weight, 1, 0)
        mass = total[QUERY_ROWS : QUERY_ROWS + 1]
        inverse = 1.0 / mass
        low = (total[HEAD_SIZE:QUERY_ROWS] * inverse).astype(BF16)
        shift = dot(value_up, of_adapter(low, adapters), 0, 0)
        result = (total[0:HEAD_SIZE] * inverse + shift).astype(BF16)
        parts = split_float(peak * SCORE_SCALE + jnp.log(mass))
        stats = [part[:, tile * LANES : (tile + 1) * LANES] for tile in range(TILES) for part in parts]
        stats = jnp.concatenate(stats + [jnp.zeros((16 - len(stats), LANES), F32)], axis=0)
        for tile in range(TILES):
            message[head, tile * HEAD_SIZE : (tile + 1) * HEAD_SIZE, :] = result[
                :, tile * LANES : (tile + 1) * LANES
            ]
        message[head, TILES * HEAD_SIZE : RETURN_ROWS, :] = stats.astype(BF16)
        message[head, RETURN_ROWS:, :] = fresh[...]

    def two_heads(pair, carry):
        first = score_head(2 * pair, 0)
        second = score_head(2 * pair + 1, 1)
        sum_head(2 * pair, 0, first)
        sum_head(2 * pair + 1, 1, second)
        return carry

    lax.fori_loop(0, BLOCK // 2, two_heads, 0)


def merge_kernel(groups, partials, message):
    capacity = SLOTS // groups
    stats = [partials[member, TILES * HEAD_SIZE : RETURN_ROWS, :].astype(F32) for member in range(BLOCK)]
    results, masses = [], []
    for tile in range(TILES):
        first = 3 * tile
        logs = [s[first : first + 1] + s[first + 1 : first + 2] + s[first + 2 : first + 3] for s in stats]
        peak = functools.reduce(jnp.maximum, logs)
        weights = [jnp.exp(one - peak) for one in logs]
        whole = functools.reduce(jnp.add, weights)
        rows = slice(tile * HEAD_SIZE, (tile + 1) * HEAD_SIZE)
        total = jnp.zeros((HEAD_SIZE, LANES), F32)
        for member in range(BLOCK):
            total = total + partials[member, rows, :].astype(F32) * weights[member]
        results.append((total / whole).T.astype(BF16))
        parts = list(split_float(peak + jnp.log(whole)))
        parts = jnp.concatenate(parts + [jnp.zeros((LANES - 3, LANES), F32)], axis=0)
        masses.append(parts.T.astype(BF16))
    message[:, 0:capacity, :] = jnp.concatenate(results, axis=0).reshape(groups, capacity, HEAD_SIZE)
    message[:, capacity:, :] = jnp.concatenate(masses, axis=0).reshape(groups, capacity, LANES)


def finish_kernel(groups, received, placing, queries_t, partials, out):
    capacity = SLOTS // groups
    place = placing[...]
    shared = dot(received[:, 0:capacity, :].reshape(SLOTS, HEAD_SIZE), place, 0, 0)
    stats = dot(received[:, capacity:, :].reshape(SLOTS, LANES), place, 0, 0)
    log_mass = stats[0:1] + stats[1:2] + stats[2:3]
    new = partials[:, RETURN_ROWS:, :]
    key = new[0:X].reshape(HEAD_SIZE, LANES).astype(F32)
    value = new[X:].reshape(HEAD_SIZE, LANES).astype(F32)
    own = jnp.sum(queries_t[...].astype(F32) * key, axis=0, keepdims=True) * SCORE_SCALE
    peak = jnp.maximum(log_mass, own)
    shared_weight = jnp.exp(log_mass - peak)
    own_weight = jnp.exp(own - peak)
    result = (shared * shared_weight + value * own_weight) / (shared_weight + own_weight)
    out[...] = result.T.astype(BF16)


def send(value, shift):
    return lax.ppermute(value, "yh", [(i, (i + shift) % Y_HIGH) for i in range(Y_HIGH)])


def per_device(
    residual_input,
    input_norm_gain,
    query_weight,
    key_value_weight,
    shared_down_factors,
    query_up_factors,
    key_value_up_factors,
    paged_base_keys,
    paged_base_values,
    paged_down_factors,
    adapter_of_row,
    document_of_row,
    document_page_slots,
):
    groups = lax.axis_size("grp")
    capacity = SLOTS // groups
    rows, part = residual_input.shape
    width = part * Y * X
    y_high = lax.axis_index("yh")
    device = (y_high * Y_LOW + lax.axis_index("yl")) * X + lax.axis_index("x")
    place = jnp.stack([device, y_high]).astype(jnp.int32)
    query_up = query_up_factors.reshape(-1, HEAD_SIZE)
    key_value_up = key_value_up_factors.reshape(-1, key_value_up_factors.shape[2])

    piece_shapes = [shape(2 * n + 2 * RANK * n // LANES, HEAD_SIZE) for _, _, n in PIECES]
    features, own, right, left, far_right, far_left = call(
        pack_kernel,
        [shape(Y, part, rows)] + piece_shapes,
        [SMEM, HBM, HBM, HBM, VMEM],
        [pltpu.SemaphoreType.DMA((3 * len(PIECES),))],
        moved=3 * 1024 * 1024,
        limit=60,
        out_specs=[VMEM] + [HBM] * len(PIECES),
    )(
        place,
        paged_base_keys.reshape(PIECE_TOKENS, -1),
        paged_base_values.reshape(PIECE_TOKENS, -1),
        paged_down_factors.transpose(0, 2, 1).reshape(-1, LANES),
        residual_input.T,
    )
    far_right, far_left = send(far_right, 1), send(far_left, -1)
    features = lax.all_to_all(features, ("yh", "yl"), 0, 0, tiled=True)

    features = call(
        spread_kernel,
        shape(X, Y * part, rows),
        [VMEM, ANY, ANY],
        moved=1024 * 1024,
    )(features.reshape(Y * part, rows), far_right, far_left)
    far_right, far_left = send(far_right, 1), send(far_left, -1)
    right, left = send(right, 1), send(left, -1)
    features = lax.all_to_all(features, "x", 0, 0, tiled=True).reshape(X, Y, part, rows)

    message, fresh, queries_t, placing = call(
        functools.partial(project_kernel, groups),
        [
            shape(groups, 2 * capacity, HEAD_SIZE),
            shape(FRESH_ROWS, rows),
            shape(HEAD_SIZE, rows),
            shape(SLOTS, rows),
        ],
        [SMEM, SMEM, VMEM, HBM, HBM, HBM, VMEM, HBM, HBM, VMEM, VMEM] + [ANY] * 4,
        [
            pltpu.VMEM((width, rows), BF16),
            pltpu.VMEM((width, HEAD_SIZE), BF16),
            pltpu.VMEM((FRESH_ROWS + 3 * RANK, width), BF16),
            pltpu.VMEM(query_up.shape, BF16),
            pltpu.VMEM((key_value_up.shape[0], HEAD_SIZE), BF16),
            pltpu.VMEM((HEAD_SIZE, rows), F32),
            pltpu.SemaphoreType.DMA((5,)),
        ],
        flops=2 * width * rows * 256,
        moved=6 * 1024 * 1024,
    )(
        place,
        document_page_slots,
        features,
        query_weight,
        key_value_weight.T,
        shared_down_factors.T,
        input_norm_gain.reshape(Y * X, part),
        query_up,
        key_value_up,
        adapter_of_row.reshape(1, rows),
        document_of_row.reshape(1, rows),
        right,
        left,
        far_right,
        far_left,
    )
    fresh = lax.ppermute(
        fresh,
        ("yh", "yl"),
        [(y, 2 * y if y < Y_HIGH else 2 * (y - Y_HIGH) + 1) for y in range(Y)],
    )
    received = lax.all_to_all(message, "grp", 0, 0, tiled=True)

    message, slot_adapters = call(
        functools.partial(factor_kernel, groups),
        [shape(BLOCK, MESSAGE_ROWS, LANES), shape(8, SLOTS, dtype=F32)],
        [SMEM] + [VMEM] * 2,
        flops=2 * 256 * 256 * 128,
        moved=1024 * 1024,
    )(place, received, key_value_up)
    pieces = (own, right, left, far_right, far_left)
    gathered = lax.all_to_all(message, ("yl", "x"), 0, 0, tiled=True)

    tokens = PIECE_TOKENS * Y_HIGH
    keys, values_t = call(
        prepare_kernel,
        [shape(tokens, 2 * HEAD_SIZE), shape(QUERY_ROWS + 16, tokens)],
        [VMEM] * len(pieces),
        moved=3 * 1024 * 1024,
    )(*pieces)
    message = call(
        attend_kernel,
        shape(BLOCK, RETURN_ROWS + FRESH_ROWS, LANES),
        [SMEM] + [VMEM] * 6,
        [
            pltpu.VMEM((2, 2 * HEAD_SIZE, SLOTS), BF16),
            pltpu.VMEM((2, tokens, SLOTS), F32),
        ],
        flops=4 * SLOTS * BLOCK * tokens * 256,
        moved=3 * 1024 * 1024,
    )(place, gathered, slot_adapters, key_value_up, keys, values_t, fresh)
    partials = lax.all_to_all(message, ("yl", "x"), 0, 0, tiled=True)

    message = call(
        functools.partial(merge_kernel, groups),
        shape(groups, 2 * capacity, HEAD_SIZE),
        [VMEM],
        flops=SLOTS * HEAD_SIZE * 16,
        moved=1024 * 1024,
    )(partials)
    received = lax.all_to_all(message, "grp", 0, 0, tiled=True)

    return call(
        functools.partial(finish_kernel, groups),
        shape(rows, HEAD_SIZE),
        [VMEM] * 4,
        flops=2 * SLOTS * rows * 256,
        moved=1024 * 1024,
    )(received, placing, queries_t, partials)


def solution(mesh):
    groups = mesh.devices.shape[0]
    split = Mesh(
        mesh.devices.reshape(groups, Y_HIGH, Y_LOW, X), ("grp", "yh", "yl", "x")
    )
    tp = ("yh", "yl", "x")
    in_specs = (
        P("grp", tp),
        P(),
        P(None, tp),
        P(None, tp),
        P(),
        P(None, None, tp),
        P(),
        P(("grp",) + tp, None, None),
        P(("grp",) + tp, None, None),
        P(("grp",) + tp, None, None),
        P("grp"),
        P("grp", None),
        P(),
    )
    return jax.shard_map(
        per_device, mesh=split, in_specs=in_specs, out_specs=P("grp", tp), check_vma=False
    )
```

```python
import functools
import math

import jax
import jax.numpy as jnp
from jax import lax
from jax.experimental import pallas as pl
from jax.experimental.pallas import tpu as pltpu
from jax.sharding import Mesh, PartitionSpec as P

HEAD_SIZE = 128
RANK = 16
LANES = 128
Y_HIGH, Y_LOW, X = 4, 2, 4
Y = Y_HIGH * Y_LOW
BLOCK = Y_LOW * X
SLOTS = 256
TILES = SLOTS // LANES
QUERY_ROWS = HEAD_SIZE + RANK
MESSAGE_ROWS = TILES * QUERY_ROWS
RETURN_ROWS = TILES * HEAD_SIZE + 16
FRESH_ROWS = 32
PIECE_TOKENS = 512
PIECE_ROWS = 2 * PIECE_TOKENS + 2 * RANK * PIECE_TOKENS // LANES
SHIFTS = (0, 1, 3, 2)
SCORE_SCALE = HEAD_SIZE**-0.5
F32 = jnp.float32
BF16 = jnp.bfloat16
VMEM = pl.BlockSpec(memory_space=pltpu.VMEM)
SMEM = pl.BlockSpec(memory_space=pltpu.SMEM)
ANY = pl.BlockSpec(memory_space=pl.ANY)
HBM = pl.BlockSpec(memory_space=pltpu.HBM)


def dot(left, right, left_dim, right_dim):
    return lax.dot_general(
        left, right, (((left_dim,), (right_dim,)), ((), ())), preferred_element_type=F32
    )


def call(kernel, out_shape, in_specs, scratch=(), flops=0, moved=0, limit=32, out_specs=None):
    return pl.pallas_call(
        kernel,
        out_shape=out_shape,
        in_specs=in_specs,
        out_specs=out_specs or jax.tree.map(lambda _: VMEM, out_shape),
        scratch_shapes=list(scratch),
        compiler_params=pltpu.CompilerParams(vmem_limit_bytes=limit * 1024 * 1024),
        cost_estimate=pl.CostEstimate(flops=flops, bytes_accessed=moved, transcendentals=0),
    )


def shape(*dims, dtype=BF16):
    return jax.ShapeDtypeStruct(dims, dtype)


def of_adapter(low, adapters):
    repeated = jnp.concatenate([low] * 16, axis=0)
    adapter = lax.broadcasted_iota(jnp.int32, repeated.shape, 0) // RANK
    return jnp.where(adapter == adapters, repeated, jnp.zeros_like(repeated))


def split_float(value):
    high = value.astype(BF16).astype(F32)
    middle = (value - high).astype(BF16).astype(F32)
    return high, middle, value - high - middle


def pack_kernel(keys, values, factors, message):
    for head in range(Y_HIGH):
        columns = slice(head * HEAD_SIZE, (head + 1) * HEAD_SIZE)
        message[head, 0:PIECE_TOKENS, :] = keys[:, columns]
        message[head, PIECE_TOKENS : 2 * PIECE_TOKENS, :] = values[:, columns]
        message[head, 2 * PIECE_TOKENS :, :] = factors[...]


def project_kernel(
    groups,
    place,
    page_slots,
    features_0,
    features_1,
    features_2,
    features_3,
    query_weight_far,
    key_value_weight_far,
    down_far,
    gain,
    query_up_far,
    key_value_up_far,
    adapters,
    documents,
    held,
    message,
    fresh,
    queries_t,
    placing,
    normed,
    query_weight,
    weights,
    query_up,
    key_value_up,
    update,
    sems,
):
    columns = pl.ds(pl.multiple_of(place[0] // X * HEAD_SIZE, HEAD_SIZE), HEAD_SIZE)
    moves = [
        (query_weight_far, query_weight),
        (key_value_weight_far, weights.at[pl.ds(0, FRESH_ROWS), :]),
        (down_far, weights.at[pl.ds(FRESH_ROWS, 3 * RANK), :]),
        (query_up_far, query_up),
        (key_value_up_far.at[:, columns], key_value_up),
    ]
    moves = [pltpu.make_async_copy(*move, sems.at[i]) for i, move in enumerate(moves)]
    for move in moves:
        move.start()
    device = place[0]
    part = gain.shape[2]
    width = normed.shape[0]
    rows = adapters.shape[1]
    sources = (features_0, features_1, features_2, features_3)

    squares = jnp.zeros((part, rows), F32)
    for features in sources:
        for y in range(Y):
            block = features[y].astype(F32)
            squares = squares + block * block
    scale = lax.rsqrt(jnp.sum(squares, axis=0, keepdims=True) / width + 1e-06)
    for shift, features in zip(SHIFTS, sources):
        x = lax.rem(device + shift, X)
        gain_t = gain[x].T
        for y in range(Y):
            block = features[y].astype(F32) * scale * gain_t[:, y : y + 1]
            start = pl.multiple_of((y * X + x) * part, 32)
            normed[pl.ds(start, part), :] = block.astype(BF16)
    for move in moves:
        move.wait()
    query_total = dot(query_weight[...], normed[...], 0, 0)
    total = dot(weights[...], normed[...], 1, 0)

    adapter = adapters[...]
    low = total[FRESH_ROWS:].astype(BF16)
    query_update = dot(query_up[...], of_adapter(low[0:RANK], adapter), 0, 0)
    queries = (query_total + query_update).astype(BF16)
    queries_t[...] = queries

    is_key = device < Y * X // 2
    low_kv = jnp.where(is_key, low[RANK : 2 * RANK], low[2 * RANK :])
    update[...] = dot(key_value_up[...], of_adapter(low_kv, adapter), 0, 0)
    mine = pl.ds(pl.multiple_of(lax.rem(device, X) * 32, 32), 32)
    fresh[...] = (total[0:FRESH_ROWS] + update[mine, :]).astype(BF16)

    document = documents[...]
    target = jnp.zeros_like(document)
    for d in range(page_slots.shape[0]):
        target = jnp.where(document == d, page_slots[d, 0] // page_slots.shape[1], target)
    capacity = SLOTS // groups
    group = lax.broadcasted_iota(jnp.int32, (16, rows), 0)
    match = (group == target).astype(F32)
    before = (
        lax.broadcasted_iota(jnp.int32, (rows, rows), 0)
        < lax.broadcasted_iota(jnp.int32, (rows, rows), 1)
    ).astype(F32)
    earlier = dot(match.astype(BF16), before.astype(BF16), 1, 0)
    position = jnp.sum(earlier * match, axis=0, keepdims=True).astype(jnp.int32)
    slot = target * capacity + position
    place_here = lax.broadcasted_iota(jnp.int32, (SLOTS, rows), 0) == slot
    placed = place_here.astype(F32)
    placing[...] = placed.astype(BF16)
    message[:, 0:capacity, :] = (
        dot(placed.astype(BF16), queries, 1, 1).astype(BF16).reshape(groups, capacity, HEAD_SIZE)
    )
    slot_adapter = jnp.sum(placed * adapter.astype(F32), axis=1, keepdims=True)
    message[:, capacity:, :] = (
        jnp.broadcast_to(slot_adapter, (SLOTS, LANES)).astype(BF16).reshape(groups, capacity, LANES)
    )


def factor_kernel(groups, place, received, key_value_up, message, slot_adapters):
    capacity = SLOTS // groups
    queries = received[:, 0:capacity, :].reshape(SLOTS, HEAD_SIZE)
    queries_t = queries.astype(F32).T.astype(BF16)
    adapters = received[:, capacity:, :].reshape(SLOTS, LANES).astype(F32).T[0:1]
    slot_adapters[...] = jnp.broadcast_to(adapters, slot_adapters.shape)
    columns = pl.ds(pl.multiple_of(place[1] * HEAD_SIZE, HEAD_SIZE), HEAD_SIZE)
    every = dot(key_value_up[:, columns], queries, 1, 1)
    adapter = (lax.broadcasted_iota(jnp.int32, every.shape, 0) // RANK).astype(F32)
    kept = jnp.where(adapter == adapters, every, 0.0)
    factors = kept[0:RANK]
    for a in range(1, 16):
        factors = factors + kept[a * RANK : (a + 1) * RANK]
    factors = factors.astype(BF16)
    for member in range(BLOCK):
        for tile in range(TILES):
            lanes = slice(tile * LANES, (tile + 1) * LANES)
            start = tile * QUERY_ROWS
            message[member, start : start + HEAD_SIZE, :] = queries_t[:, lanes]
            message[member, start + HEAD_SIZE : start + QUERY_ROWS, :] = factors[:, lanes]


def prepare_kernel(pieces, keys, values_t):
    tokens = keys.shape[0]
    ones = lax.broadcasted_iota(jnp.int32, (values_t.shape[0] - QUERY_ROWS, tokens), 0) == 0
    values_t[QUERY_ROWS:, :] = ones.astype(F32).astype(BF16)
    for index in range(Y_HIGH):
        for page in range(PIECE_TOKENS // LANES):
            start = page * LANES
            here = slice(index * PIECE_TOKENS + start, index * PIECE_TOKENS + start + LANES)
            row = 2 * PIECE_TOKENS + page * 2 * RANK
            factors = pieces[index, row : row + 2 * RANK, :]
            key_factors = jnp.concatenate(
                [factors[0:RANK].astype(F32), jnp.zeros((LANES - RANK, LANES), F32)], axis=0
            )
            keys[here, 0:HEAD_SIZE] = pieces[index, start : start + LANES, :]
            keys[here, HEAD_SIZE:] = key_factors.T.astype(BF16)
            value = pieces[index, PIECE_TOKENS + start : PIECE_TOKENS + start + LANES, :]
            values_t[0:HEAD_SIZE, here] = value.astype(F32).T.astype(BF16)
            values_t[HEAD_SIZE:QUERY_ROWS, here] = factors[RANK:]


def attend_kernel(
    place, queries, slot_adapters, key_value_up, keys, values_t, fresh, message, query, scores
):
    tokens = keys.shape[0]
    depth = 2 * HEAD_SIZE
    value_rows = values_t.shape[0]
    query[:, QUERY_ROWS:, :] = jnp.zeros((2, depth - QUERY_ROWS, SLOTS), BF16)
    columns = pl.ds(pl.multiple_of((place[1] + Y_HIGH) * HEAD_SIZE, HEAD_SIZE), HEAD_SIZE)
    value_up = key_value_up[:, columns]
    adapters = slot_adapters[0:1, :].astype(jnp.int32)
    chunk = 512

    def score_head(head, side):
        for tile in range(TILES):
            query[side, 0:QUERY_ROWS, tile * LANES : (tile + 1) * LANES] = queries[
                head, tile * QUERY_ROWS : (tile + 1) * QUERY_ROWS, :
            ]
        highest = None
        for start in range(0, tokens, chunk):
            score = dot(keys[start : start + chunk, :], query[side], 1, 0)
            scores[side, start : start + chunk, :] = score
            top = jnp.max(score.reshape(chunk // 8, 8, SLOTS), axis=0)
            highest = top if highest is None else jnp.maximum(highest, top)
        return jnp.max(highest, axis=0, keepdims=True)

    def sum_head(head, side, peak):
        total = jnp.zeros((value_rows, SLOTS), F32)
        for start in range(0, tokens, chunk):
            shifted = scores[side, start : start + chunk, :] - peak
            weight = jnp.exp2(shifted * (SCORE_SCALE * math.log2(math.e))).astype(BF16)
            total = total + dot(values_t[:, start : start + chunk], weight, 1, 0)
        mass = total[QUERY_ROWS : QUERY_ROWS + 1]
        inverse = 1.0 / mass
        low = (total[HEAD_SIZE:QUERY_ROWS] * inverse).astype(BF16)
        shift = dot(value_up, of_adapter(low, adapters), 0, 0)
        result = (total[0:HEAD_SIZE] * inverse + shift).astype(BF16)
        parts = split_float(peak * SCORE_SCALE + jnp.log(mass))
        stats = [part[:, tile * LANES : (tile + 1) * LANES] for tile in range(TILES) for part in parts]
        stats = jnp.concatenate(stats + [jnp.zeros((16 - len(stats), LANES), F32)], axis=0)
        for tile in range(TILES):
            message[head, tile * HEAD_SIZE : (tile + 1) * HEAD_SIZE, :] = result[
                :, tile * LANES : (tile + 1) * LANES
            ]
        message[head, TILES * HEAD_SIZE : RETURN_ROWS, :] = stats.astype(BF16)
        message[head, RETURN_ROWS:, :] = fresh[...]

    def two_heads(pair, carry):
        first = score_head(2 * pair, 0)
        second = score_head(2 * pair + 1, 1)
        sum_head(2 * pair, 0, first)
        sum_head(2 * pair + 1, 1, second)
        return carry

    lax.fori_loop(0, BLOCK // 2, two_heads, 0)


def merge_kernel(groups, partials, message):
    capacity = SLOTS // groups
    stats = [partials[member, TILES * HEAD_SIZE : RETURN_ROWS, :].astype(F32) for member in range(BLOCK)]
    results, masses = [], []
    for tile in range(TILES):
        first = 3 * tile
        logs = [s[first : first + 1] + s[first + 1 : first + 2] + s[first + 2 : first + 3] for s in stats]
        peak = functools.reduce(jnp.maximum, logs)
        weights = [jnp.exp(one - peak) for one in logs]
        whole = functools.reduce(jnp.add, weights)
        rows = slice(tile * HEAD_SIZE, (tile + 1) * HEAD_SIZE)
        total = jnp.zeros((HEAD_SIZE, LANES), F32)
        for member in range(BLOCK):
            total = total + partials[member, rows, :].astype(F32) * weights[member]
        results.append((total / whole).T.astype(BF16))
        parts = list(split_float(peak + jnp.log(whole)))
        parts = jnp.concatenate(parts + [jnp.zeros((LANES - 3, LANES), F32)], axis=0)
        masses.append(parts.T.astype(BF16))
    message[:, 0:capacity, :] = jnp.concatenate(results, axis=0).reshape(groups, capacity, HEAD_SIZE)
    message[:, capacity:, :] = jnp.concatenate(masses, axis=0).reshape(groups, capacity, LANES)


def finish_kernel(groups, received, placing, queries_t, partials, out):
    capacity = SLOTS // groups
    place = placing[...]
    shared = dot(received[:, 0:capacity, :].reshape(SLOTS, HEAD_SIZE), place, 0, 0)
    stats = dot(received[:, capacity:, :].reshape(SLOTS, LANES), place, 0, 0)
    log_mass = stats[0:1] + stats[1:2] + stats[2:3]
    new = partials[:, RETURN_ROWS:, :]
    key = new[0:X].reshape(HEAD_SIZE, LANES).astype(F32)
    value = new[X:].reshape(HEAD_SIZE, LANES).astype(F32)
    own = jnp.sum(queries_t[...].astype(F32) * key, axis=0, keepdims=True) * SCORE_SCALE
    peak = jnp.maximum(log_mass, own)
    shared_weight = jnp.exp(log_mass - peak)
    own_weight = jnp.exp(own - peak)
    result = (shared * shared_weight + value * own_weight) / (shared_weight + own_weight)
    out[...] = result.T.astype(BF16)


def per_device(
    residual_input,
    input_norm_gain,
    query_weight,
    key_value_weight,
    shared_down_factors,
    query_up_factors,
    key_value_up_factors,
    paged_base_keys,
    paged_base_values,
    paged_down_factors,
    adapter_of_row,
    document_of_row,
    document_page_slots,
):
    groups = lax.axis_size("grp")
    capacity = SLOTS // groups
    rows, part = residual_input.shape
    width = part * Y * X
    y_high = lax.axis_index("yh")
    device = (y_high * Y_LOW + lax.axis_index("yl")) * X + lax.axis_index("x")
    place = jnp.stack([device, y_high]).astype(jnp.int32)
    query_up = query_up_factors.reshape(-1, HEAD_SIZE)
    key_value_up = key_value_up_factors.reshape(-1, key_value_up_factors.shape[2])

    features = jnp.broadcast_to(residual_input.T[None], (Y, part, rows))
    features = lax.all_to_all(features, ("yh", "yl"), 0, 0, tiled=True)
    pieces = call(
        pack_kernel,
        shape(Y_HIGH, PIECE_ROWS, HEAD_SIZE),
        [VMEM] * 3,
        moved=3 * 1024 * 1024,
    )(
        paged_base_keys.reshape(PIECE_TOKENS, -1),
        paged_base_values.reshape(PIECE_TOKENS, -1),
        paged_down_factors.transpose(0, 2, 1).reshape(-1, LANES),
    )
    features, pieces = lax.optimization_barrier((features, pieces))
    pieces = lax.all_to_all(pieces, "yh", 0, 0, tiled=True)
    sources = [
        lax.ppermute(features, "x", [(i, (i - shift) % X) for i in range(X)]) if shift else features
        for shift in SHIFTS
    ]

    message, fresh, queries_t, placing = call(
        functools.partial(project_kernel, groups),
        [
            shape(groups, 2 * capacity, HEAD_SIZE),
            shape(FRESH_ROWS, rows),
            shape(HEAD_SIZE, rows),
            shape(SLOTS, rows),
        ],
        [SMEM, SMEM] + [VMEM] * X + [HBM, HBM, HBM, VMEM, HBM, HBM, VMEM, VMEM, ANY],
        [
            pltpu.VMEM((width, rows), BF16),
            pltpu.VMEM((width, HEAD_SIZE), BF16),
            pltpu.VMEM((FRESH_ROWS + 3 * RANK, width), BF16),
            pltpu.VMEM(query_up.shape, BF16),
            pltpu.VMEM((key_value_up.shape[0], HEAD_SIZE), BF16),
            pltpu.VMEM((HEAD_SIZE, rows), F32),
            pltpu.SemaphoreType.DMA((5,)),
        ],
        flops=2 * width * rows * 256,
        moved=6 * 1024 * 1024,
    )(
        place,
        document_page_slots,
        *sources,
        query_weight,
        key_value_weight.T,
        shared_down_factors.T,
        input_norm_gain.reshape(Y, X, part).transpose(1, 0, 2),
        query_up,
        key_value_up,
        adapter_of_row.reshape(1, rows),
        document_of_row.reshape(1, rows),
        pieces,
    )
    fresh = lax.ppermute(
        fresh,
        ("yh", "yl"),
        [(y, 2 * y if y < Y_HIGH else 2 * (y - Y_HIGH) + 1) for y in range(Y)],
    )
    received = lax.all_to_all(message, "grp", 0, 0, tiled=True)

    message, slot_adapters = call(
        functools.partial(factor_kernel, groups),
        [shape(BLOCK, MESSAGE_ROWS, LANES), shape(8, SLOTS, dtype=F32)],
        [SMEM] + [VMEM] * 2,
        flops=2 * 256 * 256 * 128,
        moved=1024 * 1024,
    )(place, received, key_value_up)
    gathered = lax.all_to_all(message, ("yl", "x"), 0, 0, tiled=True)

    tokens = PIECE_TOKENS * Y_HIGH
    keys, values_t = call(
        prepare_kernel,
        [shape(tokens, 2 * HEAD_SIZE), shape(QUERY_ROWS + 16, tokens)],
        [VMEM],
        moved=3 * 1024 * 1024,
    )(pieces)
    message = call(
        attend_kernel,
        shape(BLOCK, RETURN_ROWS + FRESH_ROWS, LANES),
        [SMEM] + [VMEM] * 6,
        [
            pltpu.VMEM((2, 2 * HEAD_SIZE, SLOTS), BF16),
            pltpu.VMEM((2, tokens, SLOTS), F32),
        ],
        flops=4 * SLOTS * BLOCK * tokens * 256,
        moved=3 * 1024 * 1024,
    )(place, gathered, slot_adapters, key_value_up, keys, values_t, fresh)
    partials = lax.all_to_all(message, ("yl", "x"), 0, 0, tiled=True)

    message = call(
        functools.partial(merge_kernel, groups),
        shape(groups, 2 * capacity, HEAD_SIZE),
        [VMEM],
        flops=SLOTS * HEAD_SIZE * 16,
        moved=1024 * 1024,
    )(partials)
    received = lax.all_to_all(message, "grp", 0, 0, tiled=True)

    return call(
        functools.partial(finish_kernel, groups),
        shape(rows, HEAD_SIZE),
        [VMEM] * 4,
        flops=2 * SLOTS * rows * 256,
        moved=1024 * 1024,
    )(received, placing, queries_t, partials)


def solution(mesh):
    groups = mesh.devices.shape[0]
    split = Mesh(
        mesh.devices.reshape(groups, Y_HIGH, Y_LOW, X), ("grp", "yh", "yl", "x")
    )
    tp = ("yh", "yl", "x")
    in_specs = (
        P("grp", tp),
        P(),
        P(None, tp),
        P(None, tp),
        P(),
        P(None, None, tp),
        P(),
        P(("grp",) + tp, None, None),
        P(("grp",) + tp, None, None),
        P(("grp",) + tp, None, None),
        P("grp"),
        P("grp", None),
        P(),
    )
    return jax.shard_map(
        per_device, mesh=split, in_specs=in_specs, out_specs=P("grp", tp), check_vma=False
    )
```

```python
import functools
import math

import jax
import jax.numpy as jnp
from jax import lax
from jax.experimental import pallas as pl
from jax.experimental.pallas import tpu as pltpu
from jax.sharding import Mesh, PartitionSpec as P

HEAD_SIZE = 128
RANK = 16
LANES = 128
Y_HIGH, Y_LOW, X = 4, 2, 4
Y = Y_HIGH * Y_LOW
BLOCK = Y_LOW * X
SLOTS = 256
TILES = SLOTS // LANES
QUERY_ROWS = HEAD_SIZE + RANK
MESSAGE_ROWS = TILES * QUERY_ROWS
RETURN_ROWS = TILES * HEAD_SIZE + 16
FRESH_ROWS = 32
DEPTH = 2 * HEAD_SIZE
VALUE_ROWS = QUERY_ROWS + 16
PIECE_TOKENS = 512
PIECE_ROWS = 2 * PIECE_TOKENS + 2 * RANK * PIECE_TOKENS // LANES
SHIFTS = (0, 1, 3, 2)
SCORE_SCALE = HEAD_SIZE**-0.5
F32 = jnp.float32
BF16 = jnp.bfloat16
VMEM = pl.BlockSpec(memory_space=pltpu.VMEM)
SMEM = pl.BlockSpec(memory_space=pltpu.SMEM)
ANY = pl.BlockSpec(memory_space=pl.ANY)


def dot(left, right, left_dim, right_dim):
    return lax.dot_general(
        left, right, (((left_dim,), (right_dim,)), ((), ())), preferred_element_type=F32
    )


def call(kernel, out_shape, in_specs, scratch=(), flops=0, moved=0, limit=32, out_specs=None):
    return pl.pallas_call(
        kernel,
        out_shape=out_shape,
        in_specs=in_specs,
        out_specs=out_specs or jax.tree.map(lambda _: VMEM, out_shape),
        scratch_shapes=list(scratch),
        compiler_params=pltpu.CompilerParams(vmem_limit_bytes=limit * 1024 * 1024),
        cost_estimate=pl.CostEstimate(flops=flops, bytes_accessed=moved, transcendentals=0),
    )


def shape(*dims, dtype=BF16):
    return jax.ShapeDtypeStruct(dims, dtype)


def of_adapter(low, adapters):
    repeated = jnp.concatenate([low] * 16, axis=0)
    adapter = lax.broadcasted_iota(jnp.int32, repeated.shape, 0) // RANK
    return jnp.where(adapter == adapters, repeated, jnp.zeros_like(repeated))


def split_float(value):
    high = value.astype(BF16).astype(F32)
    middle = (value - high).astype(BF16).astype(F32)
    return high, middle, value - high - middle


def pack_kernel(keys, values, factors, message):
    for head in range(Y_HIGH):
        columns = slice(head * HEAD_SIZE, (head + 1) * HEAD_SIZE)
        message[head, 0:PIECE_TOKENS, :] = keys[:, columns]
        message[head, PIECE_TOKENS : 2 * PIECE_TOKENS, :] = values[:, columns]
        message[head, 2 * PIECE_TOKENS :, :] = factors[...]


def plan_kernel(
    groups,
    page_slots,
    query_weight,
    key_value_weight,
    down,
    adapters,
    documents,
    weights,
    placing,
    slot_adapters,
):
    for start in range(0, weights.shape[1], LANES):
        block = query_weight[start : start + LANES, :].astype(F32).T
        weights[0:HEAD_SIZE, start : start + LANES] = block.astype(BF16)
    weights[HEAD_SIZE : HEAD_SIZE + FRESH_ROWS, :] = key_value_weight[...]
    weights[HEAD_SIZE + FRESH_ROWS :, :] = down[...]

    document = documents[...]
    rows = document.shape[1]
    target = jnp.zeros_like(document)
    for d in range(page_slots.shape[0]):
        target = jnp.where(document == d, page_slots[d, 0] // page_slots.shape[1], target)
    capacity = SLOTS // groups
    group = lax.broadcasted_iota(jnp.int32, (16, rows), 0)
    match = (group == target).astype(F32)
    before = (
        lax.broadcasted_iota(jnp.int32, (rows, rows), 0)
        < lax.broadcasted_iota(jnp.int32, (rows, rows), 1)
    ).astype(F32)
    earlier = dot(match.astype(BF16), before.astype(BF16), 1, 0)
    position = jnp.sum(earlier * match, axis=0, keepdims=True).astype(jnp.int32)
    slot = target * capacity + position
    placed = (lax.broadcasted_iota(jnp.int32, (SLOTS, rows), 0) == slot).astype(F32)
    placing[...] = placed.astype(BF16)
    adapter = jnp.sum(placed * adapters[...].astype(F32), axis=1, keepdims=True)
    slot_adapters[...] = jnp.broadcast_to(adapter, (SLOTS, LANES)).astype(BF16)


def project_kernel(
    groups,
    place,
    features_0,
    features_1,
    features_2,
    features_3,
    weights,
    gain,
    query_up,
    key_value_up,
    adapters,
    placing,
    slot_adapters,
    held,
    message,
    fresh,
    queries_t,
    normed,
    update,
):
    device = place[0]
    part = gain.shape[2]
    width = normed.shape[0]
    sources = (features_0, features_1, features_2, features_3)

    squares = jnp.zeros((part, normed.shape[1]), F32)
    for features in sources:
        for y in range(Y):
            block = features[y].astype(F32)
            squares = squares + block * block
    scale = lax.rsqrt(jnp.sum(squares, axis=0, keepdims=True) / width + 1e-06)
    for shift, features in zip(SHIFTS, sources):
        x = lax.rem(device + shift, X)
        gain_t = gain[x].T
        for y in range(Y):
            block = features[y].astype(F32) * scale * gain_t[:, y : y + 1]
            start = pl.multiple_of((y * X + x) * part, 32)
            normed[pl.ds(start, part), :] = block.astype(BF16)
    total = dot(weights[...], normed[...], 1, 0)

    adapter = adapters[...]
    low = total[HEAD_SIZE + FRESH_ROWS :].astype(BF16)
    query_update = dot(query_up[...], of_adapter(low[0:RANK], adapter), 0, 0)
    queries = (total[0:HEAD_SIZE] + query_update).astype(BF16)
    queries_t[...] = queries

    is_key = device < Y * X // 2
    low_kv = jnp.where(is_key, low[RANK : 2 * RANK], low[2 * RANK :])
    columns = pl.ds(pl.multiple_of(device // X * HEAD_SIZE, HEAD_SIZE), HEAD_SIZE)
    update[...] = dot(key_value_up[:, columns], of_adapter(low_kv, adapter), 0, 0)
    mine = pl.ds(pl.multiple_of(lax.rem(device, X) * FRESH_ROWS, FRESH_ROWS), FRESH_ROWS)
    new = total[HEAD_SIZE : HEAD_SIZE + FRESH_ROWS] + update[mine, :]
    fresh[...] = new.astype(BF16)

    capacity = SLOTS // groups
    placed = dot(placing[...], queries, 1, 1).astype(BF16)
    message[:, 0:capacity, :] = placed.reshape(groups, capacity, HEAD_SIZE)
    message[:, capacity:, :] = slot_adapters[...].reshape(groups, capacity, LANES)


def factor_kernel(groups, place, received, key_value_up, message, slot_adapters):
    capacity = SLOTS // groups
    queries = received[:, 0:capacity, :].reshape(SLOTS, HEAD_SIZE)
    queries_t = queries.astype(F32).T.astype(BF16)
    adapters = received[:, capacity:, :].reshape(SLOTS, LANES).astype(F32).T[0:1]
    slot_adapters[...] = jnp.broadcast_to(adapters, slot_adapters.shape)
    columns = pl.ds(pl.multiple_of(place[1] * HEAD_SIZE, HEAD_SIZE), HEAD_SIZE)
    every = dot(key_value_up[:, columns], queries, 1, 1)
    adapter = (lax.broadcasted_iota(jnp.int32, every.shape, 0) // RANK).astype(F32)
    kept = jnp.where(adapter == adapters, every, 0.0)
    factors = kept[0:RANK]
    for a in range(1, 16):
        factors = factors + kept[a * RANK : (a + 1) * RANK]
    factors = factors.astype(BF16)
    for member in range(BLOCK):
        for tile in range(TILES):
            lanes = slice(tile * LANES, (tile + 1) * LANES)
            start = tile * QUERY_ROWS
            message[member, start : start + HEAD_SIZE, :] = queries_t[:, lanes]
            message[member, start + HEAD_SIZE : start + QUERY_ROWS, :] = factors[:, lanes]


def prepare_kernel(pieces, prepared):
    tokens = PIECE_TOKENS * Y_HIGH
    ones = lax.broadcasted_iota(jnp.int32, (VALUE_ROWS - QUERY_ROWS, DEPTH), 0) == 0
    for index in range(Y_HIGH):
        for page in range(PIECE_TOKENS // LANES):
            start = page * LANES
            token = index * PIECE_TOKENS + start
            here = slice(token, token + LANES)
            row = 2 * PIECE_TOKENS + page * 2 * RANK
            factors = pieces[index, row : row + 2 * RANK, :]
            key_factors = jnp.concatenate(
                [factors[0:RANK].astype(F32), jnp.zeros((LANES - RANK, LANES), F32)], axis=0
            )
            prepared[here, 0:HEAD_SIZE] = pieces[index, start : start + LANES, :]
            prepared[here, HEAD_SIZE:] = key_factors.T.astype(BF16)
            value = pieces[index, PIECE_TOKENS + start : PIECE_TOKENS + start + LANES, :]
            base = tokens + token // DEPTH * VALUE_ROWS
            lanes = slice(token % DEPTH, token % DEPTH + LANES)
            prepared[base : base + HEAD_SIZE, lanes] = value.astype(F32).T.astype(BF16)
            prepared[base + HEAD_SIZE : base + QUERY_ROWS, lanes] = factors[RANK:]
            if token % DEPTH == 0:
                prepared[base + QUERY_ROWS : base + VALUE_ROWS, :] = ones.astype(F32).astype(BF16)


def attend_kernel(
    place, queries, slot_adapters, key_value_up, prepared, fresh, message, query, scores, totals, peaks
):
    tokens = PIECE_TOKENS * Y_HIGH
    chunk = 1024
    exponent = SCORE_SCALE * math.log2(math.e)
    query[:, QUERY_ROWS:, :] = jnp.zeros((2, DEPTH - QUERY_ROWS, SLOTS), BF16)

    def load(head, side):
        for tile in range(TILES):
            query[side, 0:QUERY_ROWS, tile * LANES : (tile + 1) * LANES] = queries[
                head, tile * QUERY_ROWS : (tile + 1) * QUERY_ROWS, :
            ]

    def score(side, start, highest):
        block = dot(prepared[start : start + chunk, :], query[side], 1, 0)
        scores[side, start : start + chunk, :] = block
        return jnp.maximum(highest, jnp.max(block.reshape(chunk // 8, 8, SLOTS), axis=0))

    def add(side, start, peak, total):
        weight = jnp.exp2(scores[side, start : start + chunk, :] * exponent - peak).astype(BF16)
        for step in range(chunk // DEPTH):
            base = tokens + (start // DEPTH + step) * VALUE_ROWS
            values = prepared[base : base + VALUE_ROWS, :]
            total = total + dot(values, weight[step * DEPTH : (step + 1) * DEPTH], 1, 0)
        return total

    lowest = jnp.full((8, SLOTS), -jnp.inf, F32)

    def one_head(head, following, side, peak):
        load(following, 1 - side)
        highest, total = lowest, jnp.zeros((VALUE_ROWS, SLOTS), F32)
        for start in range(0, tokens, chunk):
            highest = score(1 - side, start, highest)
            total = add(side, start, peak * exponent, total)
        totals[head] = total
        peaks[head] = jnp.broadcast_to(peak, (8, SLOTS))
        return jnp.max(highest, axis=0, keepdims=True)

    def two_heads(pair, peak):
        peak = one_head(2 * pair, 2 * pair + 1, 0, peak)
        return one_head(2 * pair + 1, jnp.minimum(2 * pair + 2, BLOCK - 1), 1, peak)

    load(0, 0)
    highest = lowest
    for start in range(0, tokens, chunk):
        highest = score(0, start, highest)
    lax.fori_loop(0, BLOCK // 2, two_heads, jnp.max(highest, axis=0, keepdims=True))

    columns = pl.ds(pl.multiple_of((place[1] + Y_HIGH) * HEAD_SIZE, HEAD_SIZE), HEAD_SIZE)
    value_up = key_value_up[:, columns]
    adapters = slot_adapters[0:1, :].astype(jnp.int32)
    for head in range(BLOCK):
        total, peak = totals[head], peaks[head, 0:1]
        mass = total[QUERY_ROWS : QUERY_ROWS + 1]
        inverse = 1.0 / mass
        low = (total[HEAD_SIZE:QUERY_ROWS] * inverse).astype(BF16)
        shift = dot(value_up, of_adapter(low, adapters), 0, 0)
        result = (total[0:HEAD_SIZE] * inverse + shift).astype(BF16)
        parts = split_float(peak * SCORE_SCALE + jnp.log(mass))
        stats = [part[:, tile * LANES : (tile + 1) * LANES] for tile in range(TILES) for part in parts]
        stats = jnp.concatenate(stats + [jnp.zeros((16 - len(stats), LANES), F32)], axis=0)
        for tile in range(TILES):
            message[head, tile * HEAD_SIZE : (tile + 1) * HEAD_SIZE, :] = result[
                :, tile * LANES : (tile + 1) * LANES
            ]
        message[head, TILES * HEAD_SIZE : RETURN_ROWS, :] = stats.astype(BF16)
        message[head, RETURN_ROWS:, :] = fresh[...]


def merge_kernel(groups, partials, message):
    capacity = SLOTS // groups
    stats = [partials[member, TILES * HEAD_SIZE : RETURN_ROWS, :].astype(F32) for member in range(BLOCK)]
    results, masses = [], []
    for tile in range(TILES):
        first = 3 * tile
        logs = [s[first : first + 1] + s[first + 1 : first + 2] + s[first + 2 : first + 3] for s in stats]
        peak = functools.reduce(jnp.maximum, logs)
        weights = [jnp.exp(one - peak) for one in logs]
        whole = functools.reduce(jnp.add, weights)
        rows = slice(tile * HEAD_SIZE, (tile + 1) * HEAD_SIZE)
        total = jnp.zeros((HEAD_SIZE, LANES), F32)
        for member in range(BLOCK):
            total = total + partials[member, rows, :].astype(F32) * weights[member]
        results.append((total / whole).T.astype(BF16))
        parts = list(split_float(peak + jnp.log(whole)))
        parts = jnp.concatenate(parts + [jnp.zeros((LANES - 3, LANES), F32)], axis=0)
        masses.append(parts.T.astype(BF16))
    message[:, 0:capacity, :] = jnp.concatenate(results, axis=0).reshape(groups, capacity, HEAD_SIZE)
    message[:, capacity:, :] = jnp.concatenate(masses, axis=0).reshape(groups, capacity, LANES)


def finish_kernel(groups, received, placing, queries_t, partials, out):
    capacity = SLOTS // groups
    place = placing[...]
    shared = dot(received[:, 0:capacity, :].reshape(SLOTS, HEAD_SIZE), place, 0, 0)
    stats = dot(received[:, capacity:, :].reshape(SLOTS, LANES), place, 0, 0)
    log_mass = stats[0:1] + stats[1:2] + stats[2:3]
    new = partials[:, RETURN_ROWS:, :]
    key = new[0:X].reshape(HEAD_SIZE, LANES).astype(F32)
    value = new[X:].reshape(HEAD_SIZE, LANES).astype(F32)
    own = jnp.sum(queries_t[...].astype(F32) * key, axis=0, keepdims=True) * SCORE_SCALE
    peak = jnp.maximum(log_mass, own)
    shared_weight = jnp.exp(log_mass - peak)
    own_weight = jnp.exp(own - peak)
    result = (shared * shared_weight + value * own_weight) / (shared_weight + own_weight)
    out[...] = result.T.astype(BF16)


def per_device(
    residual_input,
    input_norm_gain,
    query_weight,
    key_value_weight,
    shared_down_factors,
    query_up_factors,
    key_value_up_factors,
    paged_base_keys,
    paged_base_values,
    paged_down_factors,
    adapter_of_row,
    document_of_row,
    document_page_slots,
):
    groups = lax.axis_size("grp")
    capacity = SLOTS // groups
    rows, part = residual_input.shape
    width = part * Y * X
    y_high = lax.axis_index("yh")
    device = (y_high * Y_LOW + lax.axis_index("yl")) * X + lax.axis_index("x")
    place = jnp.stack([device, y_high]).astype(jnp.int32)
    query_up = query_up_factors.reshape(-1, HEAD_SIZE)
    key_value_up = key_value_up_factors.reshape(-1, key_value_up_factors.shape[2])

    features = jnp.broadcast_to(residual_input.T[None], (Y, part, rows))
    features = lax.all_to_all(features, ("yh", "yl"), 0, 0, tiled=True)
    pieces = call(
        pack_kernel,
        shape(Y_HIGH, PIECE_ROWS, HEAD_SIZE),
        [VMEM] * 3,
        moved=3 * 1024 * 1024,
    )(
        paged_base_keys.reshape(PIECE_TOKENS, -1),
        paged_base_values.reshape(PIECE_TOKENS, -1),
        paged_down_factors.transpose(0, 2, 1).reshape(-1, LANES),
    )
    features, pieces = lax.optimization_barrier((features, pieces))
    pieces = lax.all_to_all(pieces, "yh", 0, 0, tiled=True)
    sources = [
        lax.ppermute(features, "x", [(i, (i - shift) % X) for i in range(X)]) if shift else features
        for shift in SHIFTS
    ]

    columns = HEAD_SIZE + FRESH_ROWS + 3 * RANK
    adapters = adapter_of_row.reshape(1, rows)
    weights, placing, row_adapters = call(
        functools.partial(plan_kernel, groups),
        [shape(columns, width), shape(SLOTS, rows), shape(SLOTS, LANES)],
        [SMEM] + [VMEM] * 5,
        moved=5 * 1024 * 1024,
    )(
        document_page_slots,
        query_weight,
        key_value_weight.T,
        shared_down_factors.T,
        adapters,
        document_of_row.reshape(1, rows),
    )
    message, fresh, queries_t = call(
        functools.partial(project_kernel, groups),
        [
            shape(groups, 2 * capacity, HEAD_SIZE),
            shape(FRESH_ROWS, rows),
            shape(HEAD_SIZE, rows),
        ],
        [SMEM] + [VMEM] * (X + 7) + [ANY],
        [pltpu.VMEM((width, rows), BF16), pltpu.VMEM((HEAD_SIZE, rows), F32)],
        flops=2 * width * rows * 256,
        moved=4 * 1024 * 1024,
    )(
        place,
        *sources,
        weights,
        input_norm_gain.reshape(Y, X, part).transpose(1, 0, 2),
        query_up,
        key_value_up,
        adapters,
        placing,
        row_adapters,
        pieces,
    )
    fresh = lax.ppermute(
        fresh,
        ("yh", "yl"),
        [(y, 2 * y if y < Y_HIGH else 2 * (y - Y_HIGH) + 1) for y in range(Y)],
    )
    received = lax.all_to_all(message, "grp", 0, 0, tiled=True)

    message, slot_adapters = call(
        functools.partial(factor_kernel, groups),
        [shape(BLOCK, MESSAGE_ROWS, LANES), shape(8, SLOTS, dtype=F32)],
        [SMEM] + [VMEM] * 2,
        flops=2 * 256 * 256 * 128,
        moved=1024 * 1024,
    )(place, received, key_value_up)
    gathered = lax.all_to_all(message, ("yl", "x"), 0, 0, tiled=True)

    tokens = PIECE_TOKENS * Y_HIGH
    prepared = call(
        prepare_kernel,
        shape(tokens + tokens // DEPTH * VALUE_ROWS, DEPTH),
        [VMEM],
        moved=3 * 1024 * 1024,
    )(pieces)
    message = call(
        attend_kernel,
        shape(BLOCK, RETURN_ROWS + FRESH_ROWS, LANES),
        [SMEM] + [VMEM] * 5,
        [
            pltpu.VMEM((2, DEPTH, SLOTS), BF16),
            pltpu.VMEM((2, tokens, SLOTS), F32),
            pltpu.VMEM((BLOCK, VALUE_ROWS, SLOTS), F32),
            pltpu.VMEM((BLOCK, 8, SLOTS), F32),
        ],
        flops=4 * SLOTS * BLOCK * tokens * 256,
        moved=3 * 1024 * 1024,
    )(place, gathered, slot_adapters, key_value_up, prepared, fresh)
    partials = lax.all_to_all(message, ("yl", "x"), 0, 0, tiled=True)

    message = call(
        functools.partial(merge_kernel, groups),
        shape(groups, 2 * capacity, HEAD_SIZE),
        [VMEM],
        flops=SLOTS * HEAD_SIZE * 16,
        moved=1024 * 1024,
    )(partials)
    received = lax.all_to_all(message, "grp", 0, 0, tiled=True)

    return call(
        functools.partial(finish_kernel, groups),
        shape(rows, HEAD_SIZE),
        [VMEM] * 4,
        flops=2 * SLOTS * rows * 256,
        moved=1024 * 1024,
    )(received, placing, queries_t, partials)


def solution(mesh):
    groups = mesh.devices.shape[0]
    split = Mesh(
        mesh.devices.reshape(groups, Y_HIGH, Y_LOW, X), ("grp", "yh", "yl", "x")
    )
    tp = ("yh", "yl", "x")
    in_specs = (
        P("grp", tp),
        P(),
        P(None, tp),
        P(None, tp),
        P(),
        P(None, None, tp),
        P(),
        P(("grp",) + tp, None, None),
        P(("grp",) + tp, None, None),
        P(("grp",) + tp, None, None),
        P("grp"),
        P("grp", None),
        P(),
    )
    return jax.shard_map(
        per_device, mesh=split, in_specs=in_specs, out_specs=P("grp", tp), check_vma=False
    )
```

```python
import functools
import math

import jax
import jax.numpy as jnp
from jax import lax
from jax.experimental import pallas as pl
from jax.experimental.pallas import tpu as pltpu
from jax.sharding import Mesh, PartitionSpec as P

HEAD_SIZE = 128
RANK = 16
LANES = 128
Y_HIGH, Y_LOW, X = 4, 2, 4
Y = Y_HIGH * Y_LOW
BLOCK = Y_LOW * X
SLOTS = 256
TILES = SLOTS // LANES
QUERY_ROWS = HEAD_SIZE + RANK
MESSAGE_ROWS = TILES * QUERY_ROWS
RETURN_ROWS = TILES * HEAD_SIZE + 16
FRESH_ROWS = 32
DEPTH = 2 * HEAD_SIZE
VALUE_ROWS = QUERY_ROWS + 16
OWN_UP, KEY_UP, VALUE_UP, QUERY_UP, PLACING = range(5)
PIECE_TOKENS = 512
PIECE_ROWS = 2 * PIECE_TOKENS + 2 * RANK * PIECE_TOKENS // LANES
SHIFTS = (0, 1, 3, 2)
SCORE_SCALE = HEAD_SIZE**-0.5
F32 = jnp.float32
BF16 = jnp.bfloat16
VMEM = pl.BlockSpec(memory_space=pltpu.VMEM)
SMEM = pl.BlockSpec(memory_space=pltpu.SMEM)
ANY = pl.BlockSpec(memory_space=pl.ANY)


def dot(left, right, left_dim, right_dim):
    return lax.dot_general(
        left, right, (((left_dim,), (right_dim,)), ((), ())), preferred_element_type=F32
    )


def call(kernel, out_shape, in_specs, scratch=(), flops=0, moved=0, limit=16, out_specs=None):
    return pl.pallas_call(
        kernel,
        out_shape=out_shape,
        in_specs=in_specs,
        out_specs=out_specs or jax.tree.map(lambda _: VMEM, out_shape),
        scratch_shapes=list(scratch),
        compiler_params=pltpu.CompilerParams(vmem_limit_bytes=limit * 1024 * 1024),
        cost_estimate=pl.CostEstimate(flops=flops, bytes_accessed=moved, transcendentals=0),
    )


def shape(*dims, dtype=BF16):
    return jax.ShapeDtypeStruct(dims, dtype)


def of_adapter(low, adapters):
    repeated = jnp.concatenate([low] * 16, axis=0)
    adapter = lax.broadcasted_iota(jnp.int32, repeated.shape, 0) // RANK
    return jnp.where(adapter == adapters, repeated, jnp.zeros_like(repeated))


def split_float(value):
    high = value.astype(BF16).astype(F32)
    middle = (value - high).astype(BF16).astype(F32)
    return high, middle, value - high - middle


def pack_kernel(keys, values, factors, message):
    for head in range(Y_HIGH):
        columns = slice(head * HEAD_SIZE, (head + 1) * HEAD_SIZE)
        message[head, 0:PIECE_TOKENS, :] = keys[:, columns]
        message[head, PIECE_TOKENS : 2 * PIECE_TOKENS, :] = values[:, columns]
        message[head, 2 * PIECE_TOKENS :, :] = factors[...]


def plan_kernel(
    groups,
    place,
    page_slots,
    query_weight,
    key_value_weight,
    down,
    query_up,
    key_value_up,
    documents,
    weights,
    smalls,
):
    for start in range(0, weights.shape[1], LANES):
        block = query_weight[start : start + LANES, :].astype(F32).T
        weights[0:HEAD_SIZE, start : start + LANES] = block.astype(BF16)
    weights[HEAD_SIZE : HEAD_SIZE + FRESH_ROWS, :] = key_value_weight[...]
    weights[HEAD_SIZE + FRESH_ROWS :, :] = down[...]
    for index, head in enumerate((place[0] // X, place[1], place[1] + Y_HIGH)):
        columns = pl.ds(pl.multiple_of(head * HEAD_SIZE, HEAD_SIZE), HEAD_SIZE)
        smalls[index] = key_value_up[:, columns]
    smalls[QUERY_UP] = query_up[...]

    document = documents[...]
    rows = document.shape[1]
    target = jnp.zeros_like(document)
    for d in range(page_slots.shape[0]):
        target = jnp.where(document == d, page_slots[d, 0] // page_slots.shape[1], target)
    capacity = SLOTS // groups
    group = lax.broadcasted_iota(jnp.int32, (16, rows), 0)
    match = (group == target).astype(F32)
    before = (
        lax.broadcasted_iota(jnp.int32, (rows, rows), 0)
        < lax.broadcasted_iota(jnp.int32, (rows, rows), 1)
    ).astype(F32)
    earlier = dot(match.astype(BF16), before.astype(BF16), 1, 0)
    position = jnp.sum(earlier * match, axis=0, keepdims=True).astype(jnp.int32)
    slot = target * capacity + position
    placed = (lax.broadcasted_iota(jnp.int32, (SLOTS, rows), 0) == slot).astype(F32)
    smalls[PLACING] = placed.astype(BF16)


def project_kernel(
    groups,
    place,
    features_0,
    features_1,
    features_2,
    features_3,
    weights,
    gain,
    smalls,
    adapters,
    message,
    fresh,
    queries_t,
    normed,
    update,
):
    device = place[0]
    part = gain.shape[2]
    width = normed.shape[0]
    sources = (features_0, features_1, features_2, features_3)

    squares = jnp.zeros((part, normed.shape[1]), F32)
    for features in sources:
        for y in range(Y):
            block = features[y].astype(F32)
            squares = squares + block * block
    scale = lax.rsqrt(jnp.sum(squares, axis=0, keepdims=True) / width + 1e-06)
    for shift, features in zip(SHIFTS, sources):
        x = lax.rem(device + shift, X)
        gain_t = gain[x].T
        for y in range(Y):
            block = features[y].astype(F32) * scale * gain_t[:, y : y + 1]
            start = pl.multiple_of((y * X + x) * part, 32)
            normed[pl.ds(start, part), :] = block.astype(BF16)
    total = dot(weights[...], normed[...], 1, 0)

    adapter = adapters[...]
    low = total[HEAD_SIZE + FRESH_ROWS :].astype(BF16)
    query_update = dot(smalls[QUERY_UP], of_adapter(low[0:RANK], adapter), 0, 0)
    queries = (total[0:HEAD_SIZE] + query_update).astype(BF16)
    queries_t[...] = queries

    is_key = device < Y * X // 2
    low_kv = jnp.where(is_key, low[RANK : 2 * RANK], low[2 * RANK :])
    update[...] = dot(smalls[OWN_UP], of_adapter(low_kv, adapter), 0, 0)
    mine = pl.ds(pl.multiple_of(lax.rem(device, X) * FRESH_ROWS, FRESH_ROWS), FRESH_ROWS)
    new = total[HEAD_SIZE : HEAD_SIZE + FRESH_ROWS] + update[mine, :]
    fresh[...] = new.astype(BF16)

    every = dot(smalls[KEY_UP], queries, 1, 0)
    of_row = lax.broadcasted_iota(jnp.int32, every.shape, 0) // RANK == adapter
    kept = jnp.where(of_row, every, 0.0)
    factors = kept[0:RANK]
    for a in range(1, 16):
        factors = factors + kept[a * RANK : (a + 1) * RANK]
    rest = jnp.zeros((HEAD_SIZE - RANK - 1, factors.shape[1]), F32)
    beside = jnp.concatenate([factors, adapter.astype(F32), rest], axis=0).astype(BF16)

    capacity = SLOTS // groups
    place_rows = smalls[PLACING]
    placed = dot(place_rows, queries, 1, 1).astype(BF16)
    message[:, 0:capacity, :] = placed.reshape(groups, capacity, HEAD_SIZE)
    placed = dot(place_rows, beside, 1, 1).astype(BF16)
    message[:, capacity:, :] = placed.reshape(groups, capacity, LANES)


def turn_kernel(groups, received, message, slot_adapters):
    capacity = SLOTS // groups
    queries = received[:, 0:capacity, :].reshape(SLOTS, HEAD_SIZE).astype(F32).T.astype(BF16)
    beside = received[:, capacity:, :].reshape(SLOTS, LANES).astype(F32).T
    slot_adapters[...] = jnp.broadcast_to(beside[RANK : RANK + 1], slot_adapters.shape)
    factors = beside[0:RANK].astype(BF16)
    for member in range(BLOCK):
        for tile in range(TILES):
            lanes = slice(tile * LANES, (tile + 1) * LANES)
            start = tile * QUERY_ROWS
            message[member, start : start + HEAD_SIZE, :] = queries[:, lanes]
            message[member, start + HEAD_SIZE : start + QUERY_ROWS, :] = factors[:, lanes]


def prepare_kernel(pieces, prepared):
    tokens = PIECE_TOKENS * Y_HIGH
    ones = lax.broadcasted_iota(jnp.int32, (VALUE_ROWS - QUERY_ROWS, DEPTH), 0) == 0
    for index in range(Y_HIGH):
        for page in range(PIECE_TOKENS // LANES):
            start = page * LANES
            token = index * PIECE_TOKENS + start
            here = slice(token, token + LANES)
            row = 2 * PIECE_TOKENS + page * 2 * RANK
            factors = pieces[index, row : row + 2 * RANK, :]
            key_factors = jnp.concatenate(
                [factors[0:RANK].astype(F32), jnp.zeros((LANES - RANK, LANES), F32)], axis=0
            )
            prepared[here, 0:HEAD_SIZE] = pieces[index, start : start + LANES, :]
            prepared[here, HEAD_SIZE:] = key_factors.T.astype(BF16)
            value = pieces[index, PIECE_TOKENS + start : PIECE_TOKENS + start + LANES, :]
            base = tokens + token // DEPTH * VALUE_ROWS
            lanes = slice(token % DEPTH, token % DEPTH + LANES)
            prepared[base : base + HEAD_SIZE, lanes] = value.astype(F32).T.astype(BF16)
            prepared[base + HEAD_SIZE : base + QUERY_ROWS, lanes] = factors[RANK:]
            if token % DEPTH == 0:
                prepared[base + QUERY_ROWS : base + VALUE_ROWS, :] = ones.astype(F32).astype(BF16)


def attend_kernel(
    queries, slot_adapters, smalls, prepared, fresh, message, query, scores, totals, peaks
):
    tokens = PIECE_TOKENS * Y_HIGH
    chunk = 1024
    exponent = SCORE_SCALE * math.log2(math.e)
    query[:, QUERY_ROWS:, :] = jnp.zeros((2, DEPTH - QUERY_ROWS, SLOTS), BF16)

    def load(head, side):
        for tile in range(TILES):
            query[side, 0:QUERY_ROWS, tile * LANES : (tile + 1) * LANES] = queries[
                head, tile * QUERY_ROWS : (tile + 1) * QUERY_ROWS, :
            ]

    def score(side, start, highest):
        block = dot(prepared[start : start + chunk, :], query[side], 1, 0)
        scores[side, start : start + chunk, :] = block
        return jnp.maximum(highest, jnp.max(block.reshape(chunk // 8, 8, SLOTS), axis=0))

    def add(side, start, peak, total):
        weight = jnp.exp2(scores[side, start : start + chunk, :] * exponent - peak).astype(BF16)
        for step in range(chunk // DEPTH):
            base = tokens + (start // DEPTH + step) * VALUE_ROWS
            values = prepared[base : base + VALUE_ROWS, :]
            total = total + dot(values, weight[step * DEPTH : (step + 1) * DEPTH], 1, 0)
        return total

    lowest = jnp.full((8, SLOTS), -jnp.inf, F32)

    def one_head(head, following, side, peak):
        load(following, 1 - side)
        highest, total = lowest, jnp.zeros((VALUE_ROWS, SLOTS), F32)
        for start in range(0, tokens, chunk):
            highest = score(1 - side, start, highest)
            total = add(side, start, peak * exponent, total)
        totals[head] = total
        peaks[head] = jnp.broadcast_to(peak, (8, SLOTS))
        return jnp.max(highest, axis=0, keepdims=True)

    def two_heads(pair, peak):
        peak = one_head(2 * pair, 2 * pair + 1, 0, peak)
        return one_head(2 * pair + 1, jnp.minimum(2 * pair + 2, BLOCK - 1), 1, peak)

    load(0, 0)
    highest = lowest
    for start in range(0, tokens, chunk):
        highest = score(0, start, highest)
    lax.fori_loop(0, BLOCK // 2, two_heads, jnp.max(highest, axis=0, keepdims=True))

    value_up = smalls[VALUE_UP]
    adapters = slot_adapters[0:1, :].astype(jnp.int32)
    for head in range(BLOCK):
        total, peak = totals[head], peaks[head, 0:1]
        mass = total[QUERY_ROWS : QUERY_ROWS + 1]
        inverse = 1.0 / mass
        low = (total[HEAD_SIZE:QUERY_ROWS] * inverse).astype(BF16)
        shift = dot(value_up, of_adapter(low, adapters), 0, 0)
        result = (total[0:HEAD_SIZE] * inverse + shift).astype(BF16)
        parts = split_float(peak * SCORE_SCALE + jnp.log(mass))
        stats = [part[:, tile * LANES : (tile + 1) * LANES] for tile in range(TILES) for part in parts]
        stats = jnp.concatenate(stats + [jnp.zeros((16 - len(stats), LANES), F32)], axis=0)
        for tile in range(TILES):
            message[head, tile * HEAD_SIZE : (tile + 1) * HEAD_SIZE, :] = result[
                :, tile * LANES : (tile + 1) * LANES
            ]
        message[head, TILES * HEAD_SIZE : RETURN_ROWS, :] = stats.astype(BF16)
        message[head, RETURN_ROWS:, :] = fresh[...]


def merge_kernel(groups, partials, message):
    capacity = SLOTS // groups
    stats = [partials[member, TILES * HEAD_SIZE : RETURN_ROWS, :].astype(F32) for member in range(BLOCK)]
    results, masses = [], []
    for tile in range(TILES):
        first = 3 * tile
        logs = [s[first : first + 1] + s[first + 1 : first + 2] + s[first + 2 : first + 3] for s in stats]
        peak = functools.reduce(jnp.maximum, logs)
        weights = [jnp.exp(one - peak) for one in logs]
        whole = functools.reduce(jnp.add, weights)
        rows = slice(tile * HEAD_SIZE, (tile + 1) * HEAD_SIZE)
        total = jnp.zeros((HEAD_SIZE, LANES), F32)
        for member in range(BLOCK):
            total = total + partials[member, rows, :].astype(F32) * weights[member]
        results.append((total / whole).T.astype(BF16))
        parts = list(split_float(peak + jnp.log(whole)))
        parts = jnp.concatenate(parts + [jnp.zeros((LANES - 3, LANES), F32)], axis=0)
        masses.append(parts.T.astype(BF16))
    message[:, 0:capacity, :] = jnp.concatenate(results, axis=0).reshape(groups, capacity, HEAD_SIZE)
    message[:, capacity:, :] = jnp.concatenate(masses, axis=0).reshape(groups, capacity, LANES)


def finish_kernel(groups, received, smalls, queries_t, partials, out):
    capacity = SLOTS // groups
    place = smalls[PLACING]
    shared = dot(received[:, 0:capacity, :].reshape(SLOTS, HEAD_SIZE), place, 0, 0)
    stats = dot(received[:, capacity:, :].reshape(SLOTS, LANES), place, 0, 0)
    log_mass = stats[0:1] + stats[1:2] + stats[2:3]
    new = partials[:, RETURN_ROWS:, :]
    key = new[0:X].reshape(HEAD_SIZE, LANES).astype(F32)
    value = new[X:].reshape(HEAD_SIZE, LANES).astype(F32)
    own = jnp.sum(queries_t[...].astype(F32) * key, axis=0, keepdims=True) * SCORE_SCALE
    peak = jnp.maximum(log_mass, own)
    shared_weight = jnp.exp(log_mass - peak)
    own_weight = jnp.exp(own - peak)
    result = (shared * shared_weight + value * own_weight) / (shared_weight + own_weight)
    out[...] = result.T.astype(BF16)


def per_device(
    residual_input,
    input_norm_gain,
    query_weight,
    key_value_weight,
    shared_down_factors,
    query_up_factors,
    key_value_up_factors,
    paged_base_keys,
    paged_base_values,
    paged_down_factors,
    adapter_of_row,
    document_of_row,
    document_page_slots,
):
    groups = lax.axis_size("grp")
    capacity = SLOTS // groups
    rows, part = residual_input.shape
    width = part * Y * X
    y_high = lax.axis_index("yh")
    device = (y_high * Y_LOW + lax.axis_index("yl")) * X + lax.axis_index("x")
    place = jnp.stack([device, y_high]).astype(jnp.int32)
    query_up = query_up_factors.reshape(-1, HEAD_SIZE)
    key_value_up = key_value_up_factors.reshape(-1, key_value_up_factors.shape[2])

    features = jnp.broadcast_to(residual_input.T[None], (Y, part, rows))
    features = lax.all_to_all(features, ("yh", "yl"), 0, 0, tiled=True)
    pieces = call(
        pack_kernel,
        shape(Y_HIGH, PIECE_ROWS, HEAD_SIZE),
        [VMEM] * 3,
        moved=3 * 1024 * 1024,
    )(
        paged_base_keys.reshape(PIECE_TOKENS, -1),
        paged_base_values.reshape(PIECE_TOKENS, -1),
        paged_down_factors.transpose(0, 2, 1).reshape(-1, LANES),
    )
    features, pieces = lax.optimization_barrier((features, pieces))
    pieces = lax.all_to_all(pieces, "yh", 0, 0, tiled=True)
    sources = [
        lax.ppermute(features, "x", [(i, (i - shift) % X) for i in range(X)]) if shift else features
        for shift in SHIFTS
    ]

    columns = HEAD_SIZE + FRESH_ROWS + 3 * RANK
    weights, smalls = call(
        functools.partial(plan_kernel, groups),
        [shape(columns, width), shape(5, SLOTS, LANES)],
        [SMEM, SMEM] + [VMEM] * 6,
        moved=5 * 1024 * 1024,
    )(
        place,
        document_page_slots,
        query_weight,
        key_value_weight.T,
        shared_down_factors.T,
        query_up,
        key_value_up,
        document_of_row.reshape(1, rows),
    )
    message, fresh, queries_t = call(
        functools.partial(project_kernel, groups),
        [
            shape(groups, 2 * capacity, HEAD_SIZE),
            shape(FRESH_ROWS, rows),
            shape(HEAD_SIZE, rows),
        ],
        [SMEM] + [VMEM] * (X + 4),
        [pltpu.VMEM((width, rows), BF16), pltpu.VMEM((HEAD_SIZE, rows), F32)],
        flops=2 * width * rows * 256,
        moved=4 * 1024 * 1024,
    )(
        place,
        *sources,
        weights,
        input_norm_gain.reshape(Y, X, part).transpose(1, 0, 2),
        smalls,
        adapter_of_row.reshape(1, rows),
    )
    fresh = lax.ppermute(
        fresh,
        ("yh", "yl"),
        [(y, 2 * y if y < Y_HIGH else 2 * (y - Y_HIGH) + 1) for y in range(Y)],
    )
    message, pieces = lax.optimization_barrier((message, pieces))
    received = lax.all_to_all(message, "grp", 0, 0, tiled=True)

    message, slot_adapters = call(
        functools.partial(turn_kernel, groups),
        [shape(BLOCK, MESSAGE_ROWS, LANES), shape(8, SLOTS, dtype=F32)],
        [VMEM],
        moved=1024 * 1024,
    )(received)
    gathered = lax.all_to_all(message, ("yl", "x"), 0, 0, tiled=True)

    tokens = PIECE_TOKENS * Y_HIGH
    prepared = call(
        prepare_kernel,
        shape(tokens + tokens // DEPTH * VALUE_ROWS, DEPTH),
        [VMEM],
        moved=3 * 1024 * 1024,
    )(pieces)
    message = call(
        attend_kernel,
        shape(BLOCK, RETURN_ROWS + FRESH_ROWS, LANES),
        [VMEM] * 5,
        [
            pltpu.VMEM((2, DEPTH, SLOTS), BF16),
            pltpu.VMEM((2, tokens, SLOTS), F32),
            pltpu.VMEM((BLOCK, VALUE_ROWS, SLOTS), F32),
            pltpu.VMEM((BLOCK, 8, SLOTS), F32),
        ],
        flops=4 * SLOTS * BLOCK * tokens * 256,
        moved=3 * 1024 * 1024,
        limit=24,
    )(gathered, slot_adapters, smalls, prepared, fresh)
    partials = lax.all_to_all(message, ("yl", "x"), 0, 0, tiled=True)

    message = call(
        functools.partial(merge_kernel, groups),
        shape(groups, 2 * capacity, HEAD_SIZE),
        [VMEM],
        flops=SLOTS * HEAD_SIZE * 16,
        moved=1024 * 1024,
    )(partials)
    received = lax.all_to_all(message, "grp", 0, 0, tiled=True)

    return call(
        functools.partial(finish_kernel, groups),
        shape(rows, HEAD_SIZE),
        [VMEM] * 4,
        flops=2 * SLOTS * rows * 256,
        moved=1024 * 1024,
    )(received, smalls, queries_t, partials)


def solution(mesh):
    groups = mesh.devices.shape[0]
    split = Mesh(
        mesh.devices.reshape(groups, Y_HIGH, Y_LOW, X), ("grp", "yh", "yl", "x")
    )
    tp = ("yh", "yl", "x")
    in_specs = (
        P("grp", tp),
        P(),
        P(None, tp),
        P(None, tp),
        P(),
        P(None, None, tp),
        P(),
        P(("grp",) + tp, None, None),
        P(("grp",) + tp, None, None),
        P(("grp",) + tp, None, None),
        P("grp"),
        P("grp", None),
        P(),
    )
    return jax.shard_map(
        per_device, mesh=split, in_specs=in_specs, out_specs=P("grp", tp), check_vma=False
    )
```

```python
import functools
import math

import jax
import jax.numpy as jnp
from jax import lax
from jax.experimental import pallas as pl
from jax.experimental.pallas import tpu as pltpu
from jax.sharding import Mesh, PartitionSpec as P

HEAD_SIZE = 128
RANK = 16
LANES = 128
Y_HIGH, Y_LOW, X = 4, 2, 4
Y = Y_HIGH * Y_LOW
BLOCK = Y_LOW * X
SLOTS = 256
TILES = SLOTS // LANES
QUERY_ROWS = HEAD_SIZE + RANK
MESSAGE_ROWS = TILES * QUERY_ROWS
RETURN_ROWS = TILES * HEAD_SIZE + 16
FRESH_ROWS = 32
DEPTH = 2 * HEAD_SIZE
VALUE_ROWS = QUERY_ROWS + 16
OWN_UP, KEY_UP, VALUE_UP, QUERY_UP, PLACING = range(5)
PIECE_TOKENS = 512
PIECE_ROWS = 2 * PIECE_TOKENS + 2 * RANK * PIECE_TOKENS // LANES
SHIFTS = (0, 1, 3, 2)
SCORE_SCALE = HEAD_SIZE**-0.5
F32 = jnp.float32
BF16 = jnp.bfloat16
VMEM = pl.BlockSpec(memory_space=pltpu.VMEM)
SMEM = pl.BlockSpec(memory_space=pltpu.SMEM)
ANY = pl.BlockSpec(memory_space=pl.ANY)


def dot(left, right, left_dim, right_dim):
    return lax.dot_general(
        left, right, (((left_dim,), (right_dim,)), ((), ())), preferred_element_type=F32
    )


def call(kernel, out_shape, in_specs, scratch=(), flops=0, moved=0, limit=16, out_specs=None):
    return pl.pallas_call(
        kernel,
        out_shape=out_shape,
        in_specs=in_specs,
        out_specs=out_specs or jax.tree.map(lambda _: VMEM, out_shape),
        scratch_shapes=list(scratch),
        compiler_params=pltpu.CompilerParams(vmem_limit_bytes=limit * 1024 * 1024),
        cost_estimate=pl.CostEstimate(flops=flops, bytes_accessed=moved, transcendentals=0),
    )


def shape(*dims, dtype=BF16):
    return jax.ShapeDtypeStruct(dims, dtype)


def of_adapter(low, adapters):
    repeated = jnp.concatenate([low] * 16, axis=0)
    adapter = lax.broadcasted_iota(jnp.int32, repeated.shape, 0) // RANK
    return jnp.where(adapter == adapters, repeated, jnp.zeros_like(repeated))


def split_float(value):
    high = value.astype(BF16).astype(F32)
    middle = (value - high).astype(BF16).astype(F32)
    return high, middle, value - high - middle


def fetch(pairs, sems):
    moves = [pltpu.make_async_copy(*pair, sems.at[i]) for i, pair in enumerate(pairs)]
    for move in moves:
        move.start()
    for move in moves:
        move.wait()


def pack_kernel(place, keys_far, values_far, factors_far, *refs):
    pieces, (keys, values, factors, sems) = refs[:Y_HIGH], refs[Y_HIGH:]
    fetch([(keys_far, keys), (values_far, values), (factors_far, factors)], sems)
    for shift, piece in zip(SHIFTS, pieces):
        head = lax.rem(place[1] + shift, Y_HIGH)
        columns = pl.ds(pl.multiple_of(head * HEAD_SIZE, HEAD_SIZE), HEAD_SIZE)
        piece[0:PIECE_TOKENS, :] = keys[:, columns]
        piece[PIECE_TOKENS : 2 * PIECE_TOKENS, :] = values[:, columns]
        piece[2 * PIECE_TOKENS :, :] = factors[...]


def plan_kernel(
    groups,
    place,
    page_slots,
    query_weight_far,
    key_value_weight,
    down,
    query_up,
    key_value_up,
    documents,
    weights,
    smalls,
    query_weight,
    sems,
):
    pairs = [
        (query_weight_far, query_weight),
        (key_value_weight, weights.at[pl.ds(HEAD_SIZE, FRESH_ROWS), :]),
        (down, weights.at[pl.ds(HEAD_SIZE + FRESH_ROWS, 3 * RANK), :]),
        (query_up, smalls.at[QUERY_UP]),
    ]
    for index, head in enumerate((place[0] // X, place[1], place[1] + Y_HIGH)):
        columns = pl.ds(pl.multiple_of(head * HEAD_SIZE, HEAD_SIZE), HEAD_SIZE)
        pairs.append((key_value_up.at[:, columns], smalls.at[index]))
    fetch(pairs, sems)
    for start in range(0, weights.shape[1], LANES):
        block = query_weight[start : start + LANES, :].astype(F32).T
        weights[0:HEAD_SIZE, start : start + LANES] = block.astype(BF16)

    document = documents[...]
    rows = document.shape[1]
    target = jnp.zeros_like(document)
    for d in range(page_slots.shape[0]):
        target = jnp.where(document == d, page_slots[d, 0] // page_slots.shape[1], target)
    capacity = SLOTS // groups
    group = lax.broadcasted_iota(jnp.int32, (16, rows), 0)
    match = (group == target).astype(F32)
    before = (
        lax.broadcasted_iota(jnp.int32, (rows, rows), 0)
        < lax.broadcasted_iota(jnp.int32, (rows, rows), 1)
    ).astype(F32)
    earlier = dot(match.astype(BF16), before.astype(BF16), 1, 0)
    position = jnp.sum(earlier * match, axis=0, keepdims=True).astype(jnp.int32)
    slot = target * capacity + position
    placed = (lax.broadcasted_iota(jnp.int32, (SLOTS, rows), 0) == slot).astype(F32)
    smalls[PLACING] = placed.astype(BF16)


def project_kernel(
    groups,
    place,
    sources,
    weights,
    gain,
    smalls,
    adapters,
    message,
    fresh,
    queries_t,
    normed,
    update,
):
    device = place[0]
    part = gain.shape[2]
    width = normed.shape[0]
    squares = jnp.zeros((part, normed.shape[1]), F32)
    for x in range(X):
        for y in range(Y):
            block = sources[x, y].astype(F32)
            squares = squares + block * block
    scale = lax.rsqrt(jnp.sum(squares, axis=0, keepdims=True) / width + 1e-06)
    for x in range(X):
        gain_t = gain[x].T
        for y in range(Y):
            block = sources[x, y].astype(F32) * scale * gain_t[:, y : y + 1]
            start = (y * X + x) * part
            normed[pl.ds(start, part), :] = block.astype(BF16)
    total = dot(weights[...], normed[...], 1, 0)

    adapter = adapters[...]
    low = total[HEAD_SIZE + FRESH_ROWS :].astype(BF16)
    query_update = dot(smalls[QUERY_UP], of_adapter(low[0:RANK], adapter), 0, 0)
    queries = (total[0:HEAD_SIZE] + query_update).astype(BF16)
    queries_t[...] = queries

    is_key = device < Y * X // 2
    low_kv = jnp.where(is_key, low[RANK : 2 * RANK], low[2 * RANK :])
    update[...] = dot(smalls[OWN_UP], of_adapter(low_kv, adapter), 0, 0)
    mine = pl.ds(pl.multiple_of(lax.rem(device, X) * FRESH_ROWS, FRESH_ROWS), FRESH_ROWS)
    new = total[HEAD_SIZE : HEAD_SIZE + FRESH_ROWS] + update[mine, :]
    fresh[...] = new.astype(BF16)

    every = dot(smalls[KEY_UP], queries, 1, 0)
    of_row = lax.broadcasted_iota(jnp.int32, every.shape, 0) // RANK == adapter
    kept = jnp.where(of_row, every, 0.0)
    factors = kept[0:RANK]
    for a in range(1, 16):
        factors = factors + kept[a * RANK : (a + 1) * RANK]
    rest = jnp.zeros((HEAD_SIZE - RANK - 1, factors.shape[1]), F32)
    beside = jnp.concatenate([factors, adapter.astype(F32), rest], axis=0).astype(BF16)

    capacity = SLOTS // groups
    place_rows = smalls[PLACING]
    placed = dot(place_rows, queries, 1, 1).astype(BF16)
    message[:, 0:capacity, :] = placed.reshape(groups, capacity, HEAD_SIZE)
    placed = dot(place_rows, beside, 1, 1).astype(BF16)
    message[:, capacity:, :] = placed.reshape(groups, capacity, LANES)


def turn_kernel(groups, received, message, slot_adapters):
    capacity = SLOTS // groups
    queries = received[:, 0:capacity, :].reshape(SLOTS, HEAD_SIZE).astype(F32).T.astype(BF16)
    beside = received[:, capacity:, :].reshape(SLOTS, LANES).astype(F32).T
    slot_adapters[...] = jnp.broadcast_to(beside[RANK : RANK + 1], slot_adapters.shape)
    factors = beside[0:RANK].astype(BF16)
    for member in range(BLOCK):
        for tile in range(TILES):
            lanes = slice(tile * LANES, (tile + 1) * LANES)
            start = tile * QUERY_ROWS
            message[member, start : start + HEAD_SIZE, :] = queries[:, lanes]
            message[member, start + HEAD_SIZE : start + QUERY_ROWS, :] = factors[:, lanes]


def prepare_kernel(piece_0, piece_1, piece_2, piece_3, prepared):
    tokens = PIECE_TOKENS * Y_HIGH
    ones = lax.broadcasted_iota(jnp.int32, (VALUE_ROWS - QUERY_ROWS, DEPTH), 0) == 0
    for index, piece in enumerate((piece_0, piece_1, piece_2, piece_3)):
        for page in range(PIECE_TOKENS // LANES):
            start = page * LANES
            token = index * PIECE_TOKENS + start
            here = slice(token, token + LANES)
            row = 2 * PIECE_TOKENS + page * 2 * RANK
            factors = piece[row : row + 2 * RANK, :]
            key_factors = jnp.concatenate(
                [factors[0:RANK].astype(F32), jnp.zeros((LANES - RANK, LANES), F32)], axis=0
            )
            prepared[here, 0:HEAD_SIZE] = piece[start : start + LANES, :]
            prepared[here, HEAD_SIZE:] = key_factors.T.astype(BF16)
            value = piece[PIECE_TOKENS + start : PIECE_TOKENS + start + LANES, :]
            base = tokens + token // DEPTH * VALUE_ROWS
            lanes = slice(token % DEPTH, token % DEPTH + LANES)
            prepared[base : base + HEAD_SIZE, lanes] = value.astype(F32).T.astype(BF16)
            prepared[base + HEAD_SIZE : base + QUERY_ROWS, lanes] = factors[RANK:]
            if token % DEPTH == 0:
                prepared[base + QUERY_ROWS : base + VALUE_ROWS, :] = ones.astype(F32).astype(BF16)


def attend_kernel(
    queries, slot_adapters, smalls, prepared, fresh, message, query, scores, totals, peaks
):
    tokens = PIECE_TOKENS * Y_HIGH
    chunk = 1024
    exponent = SCORE_SCALE * math.log2(math.e)
    query[:, QUERY_ROWS:, :] = jnp.zeros((2, DEPTH - QUERY_ROWS, SLOTS), BF16)

    def load(head, side):
        for tile in range(TILES):
            query[side, 0:QUERY_ROWS, tile * LANES : (tile + 1) * LANES] = queries[
                head, tile * QUERY_ROWS : (tile + 1) * QUERY_ROWS, :
            ]

    def score(side, start, highest):
        block = dot(prepared[start : start + chunk, :], query[side], 1, 0)
        scores[side, start : start + chunk, :] = block
        return jnp.maximum(highest, jnp.max(block.reshape(chunk // 8, 8, SLOTS), axis=0))

    def add(side, start, peak, total):
        weight = jnp.exp2(scores[side, start : start + chunk, :] * exponent - peak).astype(BF16)
        for step in range(chunk // DEPTH):
            base = tokens + (start // DEPTH + step) * VALUE_ROWS
            values = prepared[base : base + VALUE_ROWS, :]
            total = total + dot(values, weight[step * DEPTH : (step + 1) * DEPTH], 1, 0)
        return total

    lowest = jnp.full((8, SLOTS), -jnp.inf, F32)

    def one_head(head, following, side, peak):
        load(following, 1 - side)
        highest, total = lowest, jnp.zeros((VALUE_ROWS, SLOTS), F32)
        for start in range(0, tokens, chunk):
            highest = score(1 - side, start, highest)
            total = add(side, start, peak * exponent, total)
        totals[head] = total
        peaks[head] = jnp.broadcast_to(peak, (8, SLOTS))
        return jnp.max(highest, axis=0, keepdims=True)

    def two_heads(pair, peak):
        peak = one_head(2 * pair, 2 * pair + 1, 0, peak)
        return one_head(2 * pair + 1, jnp.minimum(2 * pair + 2, BLOCK - 1), 1, peak)

    load(0, 0)
    highest = lowest
    for start in range(0, tokens, chunk):
        highest = score(0, start, highest)
    lax.fori_loop(0, BLOCK // 2, two_heads, jnp.max(highest, axis=0, keepdims=True))

    value_up = smalls[VALUE_UP]
    adapters = slot_adapters[0:1, :].astype(jnp.int32)
    for head in range(BLOCK):
        total, peak = totals[head], peaks[head, 0:1]
        mass = total[QUERY_ROWS : QUERY_ROWS + 1]
        inverse = 1.0 / mass
        low = (total[HEAD_SIZE:QUERY_ROWS] * inverse).astype(BF16)
        shift = dot(value_up, of_adapter(low, adapters), 0, 0)
        result = (total[0:HEAD_SIZE] * inverse + shift).astype(BF16)
        parts = split_float(peak * SCORE_SCALE + jnp.log(mass))
        stats = [part[:, tile * LANES : (tile + 1) * LANES] for tile in range(TILES) for part in parts]
        stats = jnp.concatenate(stats + [jnp.zeros((16 - len(stats), LANES), F32)], axis=0)
        for tile in range(TILES):
            message[head, tile * HEAD_SIZE : (tile + 1) * HEAD_SIZE, :] = result[
                :, tile * LANES : (tile + 1) * LANES
            ]
        message[head, TILES * HEAD_SIZE : RETURN_ROWS, :] = stats.astype(BF16)
        message[head, RETURN_ROWS:, :] = fresh[...]


def merge_kernel(groups, partials, message):
    capacity = SLOTS // groups
    stats = [partials[member, TILES * HEAD_SIZE : RETURN_ROWS, :].astype(F32) for member in range(BLOCK)]
    results, masses = [], []
    for tile in range(TILES):
        first = 3 * tile
        logs = [s[first : first + 1] + s[first + 1 : first + 2] + s[first + 2 : first + 3] for s in stats]
        peak = functools.reduce(jnp.maximum, logs)
        weights = [jnp.exp(one - peak) for one in logs]
        whole = functools.reduce(jnp.add, weights)
        rows = slice(tile * HEAD_SIZE, (tile + 1) * HEAD_SIZE)
        total = jnp.zeros((HEAD_SIZE, LANES), F32)
        for member in range(BLOCK):
            total = total + partials[member, rows, :].astype(F32) * weights[member]
        results.append((total / whole).T.astype(BF16))
        parts = list(split_float(peak + jnp.log(whole)))
        parts = jnp.concatenate(parts + [jnp.zeros((LANES - 3, LANES), F32)], axis=0)
        masses.append(parts.T.astype(BF16))
    message[:, 0:capacity, :] = jnp.concatenate(results, axis=0).reshape(groups, capacity, HEAD_SIZE)
    message[:, capacity:, :] = jnp.concatenate(masses, axis=0).reshape(groups, capacity, LANES)


def finish_kernel(groups, received, smalls, queries_t, partials, out):
    capacity = SLOTS // groups
    place = smalls[PLACING]
    shared = dot(received[:, 0:capacity, :].reshape(SLOTS, HEAD_SIZE), place, 0, 0)
    stats = dot(received[:, capacity:, :].reshape(SLOTS, LANES), place, 0, 0)
    log_mass = stats[0:1] + stats[1:2] + stats[2:3]
    new = partials[:, RETURN_ROWS:, :]
    key = new[0:X].reshape(HEAD_SIZE, LANES).astype(F32)
    value = new[X:].reshape(HEAD_SIZE, LANES).astype(F32)
    own = jnp.sum(queries_t[...].astype(F32) * key, axis=0, keepdims=True) * SCORE_SCALE
    peak = jnp.maximum(log_mass, own)
    shared_weight = jnp.exp(log_mass - peak)
    own_weight = jnp.exp(own - peak)
    result = (shared * shared_weight + value * own_weight) / (shared_weight + own_weight)
    out[...] = result.T.astype(BF16)


def per_device(
    residual_input,
    input_norm_gain,
    query_weight,
    key_value_weight,
    shared_down_factors,
    query_up_factors,
    key_value_up_factors,
    paged_base_keys,
    paged_base_values,
    paged_down_factors,
    adapter_of_row,
    document_of_row,
    document_page_slots,
):
    groups = lax.axis_size("grp")
    capacity = SLOTS // groups
    rows, part = residual_input.shape
    width = part * Y * X
    y_high = lax.axis_index("yh")
    device = (y_high * Y_LOW + lax.axis_index("yl")) * X + lax.axis_index("x")
    place = jnp.stack([device, y_high]).astype(jnp.int32)
    query_up = query_up_factors.reshape(-1, HEAD_SIZE)
    key_value_up = key_value_up_factors.reshape(-1, key_value_up_factors.shape[2])

    features = jnp.broadcast_to(residual_input.T[None], (Y, part, rows))
    features = lax.all_to_all(features, ("yh", "yl"), 0, 0, tiled=True)
    pieces = call(
        pack_kernel,
        [shape(PIECE_ROWS, HEAD_SIZE)] * Y_HIGH,
        [SMEM] + [ANY] * 3,
        [
            pltpu.VMEM((PIECE_TOKENS, Y_HIGH * HEAD_SIZE), BF16),
            pltpu.VMEM((PIECE_TOKENS, Y_HIGH * HEAD_SIZE), BF16),
            pltpu.VMEM((PIECE_ROWS - 2 * PIECE_TOKENS, LANES), BF16),
            pltpu.SemaphoreType.DMA((3,)),
        ],
        moved=3 * 1024 * 1024,
        limit=60,
    )(
        place,
        paged_base_keys.reshape(PIECE_TOKENS, -1),
        paged_base_values.reshape(PIECE_TOKENS, -1),
        paged_down_factors.transpose(0, 2, 1).reshape(-1, LANES),
    )
    columns = HEAD_SIZE + FRESH_ROWS + 3 * RANK
    weights, smalls = call(
        functools.partial(plan_kernel, groups),
        [shape(columns, width), shape(5, SLOTS, LANES)],
        [SMEM, SMEM] + [ANY] * 5 + [VMEM],
        [pltpu.VMEM((width, HEAD_SIZE), BF16), pltpu.SemaphoreType.DMA((7,))],
        moved=5 * 1024 * 1024,
        limit=60,
    )(
        place,
        document_page_slots,
        query_weight,
        key_value_weight.T,
        shared_down_factors.T,
        query_up,
        key_value_up,
        document_of_row.reshape(1, rows),
    )
    features, pieces, weights, smalls = lax.optimization_barrier(
        (features, pieces, weights, smalls)
    )
    pieces = [
        lax.ppermute(piece, "yh", [(i, (i + shift) % Y_HIGH) for i in range(Y_HIGH)]) if shift else piece
        for shift, piece in zip(SHIFTS, pieces)
    ]
    features = jnp.broadcast_to(features.reshape(1, Y, part, rows), (X, Y, part, rows))
    features = lax.all_to_all(features, "x", 0, 0, tiled=True)

    message, fresh, queries_t = call(
        functools.partial(project_kernel, groups),
        [
            shape(groups, 2 * capacity, HEAD_SIZE),
            shape(FRESH_ROWS, rows),
            shape(HEAD_SIZE, rows),
        ],
        [SMEM] + [VMEM] * 5,
        [pltpu.VMEM((width, rows), BF16), pltpu.VMEM((HEAD_SIZE, rows), F32)],
        flops=2 * width * rows * 256,
        moved=4 * 1024 * 1024,
    )(
        place,
        features,
        weights,
        input_norm_gain.reshape(Y, X, part).transpose(1, 0, 2),
        smalls,
        adapter_of_row.reshape(1, rows),
    )
    fresh = lax.ppermute(
        fresh,
        ("yh", "yl"),
        [(y, 2 * y if y < Y_HIGH else 2 * (y - Y_HIGH) + 1) for y in range(Y)],
    )
    received = lax.all_to_all(message, "grp", 0, 0, tiled=True)

    message, slot_adapters = call(
        functools.partial(turn_kernel, groups),
        [shape(BLOCK, MESSAGE_ROWS, LANES), shape(8, SLOTS, dtype=F32)],
        [VMEM],
        moved=1024 * 1024,
    )(received)
    message, pieces = lax.optimization_barrier((message, pieces))
    gathered = lax.all_to_all(message, ("yl", "x"), 0, 0, tiled=True)

    tokens = PIECE_TOKENS * Y_HIGH
    prepared = call(
        prepare_kernel,
        shape(tokens + tokens // DEPTH * VALUE_ROWS, DEPTH),
        [VMEM] * 4,
        moved=3 * 1024 * 1024,
    )(*pieces)
    message = call(
        attend_kernel,
        shape(BLOCK, RETURN_ROWS + FRESH_ROWS, LANES),
        [VMEM] * 5,
        [
            pltpu.VMEM((2, DEPTH, SLOTS), BF16),
            pltpu.VMEM((2, tokens, SLOTS), F32),
            pltpu.VMEM((BLOCK, VALUE_ROWS, SLOTS), F32),
            pltpu.VMEM((BLOCK, 8, SLOTS), F32),
        ],
        flops=4 * SLOTS * BLOCK * tokens * 256,
        moved=3 * 1024 * 1024,
        limit=24,
    )(gathered, slot_adapters, smalls, prepared, fresh)
    partials = lax.all_to_all(message, ("yl", "x"), 0, 0, tiled=True)

    message = call(
        functools.partial(merge_kernel, groups),
        shape(groups, 2 * capacity, HEAD_SIZE),
        [VMEM],
        flops=SLOTS * HEAD_SIZE * 16,
        moved=1024 * 1024,
    )(partials)
    received = lax.all_to_all(message, "grp", 0, 0, tiled=True)

    return call(
        functools.partial(finish_kernel, groups),
        shape(rows, HEAD_SIZE),
        [VMEM] * 4,
        flops=2 * SLOTS * rows * 256,
        moved=1024 * 1024,
    )(received, smalls, queries_t, partials)


def solution(mesh):
    groups = mesh.devices.shape[0]
    split = Mesh(
        mesh.devices.reshape(groups, Y_HIGH, Y_LOW, X), ("grp", "yh", "yl", "x")
    )
    tp = ("yh", "yl", "x")
    in_specs = (
        P("grp", tp),
        P(),
        P(None, tp),
        P(None, tp),
        P(),
        P(None, None, tp),
        P(),
        P(("grp",) + tp, None, None),
        P(("grp",) + tp, None, None),
        P(("grp",) + tp, None, None),
        P("grp"),
        P("grp", None),
        P(),
    )
    return jax.shard_map(
        per_device, mesh=split, in_specs=in_specs, out_specs=P("grp", tp), check_vma=False
    )
```

```python
import functools
import math

import jax
import jax.numpy as jnp
from jax import lax
from jax.experimental import pallas as pl
from jax.experimental.pallas import tpu as pltpu
from jax.sharding import Mesh, PartitionSpec as P

HEAD_SIZE = 128
RANK = 16
LANES = 128
Y_HIGH, Y_LOW, X = 4, 2, 4
Y = Y_HIGH * Y_LOW
BLOCK = Y_LOW * X
SLOTS = 256
TILES = SLOTS // LANES
QUERY_ROWS = HEAD_SIZE + RANK
MESSAGE_ROWS = TILES * QUERY_ROWS
RETURN_ROWS = TILES * HEAD_SIZE + 16
FRESH_ROWS = 32
DEPTH = 2 * HEAD_SIZE
VALUE_ROWS = QUERY_ROWS + 16
OWN_UP, KEY_UP, VALUE_UP, QUERY_UP, PLACING = range(5)
PIECE_TOKENS = 512
PIECE_ROWS = 2 * PIECE_TOKENS + 2 * RANK * PIECE_TOKENS // LANES
SHIFTS = (0, 1, 3, 2)
SCORE_SCALE = HEAD_SIZE**-0.5
F32 = jnp.float32
BF16 = jnp.bfloat16
VMEM = pl.BlockSpec(memory_space=pltpu.VMEM)
SMEM = pl.BlockSpec(memory_space=pltpu.SMEM)
ANY = pl.BlockSpec(memory_space=pl.ANY)


def dot(left, right, left_dim, right_dim):
    return lax.dot_general(
        left, right, (((left_dim,), (right_dim,)), ((), ())), preferred_element_type=F32
    )


def call(kernel, out_shape, in_specs, scratch=(), flops=0, moved=0, limit=16, out_specs=None):
    return pl.pallas_call(
        kernel,
        out_shape=out_shape,
        in_specs=in_specs,
        out_specs=out_specs or jax.tree.map(lambda _: VMEM, out_shape),
        scratch_shapes=list(scratch),
        compiler_params=pltpu.CompilerParams(vmem_limit_bytes=limit * 1024 * 1024),
        cost_estimate=pl.CostEstimate(flops=flops, bytes_accessed=moved, transcendentals=0),
    )


def shape(*dims, dtype=BF16):
    return jax.ShapeDtypeStruct(dims, dtype)


def of_adapter(low, adapters):
    repeated = jnp.concatenate([low] * 16, axis=0)
    adapter = lax.broadcasted_iota(jnp.int32, repeated.shape, 0) // RANK
    return jnp.where(adapter == adapters, repeated, jnp.zeros_like(repeated))


def split_float(value):
    high = value.astype(BF16).astype(F32)
    middle = (value - high).astype(BF16).astype(F32)
    return high, middle, value - high - middle


def fetch(pairs, sems):
    moves = [pltpu.make_async_copy(*pair, sems.at[i]) for i, pair in enumerate(pairs)]
    for move in moves:
        move.start()
    for move in moves:
        move.wait()


def pack_kernel(place, keys_far, values_far, factors_far, *refs):
    pieces, (keys, values, factors, sems) = refs[:Y_HIGH], refs[Y_HIGH:]
    fetch([(keys_far, keys), (values_far, values), (factors_far, factors)], sems)
    for shift, piece in zip(SHIFTS, pieces):
        head = lax.rem(place[1] + shift, Y_HIGH)
        columns = pl.ds(pl.multiple_of(head * HEAD_SIZE, HEAD_SIZE), HEAD_SIZE)
        piece[0:PIECE_TOKENS, :] = keys[:, columns]
        piece[PIECE_TOKENS : 2 * PIECE_TOKENS, :] = values[:, columns]
        piece[2 * PIECE_TOKENS :, :] = factors[...]


def plan_kernel(
    groups,
    place,
    page_slots,
    query_weight_far,
    key_value_weight,
    down,
    query_up,
    key_value_up,
    documents,
    weights,
    smalls,
    query_weight,
    sems,
):
    pairs = [
        (query_weight_far, query_weight),
        (key_value_weight, weights.at[pl.ds(HEAD_SIZE, FRESH_ROWS), :]),
        (down, weights.at[pl.ds(HEAD_SIZE + FRESH_ROWS, 3 * RANK), :]),
        (query_up, smalls.at[QUERY_UP]),
    ]
    for index, head in enumerate((place[0] // X, place[1], place[1] + Y_HIGH)):
        columns = pl.ds(pl.multiple_of(head * HEAD_SIZE, HEAD_SIZE), HEAD_SIZE)
        pairs.append((key_value_up.at[:, columns], smalls.at[index]))
    fetch(pairs, sems)
    for start in range(0, weights.shape[1], LANES):
        block = query_weight[start : start + LANES, :].astype(F32).T
        weights[0:HEAD_SIZE, start : start + LANES] = block.astype(BF16)

    document = documents[...]
    rows = document.shape[1]
    target = jnp.zeros_like(document)
    for d in range(page_slots.shape[0]):
        target = jnp.where(document == d, page_slots[d, 0] // page_slots.shape[1], target)
    capacity = SLOTS // groups
    target = target % 2 * (groups // 2) + target // 2
    group = lax.broadcasted_iota(jnp.int32, (16, rows), 0)
    match = (group == target).astype(F32)
    before = (
        lax.broadcasted_iota(jnp.int32, (rows, rows), 0)
        < lax.broadcasted_iota(jnp.int32, (rows, rows), 1)
    ).astype(F32)
    earlier = dot(match.astype(BF16), before.astype(BF16), 1, 0)
    position = jnp.sum(earlier * match, axis=0, keepdims=True).astype(jnp.int32)
    slot = target * capacity + position
    placed = (lax.broadcasted_iota(jnp.int32, (SLOTS, rows), 0) == slot).astype(F32)
    smalls[PLACING] = placed.astype(BF16)


def project_kernel(
    groups,
    place,
    sources,
    weights,
    gain,
    smalls,
    adapters,
    message,
    fresh,
    queries_t,
    normed,
    update,
):
    device = place[0]
    part = gain.shape[2]
    width = normed.shape[0]
    squares = jnp.zeros((part, normed.shape[1]), F32)
    for x in range(X):
        for y in range(Y):
            block = sources[x, y].astype(F32)
            squares = squares + block * block
    scale = lax.rsqrt(jnp.sum(squares, axis=0, keepdims=True) / width + 1e-06)
    for x in range(X):
        gain_t = gain[x].T
        for y in range(Y):
            block = sources[x, y].astype(F32) * scale * gain_t[:, y : y + 1]
            start = (y * X + x) * part
            normed[pl.ds(start, part), :] = block.astype(BF16)
    total = dot(weights[...], normed[...], 1, 0)

    adapter = adapters[...]
    low = total[HEAD_SIZE + FRESH_ROWS :].astype(BF16)
    query_update = dot(smalls[QUERY_UP], of_adapter(low[0:RANK], adapter), 0, 0)
    queries = (total[0:HEAD_SIZE] + query_update).astype(BF16)
    queries_t[...] = queries

    is_key = device < Y * X // 2
    low_kv = jnp.where(is_key, low[RANK : 2 * RANK], low[2 * RANK :])
    update[...] = dot(smalls[OWN_UP], of_adapter(low_kv, adapter), 0, 0)
    mine = pl.ds(pl.multiple_of(lax.rem(device, X) * FRESH_ROWS, FRESH_ROWS), FRESH_ROWS)
    new = total[HEAD_SIZE : HEAD_SIZE + FRESH_ROWS] + update[mine, :]
    fresh[...] = new.astype(BF16)

    every = dot(smalls[KEY_UP], queries, 1, 0)
    of_row = lax.broadcasted_iota(jnp.int32, every.shape, 0) // RANK == adapter
    kept = jnp.where(of_row, every, 0.0)
    factors = kept[0:RANK]
    for a in range(1, 16):
        factors = factors + kept[a * RANK : (a + 1) * RANK]
    rest = jnp.zeros((HEAD_SIZE - RANK - 1, factors.shape[1]), F32)
    beside = jnp.concatenate([factors, adapter.astype(F32), rest], axis=0).astype(BF16)

    capacity = SLOTS // groups
    place_rows = smalls[PLACING]
    placed = dot(place_rows, queries, 1, 1).astype(BF16)
    message[:, 0:capacity, :] = placed.reshape(groups, capacity, HEAD_SIZE)
    placed = dot(place_rows, beside, 1, 1).astype(BF16)
    message[:, capacity:, :] = placed.reshape(groups, capacity, LANES)


def turn_kernel(groups, received, message, slot_adapters):
    capacity = SLOTS // groups
    queries = received[:, 0:capacity, :].reshape(SLOTS, HEAD_SIZE).astype(F32).T.astype(BF16)
    beside = received[:, capacity:, :].reshape(SLOTS, LANES).astype(F32).T
    slot_adapters[...] = jnp.broadcast_to(beside[RANK : RANK + 1], slot_adapters.shape)
    factors = beside[0:RANK].astype(BF16)
    for member in range(BLOCK):
        for tile in range(TILES):
            lanes = slice(tile * LANES, (tile + 1) * LANES)
            start = tile * QUERY_ROWS
            message[member, start : start + HEAD_SIZE, :] = queries[:, lanes]
            message[member, start + HEAD_SIZE : start + QUERY_ROWS, :] = factors[:, lanes]


def prepare_kernel(piece_0, piece_1, piece_2, piece_3, prepared):
    tokens = PIECE_TOKENS * Y_HIGH
    ones = lax.broadcasted_iota(jnp.int32, (VALUE_ROWS - QUERY_ROWS, DEPTH), 0) == 0
    for index, piece in enumerate((piece_0, piece_1, piece_2, piece_3)):
        for page in range(PIECE_TOKENS // LANES):
            start = page * LANES
            token = index * PIECE_TOKENS + start
            here = slice(token, token + LANES)
            row = 2 * PIECE_TOKENS + page * 2 * RANK
            factors = piece[row : row + 2 * RANK, :]
            key_factors = jnp.concatenate(
                [factors[0:RANK].astype(F32), jnp.zeros((LANES - RANK, LANES), F32)], axis=0
            )
            prepared[here, 0:HEAD_SIZE] = piece[start : start + LANES, :]
            prepared[here, HEAD_SIZE:] = key_factors.T.astype(BF16)
            value = piece[PIECE_TOKENS + start : PIECE_TOKENS + start + LANES, :]
            base = tokens + token // DEPTH * VALUE_ROWS
            lanes = slice(token % DEPTH, token % DEPTH + LANES)
            prepared[base : base + HEAD_SIZE, lanes] = value.astype(F32).T.astype(BF16)
            prepared[base + HEAD_SIZE : base + QUERY_ROWS, lanes] = factors[RANK:]
            if token % DEPTH == 0:
                prepared[base + QUERY_ROWS : base + VALUE_ROWS, :] = ones.astype(F32).astype(BF16)


def attend_kernel(
    queries, slot_adapters, smalls, prepared, fresh, message, query, scores, totals, peaks
):
    tokens = PIECE_TOKENS * Y_HIGH
    chunk = 1024
    exponent = SCORE_SCALE * math.log2(math.e)
    query[:, QUERY_ROWS:, :] = jnp.zeros((2, DEPTH - QUERY_ROWS, SLOTS), BF16)

    def load(head, side):
        for tile in range(TILES):
            query[side, 0:QUERY_ROWS, tile * LANES : (tile + 1) * LANES] = queries[
                head, tile * QUERY_ROWS : (tile + 1) * QUERY_ROWS, :
            ]

    def score(side, start, highest):
        block = dot(prepared[start : start + chunk, :], query[side], 1, 0)
        scores[side, start : start + chunk, :] = block
        return jnp.maximum(highest, jnp.max(block.reshape(chunk // 8, 8, SLOTS), axis=0))

    def add(side, start, peak, total):
        weight = jnp.exp2(scores[side, start : start + chunk, :] * exponent - peak).astype(BF16)
        for step in range(chunk // DEPTH):
            base = tokens + (start // DEPTH + step) * VALUE_ROWS
            values = prepared[base : base + VALUE_ROWS, :]
            total = total + dot(values, weight[step * DEPTH : (step + 1) * DEPTH], 1, 0)
        return total

    lowest = jnp.full((8, SLOTS), -jnp.inf, F32)

    def one_head(head, following, side, peak):
        load(following, 1 - side)
        highest, total = lowest, jnp.zeros((VALUE_ROWS, SLOTS), F32)
        for start in range(0, tokens, chunk):
            highest = score(1 - side, start, highest)
            total = add(side, start, peak * exponent, total)
        totals[head] = total
        peaks[head] = jnp.broadcast_to(peak, (8, SLOTS))
        return jnp.max(highest, axis=0, keepdims=True)

    def two_heads(pair, peak):
        peak = one_head(2 * pair, 2 * pair + 1, 0, peak)
        return one_head(2 * pair + 1, jnp.minimum(2 * pair + 2, BLOCK - 1), 1, peak)

    load(0, 0)
    highest = lowest
    for start in range(0, tokens, chunk):
        highest = score(0, start, highest)
    lax.fori_loop(0, BLOCK // 2, two_heads, jnp.max(highest, axis=0, keepdims=True))

    value_up = smalls[VALUE_UP]
    adapters = slot_adapters[0:1, :].astype(jnp.int32)
    for head in range(BLOCK):
        total, peak = totals[head], peaks[head, 0:1]
        mass = total[QUERY_ROWS : QUERY_ROWS + 1]
        inverse = 1.0 / mass
        low = (total[HEAD_SIZE:QUERY_ROWS] * inverse).astype(BF16)
        shift = dot(value_up, of_adapter(low, adapters), 0, 0)
        result = (total[0:HEAD_SIZE] * inverse + shift).astype(BF16)
        parts = split_float(peak * SCORE_SCALE + jnp.log(mass))
        stats = [part[:, tile * LANES : (tile + 1) * LANES] for tile in range(TILES) for part in parts]
        stats = jnp.concatenate(stats + [jnp.zeros((16 - len(stats), LANES), F32)], axis=0)
        for tile in range(TILES):
            message[head, tile * HEAD_SIZE : (tile + 1) * HEAD_SIZE, :] = result[
                :, tile * LANES : (tile + 1) * LANES
            ]
        message[head, TILES * HEAD_SIZE : RETURN_ROWS, :] = stats.astype(BF16)
        message[head, RETURN_ROWS:, :] = fresh[...]


def merge_kernel(groups, partials, message):
    capacity = SLOTS // groups
    stats = [partials[member, TILES * HEAD_SIZE : RETURN_ROWS, :].astype(F32) for member in range(BLOCK)]
    results, masses = [], []
    for tile in range(TILES):
        first = 3 * tile
        logs = [s[first : first + 1] + s[first + 1 : first + 2] + s[first + 2 : first + 3] for s in stats]
        peak = functools.reduce(jnp.maximum, logs)
        weights = [jnp.exp(one - peak) for one in logs]
        whole = functools.reduce(jnp.add, weights)
        rows = slice(tile * HEAD_SIZE, (tile + 1) * HEAD_SIZE)
        total = jnp.zeros((HEAD_SIZE, LANES), F32)
        for member in range(BLOCK):
            total = total + partials[member, rows, :].astype(F32) * weights[member]
        results.append((total / whole).T.astype(BF16))
        parts = list(split_float(peak + jnp.log(whole)))
        parts = jnp.concatenate(parts + [jnp.zeros((LANES - 3, LANES), F32)], axis=0)
        masses.append(parts.T.astype(BF16))
    message[:, 0:capacity, :] = jnp.concatenate(results, axis=0).reshape(groups, capacity, HEAD_SIZE)
    message[:, capacity:, :] = jnp.concatenate(masses, axis=0).reshape(groups, capacity, LANES)


def finish_kernel(groups, received, smalls, queries_t, partials, out):
    capacity = SLOTS // groups
    place = smalls[PLACING]
    shared = dot(received[:, 0:capacity, :].reshape(SLOTS, HEAD_SIZE), place, 0, 0)
    stats = dot(received[:, capacity:, :].reshape(SLOTS, LANES), place, 0, 0)
    log_mass = stats[0:1] + stats[1:2] + stats[2:3]
    new = partials[:, RETURN_ROWS:, :]
    key = new[0:X].reshape(HEAD_SIZE, LANES).astype(F32)
    value = new[X:].reshape(HEAD_SIZE, LANES).astype(F32)
    own = jnp.sum(queries_t[...].astype(F32) * key, axis=0, keepdims=True) * SCORE_SCALE
    peak = jnp.maximum(log_mass, own)
    shared_weight = jnp.exp(log_mass - peak)
    own_weight = jnp.exp(own - peak)
    result = (shared * shared_weight + value * own_weight) / (shared_weight + own_weight)
    out[...] = result.T.astype(BF16)


def per_device(
    residual_input,
    input_norm_gain,
    query_weight,
    key_value_weight,
    shared_down_factors,
    query_up_factors,
    key_value_up_factors,
    paged_base_keys,
    paged_base_values,
    paged_down_factors,
    adapter_of_row,
    document_of_row,
    document_page_slots,
):
    groups = lax.axis_size("z") * lax.axis_size("core")
    capacity = SLOTS // groups
    rows, part = residual_input.shape
    width = part * Y * X
    y_high = lax.axis_index("yh")
    device = (y_high * Y_LOW + lax.axis_index("yl")) * X + lax.axis_index("x")
    place = jnp.stack([device, y_high]).astype(jnp.int32)
    query_up = query_up_factors.reshape(-1, HEAD_SIZE)
    key_value_up = key_value_up_factors.reshape(-1, key_value_up_factors.shape[2])

    features = jnp.broadcast_to(residual_input.T[None], (Y, part, rows))
    features = lax.all_to_all(features, ("yh", "yl"), 0, 0, tiled=True)
    pieces = call(
        pack_kernel,
        [shape(PIECE_ROWS, HEAD_SIZE)] * Y_HIGH,
        [SMEM] + [ANY] * 3,
        [
            pltpu.VMEM((PIECE_TOKENS, Y_HIGH * HEAD_SIZE), BF16),
            pltpu.VMEM((PIECE_TOKENS, Y_HIGH * HEAD_SIZE), BF16),
            pltpu.VMEM((PIECE_ROWS - 2 * PIECE_TOKENS, LANES), BF16),
            pltpu.SemaphoreType.DMA((3,)),
        ],
        moved=3 * 1024 * 1024,
        limit=60,
    )(
        place,
        paged_base_keys.reshape(PIECE_TOKENS, -1),
        paged_base_values.reshape(PIECE_TOKENS, -1),
        paged_down_factors.transpose(0, 2, 1).reshape(-1, LANES),
    )
    columns = HEAD_SIZE + FRESH_ROWS + 3 * RANK
    weights, smalls = call(
        functools.partial(plan_kernel, groups),
        [shape(columns, width), shape(5, SLOTS, LANES)],
        [SMEM, SMEM] + [ANY] * 5 + [VMEM],
        [pltpu.VMEM((width, HEAD_SIZE), BF16), pltpu.SemaphoreType.DMA((7,))],
        moved=5 * 1024 * 1024,
        limit=60,
    )(
        place,
        document_page_slots,
        query_weight,
        key_value_weight.T,
        shared_down_factors.T,
        query_up,
        key_value_up,
        document_of_row.reshape(1, rows),
    )
    features, pieces, weights, smalls = lax.optimization_barrier(
        (features, pieces, weights, smalls)
    )
    pieces = [
        lax.ppermute(piece, "yh", [(i, (i + shift) % Y_HIGH) for i in range(Y_HIGH)]) if shift else piece
        for shift, piece in zip(SHIFTS, pieces)
    ]
    features = jnp.broadcast_to(features.reshape(1, Y, part, rows), (X, Y, part, rows))
    features = lax.all_to_all(features, "x", 0, 0, tiled=True)

    message, fresh, queries_t = call(
        functools.partial(project_kernel, groups),
        [
            shape(groups, 2 * capacity, HEAD_SIZE),
            shape(FRESH_ROWS, rows),
            shape(HEAD_SIZE, rows),
        ],
        [SMEM] + [VMEM] * 5,
        [pltpu.VMEM((width, rows), BF16), pltpu.VMEM((HEAD_SIZE, rows), F32)],
        flops=2 * width * rows * 256,
        moved=4 * 1024 * 1024,
    )(
        place,
        features,
        weights,
        input_norm_gain.reshape(Y, X, part).transpose(1, 0, 2),
        smalls,
        adapter_of_row.reshape(1, rows),
    )
    fresh = lax.ppermute(
        fresh,
        ("yh", "yl"),
        [(y, 2 * y if y < Y_HIGH else 2 * (y - Y_HIGH) + 1) for y in range(Y)],
    )
    received = lax.all_to_all(message, ("core", "z"), 0, 0, tiled=True)

    message, slot_adapters = call(
        functools.partial(turn_kernel, groups),
        [shape(BLOCK, MESSAGE_ROWS, LANES), shape(8, SLOTS, dtype=F32)],
        [VMEM],
        moved=1024 * 1024,
    )(received)
    message, pieces = lax.optimization_barrier((message, pieces))
    gathered = lax.all_to_all(message, ("yl", "x"), 0, 0, tiled=True)

    tokens = PIECE_TOKENS * Y_HIGH
    prepared = call(
        prepare_kernel,
        shape(tokens + tokens // DEPTH * VALUE_ROWS, DEPTH),
        [VMEM] * 4,
        moved=3 * 1024 * 1024,
    )(*pieces)
    message = call(
        attend_kernel,
        shape(BLOCK, RETURN_ROWS + FRESH_ROWS, LANES),
        [VMEM] * 5,
        [
            pltpu.VMEM((2, DEPTH, SLOTS), BF16),
            pltpu.VMEM((2, tokens, SLOTS), F32),
            pltpu.VMEM((BLOCK, VALUE_ROWS, SLOTS), F32),
            pltpu.VMEM((BLOCK, 8, SLOTS), F32),
        ],
        flops=4 * SLOTS * BLOCK * tokens * 256,
        moved=3 * 1024 * 1024,
        limit=24,
    )(gathered, slot_adapters, smalls, prepared, fresh)
    partials = lax.all_to_all(message, ("yl", "x"), 0, 0, tiled=True)

    message = call(
        functools.partial(merge_kernel, groups),
        shape(groups, 2 * capacity, HEAD_SIZE),
        [VMEM],
        flops=SLOTS * HEAD_SIZE * 16,
        moved=1024 * 1024,
    )(partials)
    received = lax.all_to_all(message, ("core", "z"), 0, 0, tiled=True)

    return call(
        functools.partial(finish_kernel, groups),
        shape(rows, HEAD_SIZE),
        [VMEM] * 4,
        flops=2 * SLOTS * rows * 256,
        moved=1024 * 1024,
    )(received, smalls, queries_t, partials)


def solution(mesh):
    groups = mesh.devices.shape[0]
    split = Mesh(
        mesh.devices.reshape(groups // 2, 2, Y_HIGH, Y_LOW, X), ("z", "core", "yh", "yl", "x")
    )
    tp = ("yh", "yl", "x")
    grp = ("z", "core")
    in_specs = (
        P(grp, tp),
        P(),
        P(None, tp),
        P(None, tp),
        P(),
        P(None, None, tp),
        P(),
        P(grp + tp, None, None),
        P(grp + tp, None, None),
        P(grp + tp, None, None),
        P(grp),
        P(grp, None),
        P(),
    )
    return jax.shard_map(
        per_device, mesh=split, in_specs=in_specs, out_specs=P(grp, tp), check_vma=False
    )
```

```python
import functools
import math

import jax
import jax.numpy as jnp
from jax import lax
from jax.experimental import pallas as pl
from jax.experimental.pallas import tpu as pltpu
from jax.sharding import Mesh, PartitionSpec as P

HEAD_SIZE = 128
RANK = 16
LANES = 128
Y_HIGH, Y_LOW, X = 4, 2, 4
Y = Y_HIGH * Y_LOW
BLOCK = Y_LOW * X
SLOTS = 256
TILES = SLOTS // LANES
QUERY_ROWS = HEAD_SIZE + RANK
MESSAGE_ROWS = TILES * QUERY_ROWS
RETURN_ROWS = TILES * HEAD_SIZE + 16
FRESH_ROWS = 32
DEPTH = 2 * HEAD_SIZE
VALUE_ROWS = QUERY_ROWS + 16
OWN_UP, KEY_UP, VALUE_UP, QUERY_UP, PLACING = range(5)
PIECE_TOKENS = 512
PIECE_ROWS = 2 * PIECE_TOKENS + 2 * RANK * PIECE_TOKENS // LANES
SHIFTS = (0, 1, 3, 2)
SCORE_SCALE = HEAD_SIZE**-0.5
F32 = jnp.float32
BF16 = jnp.bfloat16
VMEM = pl.BlockSpec(memory_space=pltpu.VMEM)
SMEM = pl.BlockSpec(memory_space=pltpu.SMEM)
ANY = pl.BlockSpec(memory_space=pl.ANY)


def dot(left, right, left_dim, right_dim):
    return lax.dot_general(
        left, right, (((left_dim,), (right_dim,)), ((), ())), preferred_element_type=F32
    )


def call(kernel, out_shape, in_specs, scratch=(), flops=0, moved=0, limit=16, out_specs=None):
    return pl.pallas_call(
        kernel,
        out_shape=out_shape,
        in_specs=in_specs,
        out_specs=out_specs or jax.tree.map(lambda _: VMEM, out_shape),
        scratch_shapes=list(scratch),
        compiler_params=pltpu.CompilerParams(vmem_limit_bytes=limit * 1024 * 1024),
        cost_estimate=pl.CostEstimate(flops=flops, bytes_accessed=moved, transcendentals=0),
    )


def shape(*dims, dtype=BF16):
    return jax.ShapeDtypeStruct(dims, dtype)


def of_adapter(low, adapters):
    repeated = jnp.concatenate([low] * 16, axis=0)
    adapter = lax.broadcasted_iota(jnp.int32, repeated.shape, 0) // RANK
    return jnp.where(adapter == adapters, repeated, jnp.zeros_like(repeated))


def split_float(value):
    high = value.astype(BF16).astype(F32)
    middle = (value - high).astype(BF16).astype(F32)
    return high, middle, value - high - middle


def fetch(pairs, sems):
    moves = [pltpu.make_async_copy(*pair, sems.at[i]) for i, pair in enumerate(pairs)]
    for move in moves:
        move.start()
    for move in moves:
        move.wait()


def pack_kernel(place, keys_far, values_far, factors_far, *refs):
    pieces, (keys, values, factors, sems) = refs[:Y_HIGH], refs[Y_HIGH:]
    fetch([(keys_far, keys), (values_far, values), (factors_far, factors)], sems)
    for shift, piece in zip(SHIFTS, pieces):
        head = lax.rem(place[1] + shift, Y_HIGH)
        columns = pl.ds(pl.multiple_of(head * HEAD_SIZE, HEAD_SIZE), HEAD_SIZE)
        piece[0:PIECE_TOKENS, :] = keys[:, columns]
        piece[PIECE_TOKENS : 2 * PIECE_TOKENS, :] = values[:, columns]
        piece[2 * PIECE_TOKENS :, :] = factors[...]


def plan_kernel(
    groups,
    place,
    page_slots,
    query_weight_far,
    key_value_weight,
    down,
    query_up,
    key_value_up,
    documents,
    weights,
    smalls,
    query_weight,
    sems,
):
    pairs = [
        (query_weight_far, query_weight),
        (key_value_weight, weights.at[pl.ds(HEAD_SIZE, FRESH_ROWS), :]),
        (down, weights.at[pl.ds(HEAD_SIZE + FRESH_ROWS, 3 * RANK), :]),
        (query_up, smalls.at[QUERY_UP]),
    ]
    for index, head in enumerate((place[0] // X, place[1], place[1] + Y_HIGH)):
        columns = pl.ds(pl.multiple_of(head * HEAD_SIZE, HEAD_SIZE), HEAD_SIZE)
        pairs.append((key_value_up.at[:, columns], smalls.at[index]))
    fetch(pairs, sems)
    for start in range(0, weights.shape[1], LANES):
        block = query_weight[start : start + LANES, :].astype(F32).T
        weights[0:HEAD_SIZE, start : start + LANES] = block.astype(BF16)

    document = documents[...]
    rows = document.shape[1]
    target = jnp.zeros_like(document)
    for d in range(page_slots.shape[0]):
        target = jnp.where(document == d, page_slots[d, 0] // page_slots.shape[1], target)
    capacity = SLOTS // groups
    target = target % 2 * (groups // 2) + target // 2
    group = lax.broadcasted_iota(jnp.int32, (16, rows), 0)
    match = (group == target).astype(F32)
    before = (
        lax.broadcasted_iota(jnp.int32, (rows, rows), 0)
        < lax.broadcasted_iota(jnp.int32, (rows, rows), 1)
    ).astype(F32)
    earlier = dot(match.astype(BF16), before.astype(BF16), 1, 0)
    position = jnp.sum(earlier * match, axis=0, keepdims=True).astype(jnp.int32)
    slot = target * capacity + position
    placed = (lax.broadcasted_iota(jnp.int32, (SLOTS, rows), 0) == slot).astype(F32)
    smalls[PLACING] = placed.astype(BF16)


def project_kernel(
    groups,
    place,
    sources,
    weights,
    gain,
    smalls_far,
    adapters,
    message,
    fresh,
    queries_t,
    normed,
    update,
    smalls,
    sems,
):
    load = pltpu.make_async_copy(smalls_far, smalls, sems.at[0])
    load.start()
    device = place[0]
    part = gain.shape[2]
    width = normed.shape[0]
    squares = jnp.zeros((part, normed.shape[1]), F32)
    for x in range(X):
        for y in range(Y):
            block = sources[x, y].astype(F32)
            squares = squares + block * block
    scale = lax.rsqrt(jnp.sum(squares, axis=0, keepdims=True) / width + 1e-06)
    for x in range(X):
        gain_t = gain[x].T
        for y in range(Y):
            block = sources[x, y].astype(F32) * scale * gain_t[:, y : y + 1]
            start = (y * X + x) * part
            normed[pl.ds(start, part), :] = block.astype(BF16)
    total = dot(weights[...], normed[...], 1, 0)
    load.wait()

    adapter = adapters[...]
    low = total[HEAD_SIZE + FRESH_ROWS :].astype(BF16)
    query_update = dot(smalls[QUERY_UP], of_adapter(low[0:RANK], adapter), 0, 0)
    queries = (total[0:HEAD_SIZE] + query_update).astype(BF16)
    queries_t[...] = queries

    is_key = device < Y * X // 2
    low_kv = jnp.where(is_key, low[RANK : 2 * RANK], low[2 * RANK :])
    update[...] = dot(smalls[OWN_UP], of_adapter(low_kv, adapter), 0, 0)
    mine = pl.ds(pl.multiple_of(lax.rem(device, X) * FRESH_ROWS, FRESH_ROWS), FRESH_ROWS)
    new = total[HEAD_SIZE : HEAD_SIZE + FRESH_ROWS] + update[mine, :]
    fresh[...] = new.astype(BF16)

    every = dot(smalls[KEY_UP], queries, 1, 0)
    of_row = lax.broadcasted_iota(jnp.int32, every.shape, 0) // RANK == adapter
    kept = jnp.where(of_row, every, 0.0)
    factors = kept[0:RANK]
    for a in range(1, 16):
        factors = factors + kept[a * RANK : (a + 1) * RANK]
    rest = jnp.zeros((HEAD_SIZE - RANK - 1, factors.shape[1]), F32)
    beside = jnp.concatenate([factors, adapter.astype(F32), rest], axis=0).astype(BF16)

    capacity = SLOTS // groups
    place_rows = smalls[PLACING]
    placed = dot(place_rows, queries, 1, 1).astype(BF16)
    message[:, 0:capacity, :] = placed.reshape(groups, capacity, HEAD_SIZE)
    placed = dot(place_rows, beside, 1, 1).astype(BF16)
    message[:, capacity:, :] = placed.reshape(groups, capacity, LANES)


def turn_kernel(groups, received, message, slot_adapters):
    capacity = SLOTS // groups
    queries = received[:, 0:capacity, :].reshape(SLOTS, HEAD_SIZE).astype(F32).T.astype(BF16)
    beside = received[:, capacity:, :].reshape(SLOTS, LANES).astype(F32).T
    slot_adapters[...] = jnp.broadcast_to(beside[RANK : RANK + 1], slot_adapters.shape)
    factors = beside[0:RANK].astype(BF16)
    for member in range(BLOCK):
        for tile in range(TILES):
            lanes = slice(tile * LANES, (tile + 1) * LANES)
            start = tile * QUERY_ROWS
            message[member, start : start + HEAD_SIZE, :] = queries[:, lanes]
            message[member, start + HEAD_SIZE : start + QUERY_ROWS, :] = factors[:, lanes]


def prepare_kernel(piece_0, piece_1, piece_2, piece_3, prepared):
    tokens = PIECE_TOKENS * Y_HIGH
    ones = lax.broadcasted_iota(jnp.int32, (VALUE_ROWS - QUERY_ROWS, DEPTH), 0) == 0
    for index, piece in enumerate((piece_0, piece_1, piece_2, piece_3)):
        for page in range(PIECE_TOKENS // LANES):
            start = page * LANES
            token = index * PIECE_TOKENS + start
            here = slice(token, token + LANES)
            row = 2 * PIECE_TOKENS + page * 2 * RANK
            factors = piece[row : row + 2 * RANK, :]
            key_factors = jnp.concatenate(
                [factors[0:RANK].astype(F32), jnp.zeros((LANES - RANK, LANES), F32)], axis=0
            )
            prepared[here, 0:HEAD_SIZE] = piece[start : start + LANES, :]
            prepared[here, HEAD_SIZE:] = key_factors.T.astype(BF16)
            value = piece[PIECE_TOKENS + start : PIECE_TOKENS + start + LANES, :]
            base = tokens + token // DEPTH * VALUE_ROWS
            lanes = slice(token % DEPTH, token % DEPTH + LANES)
            prepared[base : base + HEAD_SIZE, lanes] = value.astype(F32).T.astype(BF16)
            prepared[base + HEAD_SIZE : base + QUERY_ROWS, lanes] = factors[RANK:]
            if token % DEPTH == 0:
                prepared[base + QUERY_ROWS : base + VALUE_ROWS, :] = ones.astype(F32).astype(BF16)


def attend_kernel(
    queries, slot_adapters, smalls, prepared, fresh, message, query, scores, totals, peaks
):
    tokens = PIECE_TOKENS * Y_HIGH
    chunk = 1024
    exponent = SCORE_SCALE * math.log2(math.e)
    query[:, QUERY_ROWS:, :] = jnp.zeros((2, DEPTH - QUERY_ROWS, SLOTS), BF16)

    def load(head, side):
        for tile in range(TILES):
            query[side, 0:QUERY_ROWS, tile * LANES : (tile + 1) * LANES] = queries[
                head, tile * QUERY_ROWS : (tile + 1) * QUERY_ROWS, :
            ]

    def score(side, start, highest):
        block = dot(prepared[start : start + chunk, :], query[side], 1, 0)
        scores[side, start : start + chunk, :] = block
        return jnp.maximum(highest, jnp.max(block.reshape(chunk // 8, 8, SLOTS), axis=0))

    def add(side, start, peak, total):
        weight = jnp.exp2(scores[side, start : start + chunk, :] * exponent - peak).astype(BF16)
        for step in range(chunk // DEPTH):
            base = tokens + (start // DEPTH + step) * VALUE_ROWS
            values = prepared[base : base + VALUE_ROWS, :]
            total = total + dot(values, weight[step * DEPTH : (step + 1) * DEPTH], 1, 0)
        return total

    lowest = jnp.full((8, SLOTS), -jnp.inf, F32)

    def one_head(head, following, side, peak):
        load(following, 1 - side)
        highest, total = lowest, jnp.zeros((VALUE_ROWS, SLOTS), F32)
        for start in range(0, tokens, chunk):
            highest = score(1 - side, start, highest)
            total = add(side, start, peak * exponent, total)
        totals[head] = total
        peaks[head] = jnp.broadcast_to(peak, (8, SLOTS))
        return jnp.max(highest, axis=0, keepdims=True)

    def two_heads(pair, peak):
        peak = one_head(2 * pair, 2 * pair + 1, 0, peak)
        return one_head(2 * pair + 1, jnp.minimum(2 * pair + 2, BLOCK - 1), 1, peak)

    load(0, 0)
    highest = lowest
    for start in range(0, tokens, chunk):
        highest = score(0, start, highest)
    lax.fori_loop(0, BLOCK // 2, two_heads, jnp.max(highest, axis=0, keepdims=True))

    value_up = smalls[VALUE_UP]
    adapters = slot_adapters[0:1, :].astype(jnp.int32)
    for head in range(BLOCK):
        total, peak = totals[head], peaks[head, 0:1]
        mass = total[QUERY_ROWS : QUERY_ROWS + 1]
        inverse = 1.0 / mass
        low = (total[HEAD_SIZE:QUERY_ROWS] * inverse).astype(BF16)
        shift = dot(value_up, of_adapter(low, adapters), 0, 0)
        result = (total[0:HEAD_SIZE] * inverse + shift).astype(BF16)
        parts = split_float(peak * SCORE_SCALE + jnp.log(mass))
        stats = [part[:, tile * LANES : (tile + 1) * LANES] for tile in range(TILES) for part in parts]
        stats = jnp.concatenate(stats + [jnp.zeros((16 - len(stats), LANES), F32)], axis=0)
        for tile in range(TILES):
            message[head, tile * HEAD_SIZE : (tile + 1) * HEAD_SIZE, :] = result[
                :, tile * LANES : (tile + 1) * LANES
            ]
        message[head, TILES * HEAD_SIZE : RETURN_ROWS, :] = stats.astype(BF16)
        message[head, RETURN_ROWS:, :] = fresh[...]


def merge_kernel(groups, partials, message):
    capacity = SLOTS // groups
    stats = [partials[member, TILES * HEAD_SIZE : RETURN_ROWS, :].astype(F32) for member in range(BLOCK)]
    results, masses = [], []
    for tile in range(TILES):
        first = 3 * tile
        logs = [s[first : first + 1] + s[first + 1 : first + 2] + s[first + 2 : first + 3] for s in stats]
        peak = functools.reduce(jnp.maximum, logs)
        weights = [jnp.exp(one - peak) for one in logs]
        whole = functools.reduce(jnp.add, weights)
        rows = slice(tile * HEAD_SIZE, (tile + 1) * HEAD_SIZE)
        total = jnp.zeros((HEAD_SIZE, LANES), F32)
        for member in range(BLOCK):
            total = total + partials[member, rows, :].astype(F32) * weights[member]
        results.append((total / whole).T.astype(BF16))
        parts = list(split_float(peak + jnp.log(whole)))
        parts = jnp.concatenate(parts + [jnp.zeros((LANES - 3, LANES), F32)], axis=0)
        masses.append(parts.T.astype(BF16))
    message[:, 0:capacity, :] = jnp.concatenate(results, axis=0).reshape(groups, capacity, HEAD_SIZE)
    message[:, capacity:, :] = jnp.concatenate(masses, axis=0).reshape(groups, capacity, LANES)


def finish_kernel(groups, received, smalls, queries_t, partials, out):
    capacity = SLOTS // groups
    place = smalls[PLACING]
    shared = dot(received[:, 0:capacity, :].reshape(SLOTS, HEAD_SIZE), place, 0, 0)
    stats = dot(received[:, capacity:, :].reshape(SLOTS, LANES), place, 0, 0)
    log_mass = stats[0:1] + stats[1:2] + stats[2:3]
    new = partials[:, RETURN_ROWS:, :]
    key = new[0:X].reshape(HEAD_SIZE, LANES).astype(F32)
    value = new[X:].reshape(HEAD_SIZE, LANES).astype(F32)
    own = jnp.sum(queries_t[...].astype(F32) * key, axis=0, keepdims=True) * SCORE_SCALE
    peak = jnp.maximum(log_mass, own)
    shared_weight = jnp.exp(log_mass - peak)
    own_weight = jnp.exp(own - peak)
    result = (shared * shared_weight + value * own_weight) / (shared_weight + own_weight)
    out[...] = result.T.astype(BF16)


def per_device(
    residual_input,
    input_norm_gain,
    query_weight,
    key_value_weight,
    shared_down_factors,
    query_up_factors,
    key_value_up_factors,
    paged_base_keys,
    paged_base_values,
    paged_down_factors,
    adapter_of_row,
    document_of_row,
    document_page_slots,
):
    groups = lax.axis_size("z") * lax.axis_size("core")
    capacity = SLOTS // groups
    rows, part = residual_input.shape
    width = part * Y * X
    y_high = lax.axis_index("yh")
    device = (y_high * Y_LOW + lax.axis_index("yl")) * X + lax.axis_index("x")
    place = jnp.stack([device, y_high]).astype(jnp.int32)
    query_up = query_up_factors.reshape(-1, HEAD_SIZE)
    key_value_up = key_value_up_factors.reshape(-1, key_value_up_factors.shape[2])

    features = jnp.broadcast_to(residual_input.T[None], (Y, part, rows))
    features = lax.all_to_all(features, ("yh", "yl"), 0, 0, tiled=True)
    pieces = call(
        pack_kernel,
        [shape(PIECE_ROWS, HEAD_SIZE)] * Y_HIGH,
        [SMEM] + [ANY] * 3,
        [
            pltpu.VMEM((PIECE_TOKENS, Y_HIGH * HEAD_SIZE), BF16),
            pltpu.VMEM((PIECE_TOKENS, Y_HIGH * HEAD_SIZE), BF16),
            pltpu.VMEM((PIECE_ROWS - 2 * PIECE_TOKENS, LANES), BF16),
            pltpu.SemaphoreType.DMA((3,)),
        ],
        moved=3 * 1024 * 1024,
        limit=60,
    )(
        place,
        paged_base_keys.reshape(PIECE_TOKENS, -1),
        paged_base_values.reshape(PIECE_TOKENS, -1),
        paged_down_factors.transpose(0, 2, 1).reshape(-1, LANES),
    )
    columns = HEAD_SIZE + FRESH_ROWS + 3 * RANK
    weights, smalls = call(
        functools.partial(plan_kernel, groups),
        [shape(columns, width), shape(5, SLOTS, LANES)],
        [SMEM, SMEM] + [ANY] * 5 + [VMEM],
        [pltpu.VMEM((width, HEAD_SIZE), BF16), pltpu.SemaphoreType.DMA((7,))],
        moved=5 * 1024 * 1024,
        limit=60,
    )(
        place,
        document_page_slots,
        query_weight,
        key_value_weight.T,
        shared_down_factors.T,
        query_up,
        key_value_up,
        document_of_row.reshape(1, rows),
    )
    features, pieces, weights, smalls = lax.optimization_barrier(
        (features, pieces, weights, smalls)
    )
    pieces = [
        lax.ppermute(piece, "yh", [(i, (i + shift) % Y_HIGH) for i in range(Y_HIGH)]) if shift else piece
        for shift, piece in zip(SHIFTS, pieces)
    ]
    features = jnp.broadcast_to(features.reshape(1, Y, part, rows), (X, Y, part, rows))
    features = lax.all_to_all(features, "x", 0, 0, tiled=True)

    message, fresh, queries_t = call(
        functools.partial(project_kernel, groups),
        [
            shape(groups, 2 * capacity, HEAD_SIZE),
            shape(FRESH_ROWS, rows),
            shape(HEAD_SIZE, rows),
        ],
        [SMEM, VMEM, VMEM, VMEM, ANY, VMEM],
        [
            pltpu.VMEM((width, rows), BF16),
            pltpu.VMEM((HEAD_SIZE, rows), F32),
            pltpu.VMEM((5, SLOTS, LANES), BF16),
            pltpu.SemaphoreType.DMA((1,)),
        ],
        flops=2 * width * rows * 256,
        moved=4 * 1024 * 1024,
    )(
        place,
        features,
        weights,
        input_norm_gain.reshape(Y, X, part).transpose(1, 0, 2),
        smalls,
        adapter_of_row.reshape(1, rows),
    )
    fresh = lax.ppermute(
        fresh,
        ("yh", "yl"),
        [(y, 2 * y if y < Y_HIGH else 2 * (y - Y_HIGH) + 1) for y in range(Y)],
    )
    received = lax.all_to_all(message, ("core", "z"), 0, 0, tiled=True)

    message, slot_adapters = call(
        functools.partial(turn_kernel, groups),
        [shape(BLOCK, MESSAGE_ROWS, LANES), shape(8, SLOTS, dtype=F32)],
        [VMEM],
        moved=1024 * 1024,
    )(received)
    message, pieces = lax.optimization_barrier((message, pieces))
    gathered = lax.all_to_all(message, ("yl", "x"), 0, 0, tiled=True)

    tokens = PIECE_TOKENS * Y_HIGH
    prepared = call(
        prepare_kernel,
        shape(tokens + tokens // DEPTH * VALUE_ROWS, DEPTH),
        [VMEM] * 4,
        moved=3 * 1024 * 1024,
    )(*pieces)
    message = call(
        attend_kernel,
        shape(BLOCK, RETURN_ROWS + FRESH_ROWS, LANES),
        [VMEM] * 5,
        [
            pltpu.VMEM((2, DEPTH, SLOTS), BF16),
            pltpu.VMEM((2, tokens, SLOTS), F32),
            pltpu.VMEM((BLOCK, VALUE_ROWS, SLOTS), F32),
            pltpu.VMEM((BLOCK, 8, SLOTS), F32),
        ],
        flops=4 * SLOTS * BLOCK * tokens * 256,
        moved=3 * 1024 * 1024,
        limit=24,
    )(gathered, slot_adapters, smalls, prepared, fresh)
    partials = lax.all_to_all(message, ("yl", "x"), 0, 0, tiled=True)

    message = call(
        functools.partial(merge_kernel, groups),
        shape(groups, 2 * capacity, HEAD_SIZE),
        [VMEM],
        flops=SLOTS * HEAD_SIZE * 16,
        moved=1024 * 1024,
    )(partials)
    received = lax.all_to_all(message, ("core", "z"), 0, 0, tiled=True)

    return call(
        functools.partial(finish_kernel, groups),
        shape(rows, HEAD_SIZE),
        [VMEM] * 4,
        flops=2 * SLOTS * rows * 256,
        moved=1024 * 1024,
    )(received, smalls, queries_t, partials)


def solution(mesh):
    groups = mesh.devices.shape[0]
    split = Mesh(
        mesh.devices.reshape(groups // 2, 2, Y_HIGH, Y_LOW, X), ("z", "core", "yh", "yl", "x")
    )
    tp = ("yh", "yl", "x")
    grp = ("z", "core")
    in_specs = (
        P(grp, tp),
        P(),
        P(None, tp),
        P(None, tp),
        P(),
        P(None, None, tp),
        P(),
        P(grp + tp, None, None),
        P(grp + tp, None, None),
        P(grp + tp, None, None),
        P(grp),
        P(grp, None),
        P(),
    )
    return jax.shard_map(
        per_device, mesh=split, in_specs=in_specs, out_specs=P(grp, tp), check_vma=False
    )
```
